32 devices in a mesh: section: 4 (over y, x), dp: 8 (over z, core).
Axes of the slice: x: 2, y: 2, z: 4, core: 2. Of those that a mesh axis runs over, the one named last changes fastest.
Arguments:
- tokens: bfloat16 [8192, 384], P(('section', 'dp')), may hold values from -6 to 6
- cotangent: bfloat16 [8192, 384], P(('section', 'dp')), may hold values from -6 to 6
- lengths: int32 [4, 8], P(None, 'dp'), may hold values from 32 to 256, as said below
- gain_one: bfloat16 [384], P('section'), may hold values from 0.099609375 to 1.8984375
- mixing_one: bfloat16 [384, 1152], P(None, 'section'), may hold values from -0.3125 to 0.3125
- output_one: bfloat16 [384, 384], P(None, 'section'), may hold values from -2.5 to 2.5
- gain_two: bfloat16 [384], P('section'), may hold values from 0.099609375 to 1.8984375
- up_two: bfloat16 [384, 1536], P(None, 'section'), may hold values from -0.3125 to 0.3125
- down_two: bfloat16 [1536, 384], P('section'), may hold values from -0.15625 to 0.15625
- gain_three: bfloat16 [384], P('section'), may hold values from 0.099609375 to 1.8984375
- pair_three: bfloat16 [384, 768], P(None, 'section'), may hold values from -0.3125 to 0.3125
- fresh_three: bfloat16 [384, 192], P(None, 'section'), may hold values from -0.3125 to 0.3125
- output_three: bfloat16 [384, 384], P(None, 'section'), may hold values from -2.5 to 2.5
- gain_four: bfloat16 [384], P('section'), may hold values from 0.099609375 to 1.8984375
- up_four: bfloat16 [384, 1536], P(None, 'section'), may hold values from -0.3125 to 0.3125
- down_four: bfloat16 [1536, 384], P('section'), may hold values from -0.15625 to 0.15625
Outputs:
- output: float32 [8192, 384], P(('section', 'dp'))
- input_grad: float32 [8192, 384], P(('section', 'dp'))
- grad_gain_one: float32 [384], replicated
- grad_mixing_one: float32 [384, 1152], replicated
- grad_output_one: float32 [384, 384], replicated
- grad_gain_two: float32 [384], replicated
- grad_up_two: float32 [384, 1536], replicated
- grad_down_two: float32 [1536, 384], replicated
- grad_gain_three: float32 [384], replicated
- grad_pair_three: float32 [384, 768], replicated
- grad_fresh_three: float32 [384, 192], replicated
- grad_output_three: float32 [384, 384], replicated
- grad_gain_four: float32 [384], replicated
- grad_up_four: float32 [384, 1536], replicated
- grad_down_four: float32 [1536, 384], replicated
The draws below stay inside these ranges and needn't reach their ends.
Inputs may be any that keep to these rules, and one draw needn't show every extreme that they name: lengths[m, r] is the number of valid positions of the sequence that starts at row (m * 8 + r) * 256; in every draw each data group r has some sequence 256 long, and some sequence has 32 positions.
All inputs are finite; a program needn't handle non-finite values.
Results may differ from the reference program's by a relative error of at most 0.019.
Values may be sent and summed in bfloat16 or wider, within the bound.
No kernel may reach another device: no remote copies, remote signals or barrier semaphores. Data moves between devices by JAX's collectives and lax.ppermute only.
A program may use at most 192 MiB of HBM per device.

```python
import jax
import jax.numpy as jnp
from jax import lax

D = 384
HEADS = 6
HEAD = 64
FF = 1536
SHARED = 3
SEQ = 256
LEAST = 32
MICRO = 4
GROUPS = 8
TOKENS = 8192


def draw_lengths(key, part):
    key = jax.random.fold_in(key, 7)
    first_key, second_key, third_key = jax.random.split(key, 3)
    sampled = jax.random.randint(first_key, (MICRO, GROUPS), LEAST, SEQ + 1)
    longest_slot = jax.random.randint(second_key, (GROUPS,), 0, MICRO)
    filled = jnp.arange(MICRO)[:, None] == longest_slot[None, :]
    sampled = jnp.where(filled, SEQ, sampled)
    short_group = jax.random.randint(third_key, (), 0, GROUPS)
    short_slot = (longest_slot[short_group] + 1) % MICRO
    sampled = sampled.at[short_slot, short_group].set(LEAST)
    return sampled.astype(jnp.int32)


def block_scale(key, shape, pieces, least, top_value):
    def one(dim, parts):
        draws = jax.random.uniform(jax.random.fold_in(jax.random.fold_in(key, 6), dim), (parts,), jnp.float32, least / len(pieces), top_value / len(pieces))
        return jnp.repeat(jnp.exp(draws), shape[dim] // parts).reshape((-1,) + (1,) * (len(shape) - dim - 1))

    loudness = one(*pieces[0])
    for cut in pieces[1:]:
        loudness = loudness * one(*cut)
    return loudness


def bell_draw(stream_key, shape, width, limit, shards=(), held_as=jnp.bfloat16):
    array = width * jax.random.normal(stream_key, shape, jnp.float32)
    if shards:
        array = array * block_scale(stream_key, shape, shards, -0.22, 0.18)
    return jnp.clip(array, -limit, limit).astype(held_as)


def setup_inputs(seed: int = 0) -> dict:
    splits = jax.random.split(jax.random.key(seed), 17)
    return {
        "tokens": bell_draw(splits[0], (TOKENS, D), 1.0, 6.0, ((0, 32),)),
        "cotangent": bell_draw(splits[1], (TOKENS, D), 1.0, 6.0, ((0, 32),)),
        "lengths": draw_lengths(jax.random.fold_in(splits[16], 71), 0),
        "gain_one": jnp.clip(1.0 + 0.18 * jax.random.normal(splits[3], (D,), jnp.float32), 0.099609375, 1.8984375).astype(jnp.bfloat16),
        "mixing_one": bell_draw(splits[4], (D, 3 * D), D ** -0.5, 0.3125, ((1, 4),)),
        "output_one": bell_draw(splits[5], (D, D), (D // 64) ** -0.5, 2.5, ((1, 4),)),
        "gain_two": jnp.clip(1.0 + 0.18 * jax.random.normal(splits[6], (D,), jnp.float32), 0.099609375, 1.8984375).astype(jnp.bfloat16),
        "up_two": bell_draw(splits[7], (D, FF), D ** -0.5, 0.3125, ((1, 4),)),
        "down_two": bell_draw(splits[8], (FF, D), FF ** -0.5, 0.15625, ((0, 4),)),
        "gain_three": jnp.clip(1.0 + 0.18 * jax.random.normal(splits[9], (D,), jnp.float32), 0.099609375, 1.8984375).astype(jnp.bfloat16),
        "pair_three": bell_draw(splits[10], (D, 2 * D), D ** -0.5, 0.3125, ((1, 4),)),
        "fresh_three": bell_draw(splits[11], (D, (HEADS - SHARED) * HEAD), D ** -0.5, 0.3125, ((1, 4),)),
        "output_three": bell_draw(splits[12], (D, D), (D // 64) ** -0.5, 2.5, ((1, 4),)),
        "gain_four": jnp.clip(1.0 + 0.18 * jax.random.normal(splits[13], (D,), jnp.float32), 0.099609375, 1.8984375).astype(jnp.bfloat16),
        "up_four": bell_draw(splits[14], (D, FF), D ** -0.5, 0.3125, ((1, 4),)),
        "down_four": bell_draw(splits[15], (FF, D), FF ** -0.5, 0.15625, ((0, 4),)),
    }


PRECISE = lax.Precision.HIGHEST
EPSILON = 1e-05
MASKED = -1e+30
GELU_SCALE = 0.7978845608028654

@jax.custom_vjp
def low(v):
    return lax.optimization_barrier(v.astype(jnp.bfloat16)).astype(jnp.float32)

@jax.custom_vjp
def low_back(v):
    return v

def low_keep(v):
    return (low(v), None)

def low_pass(kept, grad):
    return (grad,)

def back_keep(v):
    return (v, None)

def back_low(kept, grad):
    return (low(grad),)
low.defvjp(low_keep, low_pass)
low_back.defvjp(back_keep, back_low)

def layer_norm(hidden, norm_gain):
    centred = hidden - lax.optimization_barrier(jnp.mean(hidden, -1, keepdims=True))
    spread = lax.optimization_barrier(jnp.mean(centred * centred, -1, keepdims=True))
    return centred * lax.rsqrt(spread + EPSILON) * norm_gain

def gelu(upward):
    return 0.5 * upward * (1.0 + jnp.tanh(GELU_SCALE * (upward + 0.044715 * upward * upward * upward)))

def project(normed, weight):
    return jnp.dot(normed, weight, precision=PRECISE)

def attend(queries, key_rows, values, length):
    row_count = queries.shape[0]
    query_heads = queries.reshape(row_count, HEADS, HEAD)
    key_heads = key_rows.reshape(row_count, HEADS, HEAD)
    value_heads = values.reshape(row_count, HEADS, HEAD)
    scores = low_back(jnp.einsum('qhd,khd->hqk', query_heads, key_heads, precision=PRECISE) * HEAD ** (-0.5))
    row_index = jnp.arange(row_count)[:, None]
    col_index = jnp.arange(row_count)[None, :]
    allowed = (col_index <= row_index) & (col_index < length)
    scores = jnp.where(allowed[None], scores, MASKED)
    row_peak = lax.optimization_barrier(jnp.max(scores, -1, keepdims=True))
    raised = jnp.exp(scores - row_peak)
    probability = low(raised / lax.optimization_barrier(jnp.sum(raised, -1, keepdims=True)))
    blended = jnp.einsum('hqk,khd->qhd', probability, value_heads, precision=PRECISE)
    return blended.reshape(row_count, HEADS * HEAD)

def boundary(hidden):
    return low(low_back(hidden))

def first_attention(hidden, length, norm_gain, mixing, output):
    normed = low(layer_norm(hidden, norm_gain))
    mixed_rows = low(low_back(project(normed, mixing)))
    attended = low(low_back(attend(mixed_rows[:, :D], mixed_rows[:, D:2 * D], mixed_rows[:, 2 * D:], length)))
    return (hidden + low_back(project(attended, output)), mixed_rows[:, 2 * D:2 * D + SHARED * HEAD])

def feed_forward(hidden, norm_gain, up_weight, down_weight):
    normed = low(layer_norm(hidden, norm_gain))
    upward = low_back(project(normed, up_weight))
    return hidden + low_back(project(low(gelu(upward)), down_weight))

def second_attention(hidden, shared, length, norm_gain, pair_weight, fresh_weight, output):
    normed = low(layer_norm(hidden, norm_gain))
    pair_rows = low(low_back(project(normed, pair_weight)))
    fresh_rows = low(low_back(project(normed, fresh_weight)))
    values = jnp.concatenate([low_back(shared), fresh_rows], axis=1)
    attended = low(low_back(attend(pair_rows[:, :D], pair_rows[:, D:], values, length)))
    return hidden + low_back(project(attended, output))

def block(params, single, extent):
    middle, shared = first_attention(single, extent, params[0], params[1], params[2])
    middle = boundary(middle)
    middle = boundary(feed_forward(middle, params[3], params[4], params[5]))
    middle = boundary(second_attention(middle, shared, extent, params[6], params[7], params[8], params[9]))
    return feed_forward(middle, params[10], params[11], params[12])

def reference(tokens, cotangent, lengths, gain_one, mixing_one, output_one, gain_two, up_two, down_two, gain_three, pair_three, fresh_three, output_three, gain_four, up_four, down_four):
    weights = tuple((weight.astype(jnp.float32) for weight in (gain_one, mixing_one, output_one, gain_two, up_two, down_two, gain_three, pair_three, fresh_three, output_three, gain_four, up_four, down_four)))
    inputs = tokens.astype(jnp.float32).reshape(MICRO, GROUPS, SEQ, D).transpose(1, 0, 2, 3)
    extents = lengths.T

    def forward(params, stacked):

        def group(members):
            return jax.vmap(lambda single, extent: block(params, single, extent))(members[0], members[1])
        return lax.map(jax.checkpoint(group), (stacked, extents))
    outputs, pullback = jax.vjp(forward, weights, inputs)
    valid_rows = (jnp.arange(SEQ)[None, None, :] < extents[:, :, None]).astype(jnp.float32)[..., None]
    seed_grad = cotangent.astype(jnp.float32).reshape(MICRO, GROUPS, SEQ, D).transpose(1, 0, 2, 3) * valid_rows
    grads, grad_inputs = pullback(seed_grad)

    def restore(stacked):
        return stacked.transpose(1, 0, 2, 3).reshape(TOKENS, D)
    return (restore(outputs), restore(grad_inputs), grads[0], grads[1], grads[2], grads[3], grads[4], grads[5], grads[6], grads[7], grads[8], grads[9], grads[10], grads[11], grads[12])
```

```python
import jax
import jax.numpy as jnp
from jax import lax
from jax.sharding import PartitionSpec as P

D = 384
HEADS = 6
HEAD = 64
SHARED = 3


EPSILON = 1e-05
MASKED = -1e30
GELU_SCALE = 0.7978845608028654
block_limit = 512


def shortened(shard):
    return jax.tree.map(lambda a: a.astype(jnp.bfloat16) if a.dtype == jnp.float32 else a, shard)


def from_behind(value, axis, steps):
    count = lax.axis_size(axis)
    leading, last = (max(0, -steps), min(count, count - steps))
    return lax.ppermute(value, axis, [(source, source + steps) for source in range(leading, last)])


def layer_norm(hidden, norm_gain):
    centred = hidden - jnp.mean(hidden, -1, keepdims=True)
    spread = jnp.mean(centred * centred, -1, keepdims=True)
    return centred * lax.rsqrt(spread + EPSILON) * norm_gain


def gelu(upward):
    return (
        0.5 * upward * (1.0 + jnp.tanh(GELU_SCALE * (upward + 0.044715 * upward * upward * upward)))
    )


def product(left, right):
    return jnp.dot(left, right, preferred_element_type=jnp.float32)


def inner_rows(left, right):
    return lax.dot_general(
        left, right, (((0,), (0,)), ((), ())), preferred_element_type=jnp.float32
    )


def inner_cols(left, right):
    return lax.dot_general(
        left, right, (((1,), (1,)), ((), ())), preferred_element_type=jnp.float32
    )


def split_heads(matrix):
    return matrix.reshape(matrix.shape[0], HEADS, HEAD)


def norm_back(hidden, norm_gain, grad_normed):
    normed_out, pullback = jax.vjp(layer_norm, hidden, norm_gain)
    return pullback(grad_normed)


def block_scores(query_heads, key_heads, first_row, last_row, length):
    scores = jnp.einsum(
        "qhd,khd->hqk",
        query_heads[first_row:last_row],
        key_heads[:last_row],
        preferred_element_type=jnp.float32,
    ) * HEAD ** (-0.5)
    row_index = jnp.arange(first_row, last_row)[:, None]
    col_index = jnp.arange(last_row)[None, :]
    allowed = (col_index <= row_index) & (col_index < length)
    return jnp.where(allowed[None], scores, MASKED)


def attend_forward(queries, key_rows, values, length):
    total_rows = queries.shape[0]
    block_rows = min(total_rows, block_limit)
    query_heads = split_heads(queries)
    key_heads = split_heads(key_rows)
    value_heads = split_heads(values)
    pieces = []
    sums_kept = []
    for first_row in range(0, total_rows, block_rows):
        last_row = first_row + block_rows
        scores = block_scores(query_heads, key_heads, first_row, last_row, length)
        row_peak = jnp.max(scores, -1, keepdims=True)
        raised = jnp.exp(scores - row_peak)
        totals = jnp.sum(raised, -1, keepdims=True)
        probability = (raised / totals).astype(jnp.bfloat16)
        blended = jnp.einsum(
            "hqk,khd->qhd", probability, value_heads[:last_row], preferred_element_type=jnp.float32
        )
        pieces.append(blended.reshape(block_rows, HEADS * HEAD))
        sums_kept.append((row_peak + jnp.log(totals))[:, :, 0])
    return (jnp.concatenate(pieces, 0), jnp.concatenate(sums_kept, 1))


def attend_backward(queries, key_rows, values, grad_mixed, log_sums, length):
    total_rows = queries.shape[0]
    block_rows = min(total_rows, block_limit)
    query_heads = split_heads(queries)
    key_heads = split_heads(key_rows)
    value_heads = split_heads(values)
    grad_heads = split_heads(grad_mixed)
    grad_keys = jnp.zeros((total_rows, HEADS, HEAD), jnp.float32)
    grad_values = jnp.zeros((total_rows, HEADS, HEAD), jnp.float32)
    scores = block_scores(query_heads, key_heads, 0, block_rows, length)
    probability = jnp.exp(scores - log_sums[:, 0:block_rows, None])
    rounded = probability.astype(jnp.bfloat16)
    grad_prob = jnp.einsum(
        "qhd,khd->hqk", grad_heads, value_heads, preferred_element_type=jnp.float32
    )
    centre = jnp.sum(probability * grad_prob, -1, keepdims=True)
    grad_scores = (probability * (grad_prob - centre)).astype(jnp.bfloat16)
    query_part = jnp.einsum(
        "hqk,khd->qhd", grad_scores, key_heads, preferred_element_type=jnp.float32
    ) * HEAD ** (-0.5)
    query_pieces = [query_part]
    key_part = jnp.einsum(
        "hqk,qhd->khd", grad_scores, query_heads, preferred_element_type=jnp.float32
    ) * HEAD ** (-0.5)
    value_part = jnp.einsum("hqk,qhd->khd", rounded, grad_heads, preferred_element_type=jnp.float32)
    grad_keys = grad_keys.at[:block_rows].add(key_part)
    grad_values = grad_values.at[:block_rows].add(value_part)
    width_all = HEADS * HEAD
    grad_queries = jnp.concatenate(query_pieces, 0).reshape(total_rows, width_all)
    return (
        grad_queries,
        grad_keys.reshape(total_rows, width_all),
        grad_values.reshape(total_rows, width_all),
    )


def first_forward(hidden, length, norm_gain, mixing, output):
    normed = layer_norm(hidden, norm_gain).astype(jnp.bfloat16)
    mixed_rows = product(normed, mixing).astype(jnp.bfloat16)
    attended, log_sums = attend_forward(
        mixed_rows[:, :D], mixed_rows[:, D : 2 * D], mixed_rows[:, 2 * D :], length
    )
    attended = attended.astype(jnp.bfloat16)
    return (
        hidden + product(attended, output),
        mixed_rows[:, 2 * D : 2 * D + SHARED * HEAD],
        attended,
        log_sums,
    )


def first_backward(
    hidden, length, attended, log_sums, grad_out, grad_shared, norm_gain, mixing, output
):
    normed = layer_norm(hidden, norm_gain).astype(jnp.bfloat16)
    mixed_rows = product(normed, mixing).astype(jnp.bfloat16)
    grad_low = grad_out.astype(jnp.bfloat16)
    grad_output = inner_rows(attended, grad_low)
    grad_attended = inner_cols(grad_low, output).astype(jnp.bfloat16)
    grad_query, grad_key, grad_value = attend_backward(
        mixed_rows[:, :D],
        mixed_rows[:, D : 2 * D],
        mixed_rows[:, 2 * D :],
        grad_attended,
        log_sums,
        length,
    )
    shared_width = SHARED * HEAD
    grad_value = jnp.concatenate(
        [grad_value[:, :shared_width] + grad_shared, grad_value[:, shared_width:]], 1
    )
    grad_mixed = jnp.concatenate([grad_query, grad_key, grad_value], 1).astype(jnp.bfloat16)
    grad_mixing = inner_rows(normed, grad_mixed)
    grad_hidden, grad_gain = norm_back(hidden, norm_gain, inner_cols(grad_mixed, mixing))
    return (grad_out + grad_hidden, (grad_gain, grad_mixing, grad_output))


def feed_forward(hidden, norm_gain, up_weight, down_weight):
    normed = layer_norm(hidden, norm_gain).astype(jnp.bfloat16)
    active = gelu(product(normed, up_weight)).astype(jnp.bfloat16)
    return hidden + product(active, down_weight)


def feed_backward(hidden, grad_out, norm_gain, up_weight, down_weight):
    normed = layer_norm(hidden, norm_gain).astype(jnp.bfloat16)
    active, gelu_pull = jax.vjp(gelu, product(normed, up_weight))
    active = active.astype(jnp.bfloat16)
    grad_low = grad_out.astype(jnp.bfloat16)
    grad_down = inner_rows(active, grad_low)
    grad_upward = gelu_pull(inner_cols(grad_low, down_weight))[0].astype(jnp.bfloat16)
    grad_up = inner_rows(normed, grad_upward)
    grad_hidden, grad_gain = norm_back(hidden, norm_gain, inner_cols(grad_upward, up_weight))
    return (grad_out + grad_hidden, (grad_gain, grad_up, grad_down))


def third_forward(hidden, length, shared, norm_gain, pair_weight, fresh_weight, output):
    normed = layer_norm(hidden, norm_gain).astype(jnp.bfloat16)
    pair_rows = product(normed, pair_weight).astype(jnp.bfloat16)
    fresh_rows = product(normed, fresh_weight).astype(jnp.bfloat16)
    values = jnp.concatenate([shared, fresh_rows], 1)
    attended, log_sums = attend_forward(pair_rows[:, :D], pair_rows[:, D:], values, length)
    attended = attended.astype(jnp.bfloat16)
    return (hidden + product(attended, output), shared, attended, log_sums)


def third_backward(
    hidden,
    length,
    shared,
    attended,
    log_sums,
    grad_out,
    norm_gain,
    pair_weight,
    fresh_weight,
    output,
):
    normed = layer_norm(hidden, norm_gain).astype(jnp.bfloat16)
    pair_rows = product(normed, pair_weight).astype(jnp.bfloat16)
    fresh_rows = product(normed, fresh_weight).astype(jnp.bfloat16)
    values = jnp.concatenate([shared, fresh_rows], 1)
    grad_low = grad_out.astype(jnp.bfloat16)
    grad_output = inner_rows(attended, grad_low)
    grad_attended = inner_cols(grad_low, output).astype(jnp.bfloat16)
    grad_query, grad_key, grad_value = attend_backward(
        pair_rows[:, :D], pair_rows[:, D:], values, grad_attended, log_sums, length
    )
    shared_width = SHARED * HEAD
    grad_pair = jnp.concatenate([grad_query, grad_key], 1).astype(jnp.bfloat16)
    grad_fresh = grad_value[:, shared_width:].astype(jnp.bfloat16)
    grad_pair_weight = inner_rows(normed, grad_pair)
    grad_fresh_weight = inner_rows(normed, grad_fresh)
    grad_normed = inner_cols(grad_pair, pair_weight) + inner_cols(grad_fresh, fresh_weight)
    grad_hidden, grad_gain = norm_back(hidden, norm_gain, grad_normed)
    shared_grad = grad_value[:, :shared_width].astype(jnp.bfloat16)
    return (
        grad_out + grad_hidden,
        shared_grad,
        (grad_gain, grad_pair_weight, grad_fresh_weight, grad_output),
    )


def gathered(shard, axis):
    return lax.all_gather(shard, "section", axis=axis, tiled=True)


def shards(
    tokens,
    cotangent,
    lengths,
    gain_one,
    mixing_one,
    output_one,
    gain_two,
    up_two,
    down_two,
    gain_three,
    pair_three,
    fresh_three,
    output_three,
    gain_four,
    up_four,
    down_four,
):
    section_index = lax.axis_index("section")
    length = lengths[section_index, 0]
    gains = lax.all_gather(
        jnp.stack([gain_one, gain_two, gain_three, gain_four]), "section", axis=1, tiled=True
    ).astype(jnp.float32)
    part_one = (gains[0], gathered(mixing_one, 1), gathered(output_one, 1))
    part_two = (gains[1], gathered(up_two, 1), gathered(down_two, 0))
    part_three = (
        gains[2],
        gathered(pair_three, 1),
        gathered(fresh_three, 1),
        gathered(output_three, 1),
    )
    part_four = (gains[3], gathered(up_four, 1), gathered(down_four, 0))

    entry = tokens.astype(jnp.float32)
    h1, shared, attended_one, sums_one = first_forward(entry, length, *part_one)
    h1 = h1.astype(jnp.bfloat16).astype(jnp.float32)
    h2 = feed_forward(h1, *part_two).astype(jnp.bfloat16).astype(jnp.float32)
    h3, _, attended_three, sums_three = third_forward(h2, length, shared, *part_three)
    h3 = h3.astype(jnp.bfloat16).astype(jnp.float32)
    output = feed_forward(h3, *part_four)

    valid_rows = (jnp.arange(tokens.shape[0]) < length)[:, None]
    seeded = jnp.where(valid_rows, cotangent.astype(jnp.float32), 0.0)
    grad_h3, grads_four = feed_backward(h3, seeded, *part_four)
    grad_h3 = grad_h3.astype(jnp.bfloat16).astype(jnp.float32)
    grad_h2, shared_grad, grads_three = third_backward(
        h2, length, shared, attended_three, sums_three, grad_h3, *part_three
    )
    grad_h2 = grad_h2.astype(jnp.bfloat16).astype(jnp.float32)
    grad_h1, grads_two = feed_backward(h1, grad_h2, *part_two)
    grad_h1 = grad_h1.astype(jnp.bfloat16).astype(jnp.float32)
    input_grad, grads_one = first_backward(
        entry,
        length,
        attended_one,
        sums_one,
        grad_h1,
        shared_grad.astype(jnp.float32),
        *part_one,
    )
    local = shortened(grads_one + grads_two + grads_three + grads_four)
    totals = lax.psum(local, ("section", "dp"))
    return (output, input_grad) + tuple(total.astype(jnp.float32) for total in totals)


def solution(mesh):
    return jax.shard_map(
        shards,
        mesh=mesh,
        in_specs=(
            P(("section", "dp"), None),
            P(("section", "dp"), None),
            P(None, "dp"),
            P("section"),
            P(None, "section"),
            P(None, "section"),
            P("section"),
            P(None, "section"),
            P("section", None),
            P("section"),
            P(None, "section"),
            P(None, "section"),
            P(None, "section"),
            P("section"),
            P(None, "section"),
            P("section", None),
        ),
        out_specs=(
            P(("section", "dp"), None),
            P(("section", "dp"), None),
            P(),
            P(),
            P(),
            P(),
            P(),
            P(),
            P(),
            P(),
            P(),
            P(),
            P(),
            P(),
            P(),
        ),
        check_vma=False,
    )
```

```python
import functools

import jax
import jax.numpy as jnp
from jax import lax
from jax.experimental import pallas as pl
from jax.experimental.pallas import tpu as pltpu
from jax.sharding import PartitionSpec as P

D = 384
HEADS = 6
HEAD = 64
SHARED = 3
QUARTERS = 4

EPSILON = 1e-05
MASKED = -1e30
GELU_SCALE = 0.7978845608028654
GELU_CUBE = 0.044715

f32 = jnp.float32
bf16 = jnp.bfloat16
VMEM_BYTES = 32 * 1024 * 1024


def nn(left, right):
    return jnp.dot(left, right, preferred_element_type=f32)


def nt(left, right):
    return lax.dot_general(left, right, (((1,), (1,)), ((), ())), preferred_element_type=f32)


def centre(hidden):
    centred = hidden - jnp.mean(hidden, -1, keepdims=True)
    spread = jnp.mean(centred * centred, -1, keepdims=True)
    rstd = lax.rsqrt(spread + EPSILON)
    return centred * rstd, rstd


def norm_back(scaled, rstd, gain, grad):
    grad_gain = jnp.sum(grad * scaled, 0, keepdims=True)
    c = grad * gain
    along = jnp.mean(c * scaled, -1, keepdims=True)
    return rstd * (c - jnp.mean(c, -1, keepdims=True) - scaled * along), grad_gain


def swapped(rank):
    return ((rank & 1) << 1) | (rank >> 1)


def place_pieces(info, pieces, held):
    own0, own1, near, far, both, other_near, other_far, other_both = pieces
    section, core = info[0], info[1]
    held[0, section] = own0[...]
    held[1, section] = own1[...]
    one, two, three = section ^ 1, section ^ 2, section ^ 3

    @pl.when(core == 0)
    def _():
        held[0, one] = near[...]
        held[0, two] = far[...]
        held[0, three] = both[...]
        held[1, two] = other_near[...]
        held[1, one] = other_far[...]
        held[1, three] = other_both[...]

    @pl.when(core != 0)
    def _():
        held[1, two] = near[...]
        held[1, one] = far[...]
        held[1, three] = both[...]
        held[0, one] = other_near[...]
        held[0, two] = other_far[...]
        held[0, three] = other_both[...]


def put(info, keep, send, half, quarter, value, rows=None):
    section, core = info[0], info[1]
    rank = quarter ^ section
    if half == 1:
        rank = swapped(rank)
    where = (rank,) if rows is None else (rank, pl.ds(*rows))

    @pl.when(core == half)
    def _():
        keep[where] = value

    @pl.when(core != half)
    def _():
        send[where] = value


def usable(rows, length):
    key_index = lax.broadcasted_iota(jnp.int32, (rows, rows), 0)
    query_index = lax.broadcasted_iota(jnp.int32, (rows, rows), 1)
    return (key_index <= query_index) & (key_index < length)


def head_lanes(rows, side):
    lane = lax.broadcasted_iota(jnp.int32, (rows, 2 * HEAD), 1)
    return (lane < HEAD) if side == 0 else (lane >= HEAD)


def attend(mixed, length, stats):
    rows = mixed.shape[0]
    allowed = usable(rows, length)
    values_across = mixed[:, 2 * D :].T
    outs = []
    for pair in range(HEADS // 2):
        at = 2 * HEAD * pair
        queries = mixed[:, at : at + 2 * HEAD]
        key_rows = mixed[:, D + at : D + at + 2 * HEAD]
        for side in range(2):
            head = 2 * pair + side
            one_head = jnp.where(head_lanes(rows, side), queries, 0)
            scores = jnp.where(allowed, nt(key_rows, one_head) * HEAD ** (-0.5), MASKED)
            peak = jnp.max(scores, 0, keepdims=True)
            raised = jnp.exp(scores - peak)
            inverse = 1.0 / jnp.sum(raised, 0, keepdims=True)
            stats[head : head + 1, :] = peak
            stats[8 + head : 9 + head, :] = inverse
            probability = (raised * inverse).astype(bf16)
            outs.append(nn(values_across[HEAD * head : HEAD * head + HEAD], probability))
    return jnp.concatenate(outs, 0).T.astype(bf16)


def attend_back(mixed, grad_heads, length, stats, grad_mixed):
    rows = mixed.shape[0]
    allowed = usable(rows, length)
    keys_across = mixed[:, D : 2 * D].T
    query_parts = []
    for pair in range(HEADS // 2):
        at = 2 * HEAD * pair
        queries = mixed[:, at : at + 2 * HEAD]
        key_rows = mixed[:, D + at : D + at + 2 * HEAD]
        values = mixed[:, 2 * D + at : 2 * D + at + 2 * HEAD]
        grads = grad_heads[:, at : at + 2 * HEAD]
        key_grad = jnp.zeros((rows, 2 * HEAD), f32)
        value_grad = jnp.zeros((rows, 2 * HEAD), f32)
        for side in range(2):
            head = 2 * pair + side
            lanes = head_lanes(rows, side)
            one_head = jnp.where(lanes, queries, 0)
            one_grad = jnp.where(lanes, grads, 0)
            scores = jnp.where(allowed, nt(key_rows, one_head) * HEAD ** (-0.5), MASKED)
            probability = jnp.exp(scores - stats[head : head + 1, :]) * stats[8 + head : 9 + head, :]
            grad_prob = nt(values, one_grad)
            middle = jnp.sum(probability * grad_prob, 0, keepdims=True)
            grad_scores = (probability * (grad_prob - middle)).astype(bf16)
            key_grad += nn(grad_scores, one_head)
            value_grad += nn(probability.astype(bf16), one_grad)
            query_parts.append(nn(keys_across[HEAD * head : HEAD * head + HEAD], grad_scores))
        grad_mixed[:, D + at : D + at + 2 * HEAD] = (key_grad * HEAD ** (-0.5)).astype(bf16)
        grad_mixed[:, 2 * D + at : 2 * D + at + 2 * HEAD] = value_grad.astype(bf16)
    grad_mixed[:, :D] = (jnp.concatenate(query_parts, 0).T * HEAD ** (-0.5)).astype(bf16)


def first_kernel(
    info, tokens, *rest
):
    pieces = rest[:8]
    h1, mixed, attended, stats, mixing, output, mixing_three, output_three, gains, held = rest[8:]
    place_pieces(info, pieces, held)
    mixing_three[:, 2 * D : 2 * D + SHARED * HEAD] = jnp.zeros((D, SHARED * HEAD), bf16)
    for j in range(QUARTERS):
        one = held[0, j]
        mixing[:, 288 * j : 288 * j + 288] = one[:, :288]
        output[:, 96 * j : 96 * j + 96] = one[:, 288:]
        three = held[1, j]
        mixing_three[:, 192 * j : 192 * j + 192] = three[:, :192]
        mixing_three[:, 960 + 48 * j : 960 + 48 * j + 48] = three[:, 192:240]
        output_three[:, 96 * j : 96 * j + 96] = three[:, 240:336]
        edge = held[1, j, 0:16, 256:384].astype(f32)[:, 80:]
        for k in range(4):
            for i in range(2):
                gains[k : k + 1, 96 * j + 48 * i : 96 * j + 48 * i + 48] = edge[2 * k + i : 2 * k + i + 1]
    hidden = tokens[...].astype(f32)
    scaled, _ = centre(hidden)
    normed = (scaled * gains[0:1, :]).astype(bf16)
    mixed[...] = nn(normed, mixing[...]).astype(bf16)
    attended[...] = attend(mixed, info[2], stats)
    h1[...] = (hidden + nn(attended[...], output[...])).astype(bf16)


def middle_kernel(info, h1, gains, mixing_three, output_three, mixed_one, *rest):
    pieces = rest[:8]
    h2, held, h3, mixed, attended, stats = rest[8:]
    place_pieces(info, pieces, held)
    hidden = h1[...].astype(f32)
    scaled, _ = centre(hidden)
    normed = (scaled * gains[1:2, :]).astype(bf16)
    total = hidden
    for j in range(QUARTERS):
        upward = nn(normed, held[0, j])
        bent = jnp.tanh(GELU_SCALE * (upward + GELU_CUBE * upward * upward * upward))
        total += nn((0.5 * upward * (1.0 + bent)).astype(bf16), held[1, j])
    h2[...] = total.astype(bf16)
    hidden = h2[...].astype(f32)
    scaled, _ = centre(hidden)
    normed = (scaled * gains[2:3, :]).astype(bf16)
    mixed[...] = nn(normed, mixing_three[...]).astype(bf16)
    shared_width = SHARED * HEAD
    mixed[:, 2 * D : 2 * D + shared_width] = mixed_one[:, 2 * D : 2 * D + shared_width]
    attended[...] = attend(mixed, info[2], stats)
    h3[...] = (hidden + nn(attended[...], output_three[...])).astype(bf16)


def feed_parts(upward):
    square = upward * upward
    bent = jnp.tanh(GELU_SCALE * (upward + GELU_CUBE * square * upward))
    active = 0.5 * upward * (1.0 + bent)
    slope = 0.5 * (1.0 + bent) + 0.5 * upward * (1.0 - bent * bent) * (
        GELU_SCALE * (1.0 + 3.0 * GELU_CUBE * square)
    )
    return active.astype(bf16), slope


def feed_back(info, held, normed, grad_out, actives, slopes, keep, send):
    grad_normed = jnp.zeros(normed.shape, f32)
    normed_across = normed.T
    for j in range(QUARTERS):
        up, down = held[0, j], held[1, j]
        if slopes is None:
            active, slope = feed_parts(nn(normed, up))
        else:
            active, slope = actives[j], slopes[j]
        grad_upward = (nt(grad_out, down) * slope).astype(bf16)
        put(info, keep, send, 1, j, nn(active.T, grad_out).astype(bf16))
        put(info, keep, send, 0, j, nn(normed_across, grad_upward).astype(bf16))
        grad_normed += nt(grad_upward, up)
    return grad_normed


def last_kernel(info, h3, gains, cotangent, *rest):
    pieces = rest[:8]
    out, grad_h3, keep, send, grad_gain, held, actives, slopes = rest[8:]
    place_pieces(info, pieces, held)
    hidden = h3[...].astype(f32)
    scaled, rstd = centre(hidden)
    gain = gains[3:4, :]
    normed = (scaled * gain).astype(bf16)
    total = hidden
    for j in range(QUARTERS):
        active, slope = feed_parts(nn(normed, held[0, j]))
        actives[j] = active
        slopes[j] = slope
        total += nn(active, held[1, j])
    out[...] = total
    row = lax.broadcasted_iota(jnp.int32, hidden.shape, 0)
    grad_out = jnp.where(row < info[2], cotangent[...].astype(f32), 0.0)
    grad_normed = feed_back(
        info, held, normed, grad_out.astype(bf16), actives, slopes, keep, send
    )
    grad_hidden, one_gain = norm_back(scaled, rstd, gain, grad_normed)
    grad_gain[0:1, :] = one_gain
    grad_h3[...] = (grad_out + grad_hidden).astype(bf16)


def attention_back(info, hidden, grad_out, mixed, attended, stats, mixing, output, gain, grad_mixed, shared):
    scaled, rstd = centre(hidden)
    normed_across = (scaled * gain).astype(bf16).T
    grad_heads = nt(grad_out, output[...]).astype(bf16)
    grad_output = nn(attended[...].T, grad_out).astype(bf16)
    attend_back(mixed, grad_heads, info[2], stats, grad_mixed)
    shared(grad_mixed)
    grad_mixing = nn(normed_across, grad_mixed[...]).astype(bf16)
    grad_hidden, grad_gain = norm_back(scaled, rstd, gain, nt(grad_mixed[...], mixing[...]))
    return grad_hidden, grad_gain, grad_mixing, grad_output


def third_back_kernel(
    info, h2, gains, grad_h3, mixed, attended, stats, mixing, output,
    grad_h2, grad_weights, grad_shared, grad_gain, grad_mixed,
):
    shared_width = SHARED * HEAD

    def hand_over(grads):
        grad_shared[...] = grads[:, 2 * D : 2 * D + shared_width]
        grads[:, 2 * D : 2 * D + shared_width] = jnp.zeros((grads.shape[0], shared_width), bf16)

    grad_hidden, one_gain, grad_mixing, grad_output = attention_back(
        info, h2[...].astype(f32), grad_h3[...], mixed, attended, stats, mixing, output,
        gains[2:3, :], grad_mixed, hand_over,
    )
    grad_weights[0, :D] = grad_mixing[:, :D]
    grad_weights[0, D:] = grad_mixing[:, D : 2 * D]
    grad_weights[1, :D] = grad_mixing[:, 2 * D :]
    grad_weights[1, D:] = grad_output
    grad_gain[0:1, :] = one_gain
    grad_h2[...] = (grad_h3[...].astype(f32) + grad_hidden).astype(bf16)


def second_back_kernel(info, h1, gains, grad_h2, held, grad_h1, keep, send, grad_gain):
    scaled, rstd = centre(h1[...].astype(f32))
    gain = gains[1:2, :]
    normed = (scaled * gain).astype(bf16)
    grad_normed = feed_back(info, held, normed, grad_h2[...], None, None, keep, send)
    grad_hidden, one_gain = norm_back(scaled, rstd, gain, grad_normed)
    grad_gain[0:1, :] = one_gain
    grad_h1[...] = (grad_h2[...].astype(f32) + grad_hidden).astype(bf16)


def first_back_kernel(
    info, tokens, gains, grad_h1, mixed, attended, stats, mixing, output,
    grad_shared, third_weights, gain_two, gain_three, gain_four,
    input_grad, keep, send, grad_mixed, grad_weights,
):
    shared_width = SHARED * HEAD

    def take_over(grads):
        at = slice(2 * D, 2 * D + shared_width)
        grads[:, at] = (grads[:, at].astype(f32) + grad_shared[...].astype(f32)).astype(bf16)

    grad_hidden, gain_one, grad_mixing, grad_output = attention_back(
        info, tokens[...].astype(f32), grad_h1[...], mixed, attended, stats, mixing, output,
        gains[0:1, :], grad_mixed, take_over,
    )
    input_grad[...] = grad_h1[...].astype(f32) + grad_hidden
    grad_weights[0, :D] = grad_mixing[:, :D]
    grad_weights[0, D:] = grad_mixing[:, D : 2 * D]
    grad_weights[1, :D] = grad_mixing[:, 2 * D :]
    grad_weights[1, D:] = grad_output
    part = 2 * D // QUARTERS
    for half in range(2):
        for j in range(QUARTERS):
            put(info, keep, send, half, j, grad_weights[half, part * j : part * (j + 1)], (0, part))
            put(info, keep, send, half, j, third_weights[half, part * j : part * (j + 1)], (part, part))
    rows = []
    for grad in (gain_one, gain_two[0:1, :], gain_three[0:1, :], gain_four[0:1, :]):
        rows += [grad[:, :shared_width], grad[:, shared_width:]]
    rows.append(jnp.zeros((8, shared_width), f32))
    block = jnp.concatenate(rows, 0).astype(bf16)
    section, core = info[0], info[1]
    rank = swapped(section)

    @pl.when(core == 1)
    def _():
        keep[rank, part : part + 16, :shared_width] = block

    @pl.when(core != 1)
    def _():
        send[rank, part : part + 16, :shared_width] = block


def unpack_feed_kernel(info, *rest):
    pieces, (up, down, wide, sems) = rest[:8], rest[8:]
    section, core = info[0], info[1]

    def copies(slot, rank):
        own = slot < 4
        half_zero = (core == 0) if own else (core != 0)
        at0 = pl.multiple_of((section ^ rank) * D, D)
        at1 = pl.multiple_of((section ^ ((rank & 1) << 1 | rank >> 1)) * D, D)
        return half_zero, pltpu.make_async_copy(
            wide.at[slot], up.at[:, pl.ds(at0, D)], sems.at[slot]
        ), pltpu.make_async_copy(wide.at[slot], down.at[pl.ds(at1, D), :], sems.at[slot])

    for slot in range(8):
        wide[slot] = pieces[slot][...].astype(f32)
        half_zero, to_up, to_down = copies(slot, slot % 4)
        pl.when(half_zero)(to_up.start)
        pl.when(jnp.logical_not(half_zero))(to_down.start)
    for slot in range(8):
        half_zero, to_up, to_down = copies(slot, slot % 4)
        pl.when(half_zero)(to_up.wait)
        pl.when(jnp.logical_not(half_zero))(to_down.wait)


def unpack_attention_kernel(info, *rest):
    pieces = rest[:8]
    mixing, output, pair, fresh, output_three, g1, g2, g3, g4, wide, narrow, sems = rest[8:]
    section, core = info[0], info[1]
    part = 2 * D // QUARTERS
    shared_width = SHARED * HEAD

    def plan(slot):
        rank = slot % 4
        half_zero = (core == 0) if slot < 4 else (core != 0)
        j0, j1 = section ^ rank, section ^ swapped(rank)
        col0 = pl.multiple_of((j0 >> 1) * D, D)
        row0 = pl.multiple_of((j0 & 1) * part, part)
        row1 = pl.multiple_of((j1 & 1) * part, part)
        top, low = wide.at[slot, :part], wide.at[slot, part:]
        st, sl = sems.at[slot, 0], sems.at[slot, 1]
        copy = pltpu.make_async_copy
        is_v = j1 < 2
        not_zero = jnp.logical_not(half_zero)
        return [
            (half_zero, copy(top, mixing.at[pl.ds(row0, part), pl.ds(col0, D)], st)),
            (half_zero, copy(low, pair.at[pl.ds(row0, part), pl.ds(col0, D)], sl)),
            (not_zero & is_v, copy(top, mixing.at[pl.ds(row1, part), 2 * D :], st)),
            (not_zero & is_v, copy(narrow.at[slot], fresh.at[pl.ds(row1, part), :], sl)),
            (not_zero & (j1 >= 2), copy(top, output.at[pl.ds(row1, part), :], st)),
            (not_zero & (j1 >= 2), copy(low, output_three.at[pl.ds(row1, part), :], sl)),
        ], not_zero & is_v, not_zero & (j1 == 0)

    for slot in range(8):
        wide[slot] = pieces[slot][...].astype(f32)
        steps, is_fresh, has_gains = plan(slot)

        @pl.when(is_fresh)
        def _():
            narrow[slot] = wide[slot, part:, shared_width:]

        @pl.when(has_gains)
        def _():
            block = wide[slot, part : part + 8, :shared_width]
            for k, ref in enumerate((g1, g2, g3, g4)):
                ref[...] = jnp.concatenate([block[2 * k : 2 * k + 1], block[2 * k + 1 : 2 * k + 2]], 1)

        for flag, copy in steps:
            pl.when(flag)(copy.start)
    for slot in range(8):
        for flag, copy in plan(slot)[0]:
            pl.when(flag)(copy.wait)


def call(body, name, outs, scratch, args, flops=10**9, any_outs=()):
    vmem = pl.BlockSpec(memory_space=pltpu.VMEM)
    return pl.pallas_call(
        body,
        name=name,
        out_shape=[jax.ShapeDtypeStruct(shape, dtype) for shape, dtype in outs],
        in_specs=[pl.BlockSpec(memory_space=pltpu.SMEM)] + [vmem] * (len(args) - 1),
        out_specs=[
            pl.BlockSpec(memory_space=pl.ANY) if i in any_outs else vmem for i in range(len(outs))
        ],
        scratch_shapes=scratch,
        compiler_params=pltpu.CompilerParams(vmem_limit_bytes=VMEM_BYTES),
        cost_estimate=pl.CostEstimate(flops=flops, bytes_accessed=10**6, transcendentals=10**6),
    )(*args)


def partner_pairs(sections, groups, kind):
    found = []
    for section in range(sections):
        for group in range(groups):
            core = group & 1
            to_section, to_group = section, group
            if kind == "near":
                to_section = section ^ (1 if core == 0 else 2)
            elif kind == "far":
                to_section = section ^ (2 if core == 0 else 1)
            else:
                to_group = group ^ kind
            found.append((section * groups + group, to_section * groups + to_group))
    return found


def partner(value, kind):
    sections, groups = lax.axis_size("section"), lax.axis_size("dp")
    return lax.ppermute(value, ("section", "dp"), partner_pairs(sections, groups, kind))


def gather_chunk(own0, own1, core):
    mine = jnp.where(core == 0, own0, own1)
    near = partner(mine, "near")
    far = partner(mine, "far")
    both = partner(near, "far")
    return (own0, own1, near, far, both) + tuple(partner(v, 1) for v in (near, far, both))


def add(left, right):
    return (left.astype(f32) + right.astype(f32)).astype(bf16)


def reduce_chunk(keep, send):
    groups = lax.axis_size("dp")
    from_core = partner(send, 1)
    p3 = add(keep[3], from_core[3])
    p1 = add(keep[1], from_core[1])
    r3 = partner(p3, "near")
    r1 = partner(p1, "near")
    p2 = (keep[2].astype(f32) + from_core[2].astype(f32) + r3.astype(f32)).astype(bf16)
    r2 = partner(p2, "far")
    own = (
        keep[0].astype(f32) + from_core[0].astype(f32) + r1.astype(f32) + r2.astype(f32)
    ).astype(bf16)
    if groups > 2:
        rows = own.shape[0] // 2
        bit = (lax.axis_index("dp") >> 1) & 1
        low, high = own[:rows], own[rows:]
        kept = add(jnp.where(bit == 0, low, high), partner(jnp.where(bit == 0, high, low), 2))
        step = 4
        while step < groups:
            kept = add(kept, partner(kept, step))
            step *= 2
        back = partner(kept, 2)
        own = jnp.concatenate(
            [jnp.where(bit == 0, kept, back), jnp.where(bit == 0, back, kept)], 0
        )
    g2 = partner(own, "far")
    g1 = partner(own, "near")
    g3 = partner(g2, "near")
    mine = (own, g1, g2, g3)
    return mine + tuple(partner(v, 1) for v in mine)


def shards(
    tokens,
    cotangent,
    lengths,
    gain_one,
    mixing_one,
    output_one,
    gain_two,
    up_two,
    down_two,
    gain_three,
    pair_three,
    fresh_three,
    output_three,
    gain_four,
    up_four,
    down_four,
):
    rows = tokens.shape[0]
    section = lax.axis_index("section")
    core = lax.axis_index("dp") & 1
    info = jnp.stack([section, core, lengths[section, 0]]).astype(jnp.int32)

    edge = jnp.stack([gain_one, gain_two, gain_three, gain_four]).reshape(8, 48)
    edge = jnp.concatenate([edge, jnp.zeros((D - 8, 48), bf16)], 0)
    one = jnp.concatenate([mixing_one, output_one], 1)
    three = jnp.concatenate([pair_three, fresh_three, output_three, edge], 1)
    chunk_one = gather_chunk(one, three, core)
    chunk_two = gather_chunk(up_two, down_two, core)
    chunk_four = gather_chunk(up_four, down_four, core)

    row = (rows, D)
    wide_row = (rows, 3 * D)
    square = (D, D)
    held = (2, QUARTERS, D, D)
    stat = ((16, rows), f32)
    gain_row = ((8, D), f32)
    h1, mixed_one, attended_one, stats_one, mixing, output, mixing_three, out_three, gains = call(
        first_kernel, "first_forward",
        [(row, bf16), (wide_row, bf16), (row, bf16), stat, ((D, 3 * D), bf16), (square, bf16),
         ((D, 3 * D), bf16), (square, bf16), gain_row],
        [pltpu.VMEM(held, bf16)],
        (info, tokens) + chunk_one,
    )
    h2, held_two, h3, mixed_three, attended_three, stats_three = call(
        middle_kernel, "second_third_forward",
        [(row, bf16), (held, bf16), (row, bf16), (wide_row, bf16), (row, bf16), stat],
        [],
        (info, h1, gains, mixing_three, out_three, mixed_one) + chunk_two,
    )
    packed = ((QUARTERS, D, D), bf16)
    out, grad_h3, keep_four, send_four, gain_grad_four = call(
        last_kernel, "fourth_both",
        [(row, f32), (row, bf16), packed, packed, gain_row],
        [pltpu.VMEM(held, bf16), pltpu.VMEM((QUARTERS,) + row, bf16), pltpu.VMEM((QUARTERS,) + row, f32)],
        (info, h3, gains, cotangent) + chunk_four,
    )
    grad_h2, third_weights, grad_shared, gain_grad_three = call(
        third_back_kernel, "third_backward",
        [(row, bf16), ((2, 2 * D, D), bf16), ((rows, SHARED * HEAD), bf16), gain_row],
        [pltpu.VMEM(wide_row, bf16)],
        (info, h2, gains, grad_h3, mixed_three, attended_three, stats_three, mixing_three, out_three),
    )
    grad_h1, keep_two, send_two, gain_grad_two = call(
        second_back_kernel, "second_backward",
        [(row, bf16), packed, packed, gain_row],
        [],
        (info, h1, gains, grad_h2, held_two),
    )
    input_grad, keep_one, send_one = call(
        first_back_kernel, "first_backward",
        [(row, f32), packed, packed],
        [pltpu.VMEM(wide_row, bf16), pltpu.VMEM((2, 2 * D, D), bf16)],
        (info, tokens, gains, grad_h1, mixed_one, attended_one, stats_one, mixing, output,
         grad_shared, third_weights, gain_grad_two, gain_grad_three, gain_grad_four),
    )

    feed_outs = [((D, 4 * D), f32), ((4 * D, D), f32)]
    feed_scratch = [pltpu.VMEM((8, D, D), f32), pltpu.SemaphoreType.DMA((8,))]
    grad_up_four, grad_down_four = call(
        unpack_feed_kernel, "unpack_four", feed_outs, feed_scratch,
        (info,) + reduce_chunk(keep_four, send_four), any_outs=(0, 1),
    )
    grad_up_two, grad_down_two = call(
        unpack_feed_kernel, "unpack_two", feed_outs, feed_scratch,
        (info,) + reduce_chunk(keep_two, send_two), any_outs=(0, 1),
    )
    part = 2 * D // QUARTERS
    gain_out = ((1, D), f32)
    mixing_g, output_g, pair_g, fresh_g, output_three_g, g1, g2, g3, g4 = call(
        unpack_attention_kernel, "unpack_attention",
        [((D, 3 * D), f32), (square, f32), ((D, 2 * D), f32), ((D, D // 2), f32), (square, f32)]
        + [gain_out] * 4,
        [pltpu.VMEM((8, D, D), f32), pltpu.VMEM((8, part, part), f32),
         pltpu.SemaphoreType.DMA((8, 2))],
        (info,) + reduce_chunk(keep_one, send_one), any_outs=(0, 1, 2, 3, 4),
    )
    g1, g2, g3, g4 = (g.reshape(D) for g in (g1, g2, g3, g4))
    return (
        out, input_grad, g1, mixing_g, output_g, g2, grad_up_two, grad_down_two,
        g3, pair_g, fresh_g, output_three_g, g4, grad_up_four, grad_down_four,
    )


def solution(mesh):
    return jax.shard_map(
        shards,
        mesh=mesh,
        in_specs=(
            P(("section", "dp"), None),
            P(("section", "dp"), None),
            P(None, "dp"),
            P("section"),
            P(None, "section"),
            P(None, "section"),
            P("section"),
            P(None, "section"),
            P("section", None),
            P("section"),
            P(None, "section"),
            P(None, "section"),
            P(None, "section"),
            P("section"),
            P(None, "section"),
            P("section", None),
        ),
        out_specs=(P(("section", "dp"), None), P(("section", "dp"), None)) + (P(),) * 13,
        check_vma=False,
    )
```

```python
import functools

import jax
import jax.numpy as jnp
from jax import lax
from jax.experimental import pallas as pl
from jax.experimental.pallas import tpu as pltpu
from jax.sharding import PartitionSpec as P

D = 384
HEADS = 6
HEAD = 64
SHARED = 3
QUARTERS = 4

EPSILON = 1e-05
MASKED = -1e30
GELU_SCALE = 0.7978845608028654
GELU_CUBE = 0.044715

f32 = jnp.float32
bf16 = jnp.bfloat16


def nn(left, right):
    return jnp.dot(left, right, preferred_element_type=f32)


def nt(left, right):
    return lax.dot_general(left, right, (((1,), (1,)), ((), ())), preferred_element_type=f32)


def centre(hidden):
    centred = hidden - jnp.mean(hidden, -1, keepdims=True)
    spread = jnp.mean(centred * centred, -1, keepdims=True)
    rstd = lax.rsqrt(spread + EPSILON)
    return centred * rstd, rstd


def norm_back(scaled, rstd, gain, grad):
    grad_gain = jnp.sum(grad * scaled, 0, keepdims=True)
    c = grad * gain
    along = jnp.mean(c * scaled, -1, keepdims=True)
    return rstd * (c - jnp.mean(c, -1, keepdims=True) - scaled * along), grad_gain


def swapped(rank):
    return ((rank & 1) << 1) | (rank >> 1)


def place():
    return lax.axis_index("section"), lax.axis_index("dp") & 1


def select_pieces(pieces):
    near, far, both, other_near, other_far, other_both = pieces
    first = place()[1] == 0

    def pick(left, right):
        return jnp.where(first, left[...], right[...])

    return (
        (pick(near, other_near), pick(far, other_far), pick(both, other_both)),
        (pick(other_far, far), pick(other_near, near), pick(other_both, both)),
    )


def put(keep, send, rank, half_zero, half_one, rows=None):
    first = place()[1] == 0
    zero, one = rank, swapped(rank)
    kept, sent = jnp.where(first, zero, one), jnp.where(first, one, zero)
    if rows is None:
        keep[kept] = jnp.where(first, half_zero, half_one)
        send[sent] = jnp.where(first, half_one, half_zero)
    else:
        keep[kept, pl.ds(*rows)] = jnp.where(first, half_zero, half_one)
        send[sent, pl.ds(*rows)] = jnp.where(first, half_one, half_zero)


def usable(rows, limits):
    key_index = lax.broadcasted_iota(jnp.int32, (rows, rows), 0)
    query_index = lax.broadcasted_iota(jnp.int32, (rows, rows), 1)
    return (key_index <= query_index) & (key_index < limits[0:1, :rows])


def head_lanes(rows, side):
    lane = lax.broadcasted_iota(jnp.int32, (rows, 2 * HEAD), 1)
    return (lane < HEAD) if side == 0 else (lane >= HEAD)


def attend(mixed, limits, probabilities):
    rows = mixed.shape[0]
    allowed = usable(rows, limits)
    values_across = mixed[:, 2 * D :].T
    outs = []
    for pair in range(HEADS // 2):
        at = 2 * HEAD * pair
        queries = mixed[:, at : at + 2 * HEAD]
        key_rows = mixed[:, D + at : D + at + 2 * HEAD]
        for side in range(2):
            head = 2 * pair + side
            one_head = jnp.where(head_lanes(rows, side), queries, 0)
            scores = jnp.where(allowed, nt(key_rows, one_head) * HEAD ** (-0.5), MASKED)
            peak = jnp.max(scores, 0, keepdims=True)
            raised = jnp.exp(scores - peak)
            inverse = 1.0 / jnp.sum(raised, 0, keepdims=True)
            probability = raised * inverse
            probabilities[head] = probability
            outs.append(nn(values_across[HEAD * head : HEAD * head + HEAD], probability.astype(bf16)))
    return jnp.concatenate(outs, 0).T.astype(bf16)


def attend_back(mixed, grad_heads, probabilities, grad_mixed):
    rows = mixed.shape[0]
    keys_across = mixed[:, D : 2 * D].T
    query_parts = []
    for pair in range(HEADS // 2):
        at = 2 * HEAD * pair
        queries = mixed[:, at : at + 2 * HEAD]
        values = mixed[:, 2 * D + at : 2 * D + at + 2 * HEAD]
        grads = grad_heads[:, at : at + 2 * HEAD]
        key_grad = jnp.zeros((rows, 2 * HEAD), f32)
        value_grad = jnp.zeros((rows, 2 * HEAD), f32)
        for side in range(2):
            head = 2 * pair + side
            lanes = head_lanes(rows, side)
            one_head = jnp.where(lanes, queries, 0)
            one_grad = jnp.where(lanes, grads, 0)
            probability = probabilities[head]
            grad_prob = nt(values, one_grad)
            middle = jnp.sum(probability * grad_prob, 0, keepdims=True)
            grad_scores = (probability * (grad_prob - middle)).astype(bf16)
            key_grad += nn(grad_scores, one_head)
            value_grad += nn(probability.astype(bf16), one_grad)
            query_parts.append(nn(keys_across[HEAD * head : HEAD * head + HEAD], grad_scores))
        grad_mixed[:, D + at : D + at + 2 * HEAD] = (key_grad * HEAD ** (-0.5)).astype(bf16)
        grad_mixed[:, 2 * D + at : 2 * D + at + 2 * HEAD] = value_grad.astype(bf16)
    grad_mixed[:, :D] = (jnp.concatenate(query_parts, 0).T * HEAD ** (-0.5)).astype(bf16)


def prepare_kernel(
    mixing, output, pair, fresh, output_three, gain_one, gain_two, gain_three, gain_four,
    up_two, down_two, up_four, down_four, lengths,
    one, three, mine_one, mine_two, mine_four, limits, edge, narrow_one, narrow_two, narrow_three, narrow_four, sems,
):
    core = place()[1]
    count = mixing.shape[0]
    wide, small = output.shape[0], fresh.shape[0]
    halves = [[(mixing, 0), (output, count)],
              [(pair, 0), (fresh, 2 * wide), (output_three, 2 * wide + small)]]
    last = 3 * wide + small
    copies = []
    for half, target in ((0, one), (1, three)):
        for source, row in halves[half]:
            rows = source.shape[0]
            copies.append((None, source, target.at[pl.ds(row, rows)]))
            copies.append((half, source, mine_one.at[pl.ds(row, rows)]))
    copies += [(0, up_two, mine_two), (1, down_two, mine_two)]
    copies += [(0, up_four, mine_four), (1, down_four, mine_four)]
    made = [
        (half, pltpu.make_async_copy(source, target, sems.at[i]))
        for i, (half, source, target) in enumerate(copies)
    ]
    for half, copy in made:
        if half is None:
            copy.start()
        else:
            pl.when(core == half)(copy.start)
    gains = [
        pltpu.make_async_copy(gain, narrow, sems.at[len(copies) + k])
        for k, (gain, narrow) in enumerate(
            ((gain_one, narrow_one), (gain_two, narrow_two), (gain_three, narrow_three), (gain_four, narrow_four))
        )
    ]
    for copy in gains:
        copy.start()
    limits[...] = jnp.full(limits.shape, lengths[0, place()[0]], jnp.int32)
    edge[...] = jnp.zeros_like(edge)
    for k, narrow in enumerate((narrow_one, narrow_two, narrow_three, narrow_four)):
        gains[k].wait()
        edge[k : k + 1, : narrow.shape[0]] = narrow[...].astype(f32).reshape(1, narrow.shape[0])
    rows = D - last
    block = jnp.concatenate([edge[...], jnp.zeros((rows - 8, D), f32)], 0).astype(bf16)
    three[last:] = block

    @pl.when(core != 0)
    def _():
        mine_one[last:] = block

    for half, copy in made:
        if half is None:
            copy.wait()
        else:
            pl.when(core == half)(copy.wait)


def first_kernel(limits, tokens, own0, own1, *rest):
    h1, mixed, attended, probabilities, mixing, output, mixing_three, output_three, gains, held = rest[6:]
    section = place()[0]
    for half, (own, came) in enumerate(zip((own0, own1), select_pieces(rest[:6]))):
        held[half, section] = own[...]
        for rank in (1, 2, 3):
            held[half, section ^ rank] = came[rank - 1]
    shared_width = SHARED * HEAD
    mixing_three[2 * D : 2 * D + shared_width, :] = jnp.zeros((shared_width, D), bf16)
    for j in range(QUARTERS):
        mixing[288 * j : 288 * j + 288, :] = held[0, j, :288]
        output[96 * j : 96 * j + 96, :] = held[0, j, 288:]
        mixing_three[192 * j : 192 * j + 192, :] = held[1, j, :192]
        mixing_three[960 + 48 * j : 960 + 48 * j + 48, :] = held[1, j, 192:240]
        output_three[96 * j : 96 * j + 96, :] = held[1, j, 240:336]
        gains[0:8, 96 * j : 96 * j + 96] = held[1, j, 336:352, :96].astype(f32)[:8]
    hidden = tokens[...].astype(f32)
    scaled, _ = centre(hidden)
    normed = (scaled * gains[0:1, :]).astype(bf16)
    mixed[...] = nt(normed, mixing[...]).astype(bf16)
    attended[...] = attend(mixed, limits, probabilities)
    h1[...] = (hidden + nt(attended[...], output[...])).astype(bf16)


def bring(own0, own1, held, sems):
    copies = [
        pltpu.make_async_copy(own0, held.at[0, 0], sems.at[0]),
        pltpu.make_async_copy(own1, held.at[1, 0], sems.at[1]),
    ]
    for copy in copies:
        copy.start()
    return copies


def middle_kernel(limits, h1, gains, mixing_three, output_three, mixed_one, own0, own1, *rest):
    h2, held, h3, mixed, attended, probabilities, actives, slopes, sems = rest[6:]
    copies = bring(own0, own1, held, sems)
    hidden = h1[...].astype(f32)
    scaled, _ = centre(hidden)
    normed = (scaled * gains[1:2, :]).astype(bf16)
    ups, downs = select_pieces(rest[:6])
    total = hidden
    for rank in (1, 2, 3, 0):
        if rank:
            held[0, rank], held[1, rank] = ups[rank - 1], downs[rank - 1]
        else:
            for copy in copies:
                copy.wait()
        active, slope = feed_parts(nn(normed, held[0, rank]))
        actives[rank] = active
        slopes[rank] = slope
        total += nn(active, held[1, rank])
    h2[...] = total.astype(bf16)
    hidden = h2[...].astype(f32)
    scaled, _ = centre(hidden)
    normed = (scaled * gains[2:3, :]).astype(bf16)
    mixed[...] = nt(normed, mixing_three[...]).astype(bf16)
    shared_width = SHARED * HEAD
    mixed[:, 2 * D : 2 * D + shared_width] = mixed_one[:, 2 * D : 2 * D + shared_width]
    attended[...] = attend(mixed, limits, probabilities)
    h3[...] = (hidden + nt(attended[...], output_three[...])).astype(bf16)


def feed_parts(upward):
    square = upward * upward
    rising = 0.5 + 0.5 * jnp.tanh(upward * (GELU_SCALE + (GELU_SCALE * GELU_CUBE) * square))
    active = upward * rising
    steep = 2.0 * GELU_SCALE + (6.0 * GELU_SCALE * GELU_CUBE) * square
    return active.astype(bf16), rising + active * (1.0 - rising) * steep


def quarter_back(up, down, normed_across, grad_out, active, slope):
    grad_upward = (nt(grad_out, down) * slope).astype(bf16)
    grad_down = nn(active.T, grad_out).astype(bf16)
    return nn(normed_across, grad_upward).astype(bf16), grad_down, nt(grad_upward, up)


def seeded(limits, cotangent):
    row = lax.broadcasted_iota(jnp.int32, cotangent.shape, 0)
    return jnp.where(row < limits[0:1, :1], cotangent[...].astype(f32), 0.0)


def fourth_kernel(limits, h3, gains, cotangent, own0, own1, near, far, other_near, other_far, *rest):
    total, grad_normed, keep, send, held, sems = rest
    copies = bring(own0, own1, held, sems)
    hidden = h3[...].astype(f32)
    scaled, _ = centre(hidden)
    normed = (scaled * gains[3:4, :]).astype(bf16)
    normed_across = normed.T
    grad_out = seeded(limits, cotangent).astype(bf16)
    first = place()[1] == 0
    after, grads = hidden, jnp.zeros(hidden.shape, f32)
    for rank in (1, 2, 0):
        if rank == 1:
            up = jnp.where(first, near[...], other_near[...])
            down = jnp.where(first, other_far[...], far[...])
        elif rank == 2:
            up = jnp.where(first, far[...], other_far[...])
            down = jnp.where(first, other_near[...], near[...])
        else:
            for copy in copies:
                copy.wait()
            up, down = held[0, 0], held[1, 0]
        active, slope = feed_parts(nn(normed, up))
        after += nn(active, down)
        grad_up, grad_down, grad = quarter_back(up, down, normed_across, grad_out, active, slope)
        put(keep, send, rank, grad_up, grad_down)
        grads += grad
    total[...] = after
    grad_normed[...] = grads


def fourth_end_kernel(
    limits, h3, gains, cotangent, total, grads, both, other_both, out, grad_h3, keep, send, grad_gain
):
    scaled, rstd = centre(h3[...].astype(f32))
    gain = gains[3:4, :]
    normed = (scaled * gain).astype(bf16)
    grad_out = seeded(limits, cotangent)
    first = place()[1] == 0
    up = jnp.where(first, both[...], other_both[...])
    down = jnp.where(first, other_both[...], both[...])
    active, slope = feed_parts(nn(normed, up))
    out[...] = total[...] + nn(active, down)
    grad_up, grad_down, grad = quarter_back(up, down, normed.T, grad_out.astype(bf16), active, slope)
    keep[...] = jnp.where(first, grad_up, grad_down)
    send[...] = jnp.where(first, grad_down, grad_up)
    grad_hidden, one_gain = norm_back(scaled, rstd, gain, grads[...] + grad)
    grad_gain[0:1, :] = one_gain
    grad_h3[...] = (grad_out + grad_hidden).astype(bf16)


def attention_back(hidden, grad_out, mixed, attended, probabilities, mixing, output, gain, grad_mixed, shared, value_grad):
    scaled, rstd = centre(hidden)
    normed_across = (scaled * gain).astype(bf16).T
    grad_heads = nn(grad_out, output[...]).astype(bf16)
    grad_output = nn(attended[...].T, grad_out).astype(bf16)
    attend_back(mixed, grad_heads, probabilities, grad_mixed)
    shared(grad_mixed)
    grad_pair = nn(normed_across, grad_mixed[:, : 2 * D]).astype(bf16)
    grad_values = value_grad(scaled, gain, normed_across, grad_mixed)
    grad_hidden, grad_gain = norm_back(scaled, rstd, gain, nn(grad_mixed[...], mixing[...]))
    return grad_hidden, grad_gain, grad_pair, grad_values, grad_output


def third_back_kernel(
    h2, gains, grad_h3, mixed, attended, probabilities, mixing, output,
    grad_h2, grad_weights, grad_shared, grad_gain, grad_mixed,
):
    shared_width = SHARED * HEAD

    def hand_over(grads):
        grad_shared[...] = grads[:, 2 * D : 2 * D + shared_width]
        grads[:, 2 * D : 2 * D + shared_width] = jnp.zeros((grads.shape[0], shared_width), bf16)

    def fresh_grad(scaled, gain, normed_across, grads):
        across = grads[:, 2 * D + 2 * HEAD :].T
        return nn(across[HEAD:], (scaled * gain).astype(bf16)).astype(bf16)

    grad_hidden, one_gain, grad_pair, grad_fresh, grad_output = attention_back(
        h2[...].astype(f32), grad_h3[...], mixed, attended, probabilities, mixing, output,
        gains[2:3, :], grad_mixed, hand_over, fresh_grad,
    )
    grad_weights[0, :D] = grad_pair[:, :D]
    grad_weights[0, D:] = grad_pair[:, D:]
    grad_weights[1, :shared_width] = jnp.zeros((shared_width, D), bf16)
    grad_weights[1, shared_width:D] = grad_fresh
    grad_weights[1, D:] = grad_output
    grad_gain[0:1, :] = one_gain
    grad_h2[...] = (grad_h3[...].astype(f32) + grad_hidden).astype(bf16)


def second_back_kernel(h1, gains, grad_h2, held, actives, slopes, grad_h1, keep, send, grad_gain):
    scaled, rstd = centre(h1[...].astype(f32))
    gain = gains[1:2, :]
    normed_across = (scaled * gain).astype(bf16).T
    grads = jnp.zeros(scaled.shape, f32)
    for rank in range(QUARTERS):
        grad_up, grad_down, grad = quarter_back(
            held[0, rank], held[1, rank], normed_across, grad_h2[...], actives[rank], slopes[rank]
        )
        put(keep, send, rank, grad_up, grad_down)
        grads += grad
    grad_hidden, one_gain = norm_back(scaled, rstd, gain, grads)
    grad_gain[0:1, :] = one_gain
    grad_h1[...] = (grad_h2[...].astype(f32) + grad_hidden).astype(bf16)


def first_back_kernel(
    tokens, gains, grad_h1, mixed, attended, probabilities, mixing, output,
    grad_shared, third_weights, gain_two, gain_three, gain_four,
    input_grad, keep, send, grad_mixed,
):
    shared_width = SHARED * HEAD

    def take_over(grads):
        at = slice(2 * D, 2 * D + shared_width)
        grads[:, at] = (grads[:, at].astype(f32) + grad_shared[...].astype(f32)).astype(bf16)

    def value_grad(scaled, gain, normed_across, grads):
        return nn(normed_across, grads[:, 2 * D :]).astype(bf16)

    grad_hidden, gain_one, grad_pair, grad_values, grad_output = attention_back(
        tokens[...].astype(f32), grad_h1[...], mixed, attended, probabilities, mixing, output,
        gains[0:1, :], grad_mixed, take_over, value_grad,
    )
    input_grad[...] = grad_h1[...].astype(f32) + grad_hidden
    section, part = place()[0], D // 2
    gain_rows = jnp.concatenate(
        [gain_one, gain_two[0:1, :], gain_three[0:1, :], gain_four[0:1, :], jnp.zeros((12, D), f32)], 0
    ).astype(bf16)
    for j in range(QUARTERS):
        at = slice(part * (j % 2), part * (j % 2) + part)
        zero = (grad_pair[:, :D], grad_pair[:, D:])[j // 2][at]
        one = (grad_values, grad_output)[j // 2][at]
        put(keep, send, section ^ j, zero, one, (0, part))
        below = third_weights[1, part * j : part * j + part]
        if j == 0:
            below = jnp.concatenate([gain_rows, below[16:]], 0)
        put(keep, send, section ^ j, third_weights[0, part * j : part * j + part], below, (part, part))


def pieces_of(refs):
    for own, (mine, far, pair) in ((True, refs[:3]), (False, refs[3:])):
        yield own, 0, mine[...]
        yield own, 2, far[...]
        yield own, 1, pair[0]
        yield own, 3, pair[1]


def unpack_feed_kernel(*rest):
    up, down, wide, sems = rest[6:]
    section, core = place()
    steps = []
    for slot, (own, rank, value) in enumerate(pieces_of(rest[:6])):
        wide[slot] = value.astype(f32)
        zero = (core == 0) if own else (core != 0)
        column = pl.ds(pl.multiple_of((section ^ rank) * D, D), D)
        below = pl.ds(pl.multiple_of((section ^ swapped(rank)) * D, D), D)
        steps += [
            (zero, pltpu.make_async_copy(wide.at[slot], up.at[:, column], sems.at[slot])),
            (jnp.logical_not(zero), pltpu.make_async_copy(wide.at[slot], down.at[below, :], sems.at[slot])),
        ]
        for flag, copy in steps[-2:]:
            pl.when(flag)(copy.start)
    for flag, copy in steps:
        pl.when(flag)(copy.wait)


def unpack_attention_kernel(*rest):
    mixing, output, pair, fresh, output_three, g1, g2, g3, g4, wide, sems = rest[6:]
    section, core = place()
    part = D // 2
    steps = []
    for slot, (own, rank, value) in enumerate(pieces_of(rest[:6])):
        wide[slot] = value.astype(f32)
        zero = (core == 0) if own else (core != 0)
        j0, j1 = section ^ rank, section ^ swapped(rank)
        column = pl.ds(pl.multiple_of((j0 >> 1) * D, D), D)
        row0 = pl.ds(pl.multiple_of((j0 & 1) * part, part), part)
        row1 = pl.ds(pl.multiple_of((j1 & 1) * part, part), part)
        one = jnp.logical_not(zero)

        @pl.when(one & (j1 == 0))
        def _():
            for k, ref in enumerate((g1, g2, g3, g4)):
                ref[...] = wide[slot, part + k]

        for low, flag, target in (
            (0, zero, mixing.at[row0, column]),
            (1, zero, pair.at[row0, column]),
            (0, one & (j1 < 2), mixing.at[row1, 2 * D :]),
            (1, one & (j1 == 1), fresh),
            (0, one & (j1 >= 2), output.at[row1, :]),
            (1, one & (j1 >= 2), output_three.at[row1, :]),
        ):
            copy = pltpu.make_async_copy(
                wide.at[slot, part * low : part * low + part], target, sems.at[slot, low]
            )
            steps.append((flag, copy))
            pl.when(flag)(copy.start)
    for flag, copy in steps:
        pl.when(flag)(copy.wait)


SMEM, VMEM, HBM = pltpu.SMEM, pltpu.VMEM, pltpu.HBM


def call(body, name, args, outs, scratch=(), spaces=None, limit=12, hint=20):
    spaces = spaces or {}
    args = [
        pltpu.with_memory_space_constraint(arg, HBM) if spaces.get(i) is HBM else arg
        for i, arg in enumerate(args)
    ]
    places = {"vmem": VMEM, "hbm": HBM}
    return pl.pallas_call(
        body,
        name=name,
        out_shape=[
            places[where](shape, dtype) if where in places else jax.ShapeDtypeStruct(shape, dtype)
            for shape, dtype, where in outs
        ],
        in_specs=[pl.BlockSpec(memory_space=spaces.get(i, VMEM)) for i in range(len(args))],
        out_specs=[pl.BlockSpec(memory_space=places.get(where, VMEM)) for _, _, where in outs],
        scratch_shapes=list(scratch),
        compiler_params=pltpu.CompilerParams(vmem_limit_bytes=limit * 1024 * 1024),
        cost_estimate=pl.CostEstimate(flops=hint * 10**9, bytes_accessed=1, transcendentals=1),
    )(*args)


def partner_pairs(sections, groups, kind):
    found = []
    for section in range(sections):
        for group in range(groups):
            core = group & 1
            to_section, to_group = section, group
            if kind == "near":
                to_section = section ^ (1 if core == 0 else 2)
            elif kind == "far":
                to_section = section ^ (2 if core == 0 else 1)
            else:
                to_group = group ^ kind
            found.append((section * groups + group, to_section * groups + to_group))
    return found


def partner(value, kind):
    sections, groups = lax.axis_size("section"), lax.axis_size("dp")
    return lax.ppermute(value, ("section", "dp"), partner_pairs(sections, groups, kind))


def total(*parts):
    return sum(part.astype(f32) for part in parts).astype(bf16)


def chip_bit():
    return (lax.axis_index("dp") >> 1) & 1


def one_sum_kernel(index, keep, came, out):
    out[...] = total(keep[index], came[index])


def begin_kernel(keep, came, both, near):
    both[...] = total(keep[3], came[3])
    near[...] = total(keep[1], came[1])


def turn_kernel(keep, came, both, far):
    far[...] = total(keep[2], came[2], both[...])


def own_kernel(keep, came, near, far, away, kept, halves):
    rows = kept.shape[0]
    own = total(keep[0], came[0], near[...], far[...])
    halves[0] = own[:rows]
    halves[1] = own[rows:]
    bit = chip_bit()
    kept[...] = halves[bit]
    away[...] = halves[1 - bit]


def copy_kernel(value, out):
    out[...] = value[...]


def pair_kernel(left, right, out):
    out[0] = left[...]
    out[1] = right[...]


def sum_kernel(left, right, out):
    out[...] = total(left[...], right[...])


def join_kernel(kept, back, own):
    rows = kept.shape[0]
    bit = chip_bit()
    own[pl.ds(pl.multiple_of(bit * rows, rows), rows)] = kept[...]
    own[pl.ds(pl.multiple_of((1 - bit) * rows, rows), rows)] = back[...]


class Line:
    def __init__(self):
        self.last = ()

    def tied(self, *values):
        if not self.last:
            return values
        return lax.optimization_barrier(values + self.last)[: len(values)]

    def step(self, made, *values):
        made = made(*self.tied(*values))
        self.last = (jax.tree.leaves(made)[0],)
        return made

    def hop(self, value, kind):
        return partner(self.tied(value)[0], kind)

    def gate(self, value, hint):
        copy = [(value.shape, value.dtype, "vmem")]
        return self.step(lambda v: call(copy_kernel, "gate", (v,), copy, limit=4, hint=hint)[0], value)


class Chunk:
    def __init__(self, line, keep, send):
        self.line, self.keep = line, keep
        self.came = partner(send, 1)
        self.groups = lax.axis_size("dp")

    def made(self, hint, body, name, outs, *args, scratch=()):
        return self.line.step(
            lambda *tied: call(
                body, name, tied, [(shape, bf16, "vmem") for shape in outs], scratch, limit=4, hint=hint
            ),
            *args,
        )

    def begin(self, hint):
        block = self.keep.shape[1:]
        both, near = self.made(hint, begin_kernel, "sum_begin", [block] * 2, self.keep, self.came)
        self.both, self.near = partner(both, "near"), partner(near, "near")

    def begin_near(self, hint):
        body = functools.partial(one_sum_kernel, 1)
        (near,) = self.made(hint, body, "sum_near", [self.keep.shape[1:]], self.keep, self.came)
        self.near = partner(near, "near")

    def begin_both(self, keep, send, hint):
        (both,) = self.made(hint, sum_kernel, "sum_both", [keep.shape], keep, partner(send, 1))
        self.both = partner(both, "near")

    def turn(self, hint):
        (far,) = self.made(
            hint, turn_kernel, "sum_turn", [self.keep.shape[1:]], self.keep, self.came, self.both
        )
        self.far = partner(far, "far")

    def own(self, hint):
        rows, width = self.keep.shape[1:]
        half = (rows // 2, width)
        away, self.kept = self.made(
            hint, own_kernel, "sum_own", [half] * 2, self.keep, self.came, self.near, self.far,
            scratch=[VMEM((2,) + half, bf16)],
        )
        self.back = partner(away, 2)

    def plus(self, came, hint):
        (self.kept,) = self.made(hint, sum_kernel, "sum_chips", [self.kept.shape], self.kept, came)

    def along(self, hint):
        self.plus(self.back, hint)
        step = 4
        while step < self.groups:
            self.back = partner(self.kept, step)
            step *= 2
            if step < self.groups:
                self.plus(self.back, hint)

    def across(self, hint):
        if self.groups > 4:
            self.plus(self.back, hint)
        self.back = partner(self.kept, 2)

    def share(self, hint):
        rows, width = self.kept.shape
        (own,) = self.made(hint, join_kernel, "sum_join", [(2 * rows, width)], self.kept, self.back)
        self.mine, self.far, self.near = own, partner(own, "far"), partner(own, "near")
        self.others = [partner(own, 1)]

    def pass_on(self, hint):
        self.far = self.line.gate(self.far, hint)
        self.both = partner(self.far, "near")
        self.others.append(partner(self.far, 1))

    def end(self, hint):
        shape = (2,) + self.far.shape
        (pair,) = self.made(hint, pair_kernel, "sum_pair", [shape], self.near, self.both)
        self.pieces = [self.mine, self.far, pair] + self.others + [partner(pair, 1)]


def shards(
    tokens,
    cotangent,
    lengths,
    gain_one,
    mixing_one,
    output_one,
    gain_two,
    up_two,
    down_two,
    gain_three,
    pair_three,
    fresh_three,
    output_three,
    gain_four,
    up_four,
    down_four,
):
    rows = tokens.shape[0]
    square = (D, D)
    row, wide_row, held = (rows, D), (rows, 3 * D), (2, QUARTERS, D, D)
    gain_row, packed, chances = (8, D), (QUARTERS, D, D), (HEADS, rows, rows)
    hidden_row = (QUARTERS,) + row
    shared_width = SHARED * HEAD
    line = Line()

    half_one, half_three, mine_one, mine_two, mine_four, limits = call(
        prepare_kernel, "prepare",
        (mixing_one.T, output_one.T, pair_three.T, fresh_three.T, output_three.T,
         gain_one, gain_two, gain_three, gain_four, up_two, down_two, up_four, down_four, lengths.T),
        [(square, bf16, "vmem")] * 5 + [((8, rows), jnp.int32, "vmem")],
        [VMEM((8, D), f32)] + [VMEM(gain_one.shape, bf16)] * 4 + [pltpu.SemaphoreType.DMA((18,))],
        {i: HBM for i in range(13)} | {13: SMEM},
    )
    near_one, far_one = partner(mine_one, "near"), partner(mine_one, "far")
    near_two, far_two = partner(mine_two, "near"), partner(mine_two, "far")
    near_one = line.gate(near_one, 20)
    other_near_one = partner(near_one, 1)
    both_one = partner(near_one, "far")
    near_two = line.gate(near_two, 20)
    other_near_two = partner(near_two, 1)
    both_two = partner(near_two, "far")
    far_one = line.gate(far_one, 20)
    other_far_one = partner(far_one, 1)
    limits = line.gate(limits, 20)
    both_two = line.gate(both_two, 20)
    other_both_two = partner(both_two, 1)
    far_two = line.gate(far_two, 20)
    other_far_two = partner(far_two, 1)
    mine_four = line.gate(mine_four, 20)
    near_four, far_four = partner(mine_four, "near"), partner(mine_four, "far")
    both_one = line.gate(both_one, 20)
    other_both_one = partner(both_one, 1)
    h1, mixed_one, attended_one, chances_one, mixing, output, mixing_three, out_three, gains = line.step(
        lambda *args: call(
            first_kernel, "first_forward", args,
            [(row, bf16, "vmem"), (wide_row, bf16, "vmem"), (row, bf16, "vmem"), (chances, f32, "vmem"),
             ((3 * D, D), bf16, "vmem"), (square, bf16, "vmem"), ((3 * D, D), bf16, "vmem"),
             (square, bf16, "vmem"), (gain_row, f32, "vmem")],
            [VMEM(held, bf16)], hint=20,
        ),
        limits, tokens, half_one, half_three,
        near_one, far_one, both_one, other_near_one, other_far_one, other_both_one,
    )
    h2, held_two, h3, mixed_three, attended_three, chances_three, actives, slopes = line.step(
        lambda *args: call(
            middle_kernel, "second_third_forward", args,
            [(row, bf16, "vmem"), (held, bf16, "vmem"), (row, bf16, "vmem"), (wide_row, bf16, "vmem"),
             (row, bf16, "vmem"), (chances, f32, "vmem"), (hidden_row, bf16, "vmem"),
             (hidden_row, f32, "vmem")],
            [pltpu.SemaphoreType.DMA((2,))], {6: HBM, 7: HBM}, hint=20,
        ),
        limits, h1, gains, mixing_three, out_three, mixed_one, up_two, down_two,
        near_two, far_two, both_two, other_near_two, other_far_two, other_both_two,
    )
    far_four = line.gate(far_four, 20)
    other_far_four = partner(far_four, 1)
    near_four = line.gate(near_four, 0)
    other_near_four = partner(near_four, 1)
    both_four = partner(near_four, "far")
    three_quarters = (QUARTERS - 1, D, D)
    after, grad_normed, keep, send = line.step(
        lambda *args: call(
            fourth_kernel, "fourth_both", args,
            [(row, f32, "vmem"), (row, f32, "vmem"), (three_quarters, bf16, "vmem"),
             (three_quarters, bf16, "vmem")],
            [VMEM((2, 1, D, D), bf16), pltpu.SemaphoreType.DMA((2,))], {4: HBM, 5: HBM}, hint=20,
        ),
        limits, h3, gains, cotangent, up_four, down_four,
        near_four, far_four, other_near_four, other_far_four,
    )
    four = Chunk(line, keep, send)
    both_four = line.gate(both_four, 20)
    other_both_four = partner(both_four, 1)
    out, grad_h3, last_keep, last_send, gain_grad_four = line.step(
        lambda *args: call(
            fourth_end_kernel, "fourth_end", args,
            [(row, f32, "plain"), (row, bf16, "vmem"), (square, bf16, "vmem"), (square, bf16, "vmem"),
             (gain_row, f32, "vmem")], hint=20,
        ),
        limits, h3, gains, cotangent, after, grad_normed, both_four, other_both_four,
    )
    four.begin_near(20)
    four.begin_both(last_keep, last_send, 20)
    grad_h2, third_weights, grad_shared, gain_grad_three = line.step(
        lambda *args: call(
            third_back_kernel, "third_backward", args,
            [(row, bf16, "vmem"), ((2, 2 * D, D), bf16, "vmem"), ((rows, shared_width), bf16, "vmem"),
             (gain_row, f32, "vmem")],
            [VMEM(wide_row, bf16)], hint=3,
        ),
        h2, gains, grad_h3, mixed_three, attended_three, chances_three, mixing_three, out_three,
    )
    grad_h1, keep, send, gain_grad_two = line.step(
        lambda *args: call(
            second_back_kernel, "second_backward", args,
            [(row, bf16, "vmem"), (packed, bf16, "vmem"), (packed, bf16, "vmem"), (gain_row, f32, "vmem")], hint=20,
        ),
        h1, gains, grad_h2, held_two, actives, slopes,
    )
    two = Chunk(line, keep, send)
    four.turn(20)
    input_grad, keep, send = line.step(
        lambda *args: call(
            first_back_kernel, "first_backward", args,
            [(row, f32, "plain"), (packed, bf16, "vmem"), (packed, bf16, "vmem")],
            [VMEM(wide_row, bf16)], hint=20,
        ),
        tokens, gains, grad_h1, mixed_one, attended_one, chances_one, mixing, output,
        grad_shared, third_weights, gain_grad_two, gain_grad_three, gain_grad_four,
    )
    first = Chunk(line, keep, send)
    two.begin(20)
    four.own(3)
    two.turn(20)
    four.along(20)
    first.begin(20)
    two.own(20)
    four.across(20)
    first.turn(20)
    two.along(20)
    four.share(20)
    first.own(20)
    two.across(20)
    four.pass_on(20)
    first.along(20)
    two.share(20)
    four.end(20)
    first.across(20)
    two.pass_on(20)
    first.share(20)
    two.end(3)
    first.pass_on(2)
    feed_outs = [((D, 4 * D), f32, "hbm"), ((4 * D, D), f32, "hbm")]
    feed_scratch = [VMEM((8, D, D), f32), pltpu.SemaphoreType.DMA((8,))]
    grad_up_two, grad_down_two = line.step(
        lambda *args: call(unpack_feed_kernel, "unpack_two", args, feed_outs, feed_scratch, hint=1),
        *two.pieces,
    )
    first.end(20)
    grad_up_four, grad_down_four = line.step(
        lambda *args: call(unpack_feed_kernel, "unpack_four", args, feed_outs, feed_scratch, hint=20),
        *four.pieces,
    )
    mixing_g, output_g, pair_g, fresh_g, output_three_g, g1, g2, g3, g4 = line.step(
        lambda *args: call(
            unpack_attention_kernel, "unpack_attention", args,
            [((D, 3 * D), f32, "hbm"), (square, f32, "hbm"), ((D, 2 * D), f32, "hbm"),
             ((D // 2, D), f32, "hbm"), (square, f32, "hbm")] + [((D,), f32, "plain")] * 4,
            [VMEM((8, D, D), f32), pltpu.SemaphoreType.DMA((8, 2))], hint=20,
        ),
        *first.pieces,
    )
    return (
        out, input_grad, g1, mixing_g, output_g, g2, grad_up_two, grad_down_two,
        g3, pair_g, fresh_g.T, output_three_g, g4, grad_up_four, grad_down_four,
    )


def solution(mesh):
    return jax.shard_map(
        shards,
        mesh=mesh,
        in_specs=(
            P(("section", "dp"), None),
            P(("section", "dp"), None),
            P(None, "dp"),
            P("section"),
            P(None, "section"),
            P(None, "section"),
            P("section"),
            P(None, "section"),
            P("section", None),
            P("section"),
            P(None, "section"),
            P(None, "section"),
            P(None, "section"),
            P("section"),
            P(None, "section"),
            P("section", None),
        ),
        out_specs=(P(("section", "dp"), None), P(("section", "dp"), None)) + (P(),) * 13,
        check_vma=False,
    )
```

```python
import functools

import jax
import jax.numpy as jnp
from jax import lax
from jax.experimental import pallas as pl
from jax.experimental.pallas import tpu as pltpu
from jax.sharding import PartitionSpec as P

D = 384
HEADS = 6
HEAD = 64
SHARED = 3
QUARTERS = 4

EPSILON = 1e-05
MASKED = -1e30
GELU_SCALE = 0.7978845608028654
GELU_CUBE = 0.044715

f32 = jnp.float32
bf16 = jnp.bfloat16


def nn(left, right):
    return jnp.dot(left, right, preferred_element_type=f32)


def nt(left, right):
    return lax.dot_general(left, right, (((1,), (1,)), ((), ())), preferred_element_type=f32)


def centre(hidden):
    centred = hidden - jnp.mean(hidden, -1, keepdims=True)
    spread = jnp.mean(centred * centred, -1, keepdims=True)
    rstd = lax.rsqrt(spread + EPSILON)
    return centred * rstd, rstd


def norm_back(scaled, rstd, gain, grad):
    grad_gain = jnp.sum(grad * scaled, 0, keepdims=True)
    c = grad * gain
    along = jnp.mean(c * scaled, -1, keepdims=True)
    return rstd * (c - jnp.mean(c, -1, keepdims=True) - scaled * along), grad_gain


def swapped(rank):
    return ((rank & 1) << 1) | (rank >> 1)


def place():
    return lax.axis_index("section"), lax.axis_index("dp") & 1


def select_pieces(pieces):
    near, far, both, other_near, other_far, other_both = pieces
    first = place()[1] == 0

    def pick(left, right):
        return jnp.where(first, left[...], right[...])

    return (
        (pick(near, other_near), pick(far, other_far), pick(both, other_both)),
        (pick(other_far, far), pick(other_near, near), pick(other_both, both)),
    )


def put(keep, send, rank, half_zero, half_one, rows=None):
    first = place()[1] == 0
    zero, one = rank, swapped(rank)
    kept, sent = jnp.where(first, zero, one), jnp.where(first, one, zero)
    if rows is None:
        keep[kept] = jnp.where(first, half_zero, half_one)
        send[sent] = jnp.where(first, half_one, half_zero)
    else:
        keep[kept, pl.ds(*rows)] = jnp.where(first, half_zero, half_one)
        send[sent, pl.ds(*rows)] = jnp.where(first, half_one, half_zero)


def query_blocks(rows):
    step = min(rows, 128)
    return [(first, first + step) for first in range(0, rows, step)]


def usable(first, last, limits):
    key_index = lax.broadcasted_iota(jnp.int32, (last, last - first), 0)
    query_index = lax.broadcasted_iota(jnp.int32, (last, last - first), 1) + first
    return (key_index <= query_index) & (key_index < limits[0:1, first:last])


def one_head(block, side):
    lane = lax.broadcasted_iota(jnp.int32, block.shape, 1)
    return jnp.where((lane < HEAD) if side == 0 else (lane >= HEAD), block, 0)


def pair_at(head):
    return 2 * HEAD * (head // 2)


def attend(mixed, limits, probabilities):
    blocks = query_blocks(mixed.shape[0])
    values_across = mixed[:, 2 * D :].T
    allowed = [usable(first, last, limits) for first, last in blocks]
    for head in range(HEADS):
        at = pair_at(head)
        for (first, last), mask in zip(blocks, allowed):
            queries = one_head(mixed[first:last, at : at + 2 * HEAD], head % 2)
            scores = nt(mixed[:last, D + at : D + at + 2 * HEAD], queries) * HEAD ** (-0.5)
            probabilities[head, :last, first:last] = jnp.where(mask, scores, MASKED)
    outs = []
    for head in range(HEADS):
        parts = []
        for first, last in blocks:
            scores = probabilities[head, :last, first:last]
            raised = jnp.exp(scores - jnp.max(scores, 0, keepdims=True))
            probability = raised * (1.0 / jnp.sum(raised, 0, keepdims=True))
            probabilities[head, :last, first:last] = probability
            values = values_across[HEAD * head : HEAD * head + HEAD, :last]
            parts.append(nn(values, probability.astype(bf16)))
        outs.append(jnp.concatenate(parts, 1))
    return jnp.concatenate(outs, 0).T.astype(bf16)


def attend_back(mixed, grad_heads, probabilities, grad_mixed, grad_probs, rounded):
    rows = mixed.shape[0]
    blocks = query_blocks(rows)
    keys_across = mixed[:, D : 2 * D].T
    for head in range(HEADS):
        at = pair_at(head)
        for first, last in blocks:
            grads = one_head(grad_heads[first:last, at : at + 2 * HEAD], head % 2)
            values = mixed[:last, 2 * D + at : 2 * D + at + 2 * HEAD]
            grad_probs[head, :last, first:last] = nt(values, grads)
    for head in range(HEADS):
        for first, last in blocks:
            probability = probabilities[head, :last, first:last]
            grad_prob = grad_probs[head, :last, first:last]
            middle = jnp.sum(probability * grad_prob, 0, keepdims=True)
            rounded[0, head, :last, first:last] = (probability * (grad_prob - middle)).astype(bf16)
            rounded[1, head, :last, first:last] = probability.astype(bf16)
            if last < rows:
                unused = jnp.zeros((rows - last, last - first), bf16)
                rounded[0, head, last:, first:last] = unused
                rounded[1, head, last:, first:last] = unused
    query_parts = []
    for pair in range(HEADS // 2):
        at = 2 * HEAD * pair
        queries = mixed[:, at : at + 2 * HEAD]
        grads = grad_heads[:, at : at + 2 * HEAD]
        key_grad = value_grad = 0.0
        for side in range(2):
            head = 2 * pair + side
            key_grad += nn(rounded[0, head], one_head(queries, side))
            value_grad += nn(rounded[1, head], one_head(grads, side))
            query_parts.append(nn(keys_across[HEAD * head : HEAD * head + HEAD], rounded[0, head]))
        grad_mixed[:, D + at : D + at + 2 * HEAD] = (key_grad * HEAD ** (-0.5)).astype(bf16)
        grad_mixed[:, 2 * D + at : 2 * D + at + 2 * HEAD] = value_grad.astype(bf16)
    grad_mixed[:, :D] = (jnp.concatenate(query_parts, 0).T * HEAD ** (-0.5)).astype(bf16)


def prepare_kernel(
    mixing, output, pair, fresh, output_three, gain_one, gain_two, gain_three, gain_four,
    up_two, down_two, up_four, down_four, lengths,
    one, three, mine_one, mine_two, mine_four, limits, edge, narrow_one, narrow_two, narrow_three, narrow_four, counts, sems,
):
    core = place()[1]
    count = mixing.shape[0]
    wide, small = output.shape[0], fresh.shape[0]
    halves = [[(mixing, 0), (output, count)],
              [(pair, 0), (fresh, 2 * wide), (output_three, 2 * wide + small)]]
    last = 3 * wide + small
    copies = []
    for half, target in ((0, one), (1, three)):
        for source, row in halves[half]:
            rows = source.shape[0]
            copies.append((None, source, target.at[pl.ds(row, rows)]))
            copies.append((half, source, mine_one.at[pl.ds(row, rows)]))
    copies += [(0, up_two, mine_two), (1, down_two, mine_two)]
    copies += [(0, up_four, mine_four), (1, down_four, mine_four)]
    made = [
        (half, pltpu.make_async_copy(source, target, sems.at[i]))
        for i, (half, source, target) in enumerate(copies)
    ]
    for half, copy in made:
        if half is None:
            copy.start()
        else:
            pl.when(core == half)(copy.start)
    gains = [
        pltpu.make_async_copy(gain, narrow, sems.at[len(copies) + k])
        for k, (gain, narrow) in enumerate(
            ((gain_one, narrow_one), (gain_two, narrow_two), (gain_three, narrow_three), (gain_four, narrow_four))
        )
    ]
    for copy in gains:
        copy.start()
    counted = pltpu.make_async_copy(lengths, counts, sems.at[len(copies) + len(gains)])
    counted.start()
    edge[...] = jnp.zeros_like(edge)
    for k, narrow in enumerate((narrow_one, narrow_two, narrow_three, narrow_four)):
        gains[k].wait()
        edge[k : k + 1, : narrow.shape[0]] = narrow[...].astype(f32).reshape(1, narrow.shape[0])
    counted.wait()
    limits[...] = jnp.full(limits.shape, counts[0, place()[0]], jnp.int32)
    rows = D - last
    block = jnp.concatenate([edge[...], jnp.zeros((rows - 8, D), f32)], 0).astype(bf16)
    three[last:] = block

    @pl.when(core != 0)
    def _():
        mine_one[last:] = block

    for half, copy in made:
        if half is None:
            copy.wait()
        else:
            pl.when(core == half)(copy.wait)


def first_kernel(limits, tokens, own0, own1, *rest):
    h1, mixed, attended, probabilities, mixing, output, mixing_three, output_three, gains, held = rest[6:]
    section = place()[0]
    for half, (own, came) in enumerate(zip((own0, own1), select_pieces(rest[:6]))):
        held[half, section] = own[...]
        for rank in (1, 2, 3):
            held[half, section ^ rank] = came[rank - 1]
    shared_width = SHARED * HEAD
    mixing_three[2 * D : 2 * D + shared_width, :] = jnp.zeros((shared_width, D), bf16)
    for j in range(QUARTERS):
        mixing[288 * j : 288 * j + 288, :] = held[0, j, :288]
        output[96 * j : 96 * j + 96, :] = held[0, j, 288:]
        mixing_three[192 * j : 192 * j + 192, :] = held[1, j, :192]
        mixing_three[960 + 48 * j : 960 + 48 * j + 48, :] = held[1, j, 192:240]
        output_three[96 * j : 96 * j + 96, :] = held[1, j, 240:336]
        gains[0:8, 96 * j : 96 * j + 96] = held[1, j, 336:352, :96].astype(f32)[:8]
    hidden = tokens[...].astype(f32)
    scaled, _ = centre(hidden)
    normed = (scaled * gains[0:1, :]).astype(bf16)
    mixed[...] = nt(normed, mixing[...]).astype(bf16)
    attended[...] = attend(mixed, limits, probabilities)
    h1[...] = (hidden + nt(attended[...], output[...])).astype(bf16)


def bring(own0, own1, held, sems):
    copies = [
        pltpu.make_async_copy(own0, held.at[0, 0], sems.at[0]),
        pltpu.make_async_copy(own1, held.at[1, 0], sems.at[1]),
    ]
    for copy in copies:
        copy.start()
    return copies


def middle_kernel(limits, h1, gains, mixing_three, output_three, mixed_one, own0, own1, *rest):
    h2, held, h3, mixed, attended, probabilities, actives, slopes, sems = rest[6:]
    copies = bring(own0, own1, held, sems)
    hidden = h1[...].astype(f32)
    scaled, _ = centre(hidden)
    normed = (scaled * gains[1:2, :]).astype(bf16)
    ups, downs = select_pieces(rest[:6])
    for rank in (1, 2, 3):
        held[0, rank], held[1, rank] = ups[rank - 1], downs[rank - 1]
    for copy in copies:
        copy.wait()
    for rank in range(QUARTERS):
        slopes[rank] = nn(normed, held[0, rank])
    for rank in range(QUARTERS):
        actives[rank], slopes[rank] = feed_parts(slopes[rank])
    total = hidden
    for rank in range(QUARTERS):
        total += nn(actives[rank], held[1, rank])
    h2[...] = total.astype(bf16)
    hidden = h2[...].astype(f32)
    scaled, _ = centre(hidden)
    normed = (scaled * gains[2:3, :]).astype(bf16)
    mixed[...] = nt(normed, mixing_three[...]).astype(bf16)
    shared_width = SHARED * HEAD
    mixed[:, 2 * D : 2 * D + shared_width] = mixed_one[:, 2 * D : 2 * D + shared_width]
    attended[...] = attend(mixed, limits, probabilities)
    h3[...] = (hidden + nt(attended[...], output_three[...])).astype(bf16)


def feed_parts(upward):
    square = upward * upward
    rising = 0.5 + 0.5 * jnp.tanh(upward * (GELU_SCALE + (GELU_SCALE * GELU_CUBE) * square))
    active = upward * rising
    steep = 2.0 * GELU_SCALE + (6.0 * GELU_SCALE * GELU_CUBE) * square
    return active.astype(bf16), rising + active * (1.0 - rising) * steep


def quarter_back(up, down, normed_across, grad_out, active, slope):
    grad_upward = (nt(grad_out, down) * slope).astype(bf16)
    grad_down = nn(active.T, grad_out).astype(bf16)
    return nn(normed_across, grad_upward).astype(bf16), grad_down, nt(grad_upward, up)


def fourth_kernel(limits, h3, gains, cotangent, own0, own1, near, far, other_near, other_far, *rest):
    total, grad_normed, keep, send, seed, held, brought, sems = rest
    seeding = pltpu.make_async_copy(cotangent, brought, sems.at[2])
    seeding.start()
    copies = bring(own0, own1, held, sems)
    hidden = h3[...].astype(f32)
    scaled, _ = centre(hidden)
    normed = (scaled * gains[3:4, :]).astype(bf16)
    normed_across = normed.T
    first = place()[1] == 0
    after, grads = hidden, jnp.zeros(hidden.shape, f32)
    for rank in (1, 2, 0):
        if rank == 1:
            up = jnp.where(first, near[...], other_near[...])
            down = jnp.where(first, other_far[...], far[...])
        elif rank == 2:
            up = jnp.where(first, far[...], other_far[...])
            down = jnp.where(first, other_near[...], near[...])
        else:
            for copy in copies:
                copy.wait()
            up, down = held[0, 0], held[1, 0]
        active, slope = feed_parts(nn(normed, up))
        after += nn(active, down)
        if rank == 1:
            seeding.wait()
            row = lax.broadcasted_iota(jnp.int32, hidden.shape, 0)
            grad_out = jnp.where(row < limits[0:1, :1], brought[...], 0)
            seed[...] = grad_out
        grad_up, grad_down, grad = quarter_back(up, down, normed_across, grad_out, active, slope)
        put(keep, send, rank, grad_up, grad_down)
        grads += grad
    total[...] = after
    grad_normed[...] = grads


def fourth_end_kernel(
    h3, gains, seed, total, grads, both, other_both, out, grad_h3, keep, send, grad_gain
):
    scaled, rstd = centre(h3[...].astype(f32))
    gain = gains[3:4, :]
    normed = (scaled * gain).astype(bf16)
    first = place()[1] == 0
    up = jnp.where(first, both[...], other_both[...])
    down = jnp.where(first, other_both[...], both[...])
    active, slope = feed_parts(nn(normed, up))
    out[...] = total[...] + nn(active, down)
    grad_up, grad_down, grad = quarter_back(up, down, normed.T, seed[...], active, slope)
    keep[...] = jnp.where(first, grad_up, grad_down)
    send[...] = jnp.where(first, grad_down, grad_up)
    grad_hidden, one_gain = norm_back(scaled, rstd, gain, grads[...] + grad)
    grad_gain[0:1, :] = one_gain
    grad_h3[...] = (seed[...].astype(f32) + grad_hidden).astype(bf16)


def attention_back(hidden, grad_out, mixed, attended, probabilities, mixing, output, gain, scratch, shared, value_grad):
    scaled, rstd = centre(hidden)
    normed_across = (scaled * gain).astype(bf16).T
    grad_heads = nn(grad_out, output[...]).astype(bf16)
    grad_output = nn(attended[...].T, grad_out).astype(bf16)
    grad_mixed = scratch[0]
    attend_back(mixed, grad_heads, probabilities, *scratch)
    shared(grad_mixed)
    grad_pair = nn(normed_across, grad_mixed[:, : 2 * D]).astype(bf16)
    grad_values = value_grad(scaled, gain, normed_across, grad_mixed)
    grad_hidden, grad_gain = norm_back(scaled, rstd, gain, nn(grad_mixed[...], mixing[...]))
    return grad_hidden, grad_gain, grad_pair, grad_values, grad_output


def third_back_kernel(
    h2, gains, grad_h3, mixed, attended, probabilities, mixing, output,
    grad_h2, grad_weights, grad_shared, grad_gain, *scratch,
):
    shared_width = SHARED * HEAD

    def hand_over(grads):
        grad_shared[...] = grads[:, 2 * D : 2 * D + shared_width]
        grads[:, 2 * D : 2 * D + shared_width] = jnp.zeros((grads.shape[0], shared_width), bf16)

    def fresh_grad(scaled, gain, normed_across, grads):
        across = grads[:, 2 * D + 2 * HEAD :].T
        return nn(across[HEAD:], (scaled * gain).astype(bf16)).astype(bf16)

    grad_hidden, one_gain, grad_pair, grad_fresh, grad_output = attention_back(
        h2[...].astype(f32), grad_h3[...], mixed, attended, probabilities, mixing, output,
        gains[2:3, :], scratch, hand_over, fresh_grad,
    )
    grad_weights[0, :D] = grad_pair[:, :D]
    grad_weights[0, D:] = grad_pair[:, D:]
    grad_weights[1, :shared_width] = jnp.zeros((shared_width, D), bf16)
    grad_weights[1, shared_width:D] = grad_fresh
    grad_weights[1, D:] = grad_output
    grad_gain[0:1, :] = one_gain
    grad_h2[...] = (grad_h3[...].astype(f32) + grad_hidden).astype(bf16)


def second_back_kernel(h1, gains, grad_h2, held, actives, slopes, grad_h1, keep, send, grad_gain):
    scaled, rstd = centre(h1[...].astype(f32))
    gain = gains[1:2, :]
    normed_across = (scaled * gain).astype(bf16).T
    grads = jnp.zeros(scaled.shape, f32)
    for rank in range(QUARTERS):
        grad_up, grad_down, grad = quarter_back(
            held[0, rank], held[1, rank], normed_across, grad_h2[...], actives[rank], slopes[rank]
        )
        put(keep, send, rank, grad_up, grad_down)
        grads += grad
    grad_hidden, one_gain = norm_back(scaled, rstd, gain, grads)
    grad_gain[0:1, :] = one_gain
    grad_h1[...] = (grad_h2[...].astype(f32) + grad_hidden).astype(bf16)


def first_back_kernel(
    tokens, gains, grad_h1, mixed, attended, probabilities, mixing, output,
    grad_shared, third_weights, gain_two, gain_three, gain_four,
    input_grad, keep, send, *scratch,
):
    shared_width = SHARED * HEAD

    def take_over(grads):
        at = slice(2 * D, 2 * D + shared_width)
        grads[:, at] = (grads[:, at].astype(f32) + grad_shared[...].astype(f32)).astype(bf16)

    def value_grad(scaled, gain, normed_across, grads):
        return nn(normed_across, grads[:, 2 * D :]).astype(bf16)

    grad_hidden, gain_one, grad_pair, grad_values, grad_output = attention_back(
        tokens[...].astype(f32), grad_h1[...], mixed, attended, probabilities, mixing, output,
        gains[0:1, :], scratch, take_over, value_grad,
    )
    input_grad[...] = grad_h1[...].astype(f32) + grad_hidden
    section, part = place()[0], D // 2
    gain_rows = jnp.concatenate(
        [gain_one, gain_two[0:1, :], gain_three[0:1, :], gain_four[0:1, :], jnp.zeros((12, D), f32)], 0
    ).astype(bf16)
    for j in range(QUARTERS):
        at = slice(part * (j % 2), part * (j % 2) + part)
        zero = (grad_pair[:, :D], grad_pair[:, D:])[j // 2][at]
        one = (grad_values, grad_output)[j // 2][at]
        put(keep, send, section ^ j, zero, one, (0, part))
        below = third_weights[1, part * j : part * j + part]
        if j == 0:
            below = jnp.concatenate([gain_rows, below[16:]], 0)
        put(keep, send, section ^ j, third_weights[0, part * j : part * j + part], below, (part, part))


def pieces_of(refs):
    if len(refs) == 4:
        for own, (mine, pair) in ((True, refs[:2]), (False, refs[2:])):
            yield own, 0, mine[0]
            yield own, 2, mine[1]
            yield own, 1, pair[0]
            yield own, 3, pair[1]
        return
    for own, (mine, far, pair) in ((True, refs[:3]), (False, refs[3:])):
        yield own, 0, mine[...]
        yield own, 2, far[...]
        yield own, 1, pair[0]
        yield own, 3, pair[1]


def unpack_feed_kernel(*rest):
    up, down, wide, sems = rest[-4:]
    section, core = place()
    steps = []
    for slot, (own, rank, value) in enumerate(pieces_of(rest[:-4])):
        wide[slot] = value.astype(f32)
        zero = (core == 0) if own else (core != 0)
        column = pl.ds(pl.multiple_of((section ^ rank) * D, D), D)
        below = pl.ds(pl.multiple_of((section ^ swapped(rank)) * D, D), D)
        steps += [
            (zero, pltpu.make_async_copy(wide.at[slot], up.at[:, column], sems.at[slot])),
            (jnp.logical_not(zero), pltpu.make_async_copy(wide.at[slot], down.at[below, :], sems.at[slot])),
        ]
        for flag, copy in steps[-2:]:
            pl.when(flag)(copy.start)
    for flag, copy in steps:
        pl.when(flag)(copy.wait)


def unpack_attention(pieces, targets, gains, wide, sems):
    mixing, output, pair, fresh, output_three = targets
    section, core = place()
    part = D // 2
    steps = []
    for slot, (own, rank, value) in enumerate(pieces):
        wide[slot] = value[...].astype(f32)
        zero = (core == 0) if own else (core != 0)
        j0, j1 = section ^ rank, section ^ swapped(rank)
        column = pl.ds(pl.multiple_of((j0 >> 1) * D, D), D)
        row0 = pl.ds(pl.multiple_of((j0 & 1) * part, part), part)
        row1 = pl.ds(pl.multiple_of((j1 & 1) * part, part), part)
        one = jnp.logical_not(zero)

        @pl.when(one & (j1 == 0))
        def _():
            for k, ref in enumerate(gains):
                ref[...] = wide[slot, part + k]

        for low, flag, target in (
            (0, zero, mixing.at[row0, column]),
            (1, zero, pair.at[row0, column]),
            (0, one & (j1 < 2), mixing.at[row1, 2 * D :]),
            (1, one & (j1 == 1), fresh),
            (0, one & (j1 >= 2), output.at[row1, :]),
            (1, one & (j1 >= 2), output_three.at[row1, :]),
        ):
            copy = pltpu.make_async_copy(
                wide.at[slot, part * low : part * low + part], target, sems.at[slot, low]
            )
            steps.append((flag, copy))
            pl.when(flag)(copy.start)
    for flag, copy in steps:
        pl.when(flag)(copy.wait)


def unpack_some_kernel(*rest):
    pieces, outs, (wide, sems) = rest[:6], rest[6:-2], rest[-2:]
    ranked = [(own, rank, pieces[3 * k + i]) for k, own in enumerate((True, False)) for i, rank in enumerate((0, 2, 1))]
    for ref in outs[5:]:
        ref[...] = jnp.zeros(ref.shape, f32)
    unpack_attention(ranked, outs[:5], outs[5:], wide, sems)


def unpack_rest_kernel(*rest):
    pieces, before, outs, (wide, sems) = rest[:2], rest[7:11], rest[11:-2], rest[-2:]
    for ref, old in zip(outs[5:], before):
        ref[...] = old[...]
    unpack_attention([(True, 3, pieces[0]), (False, 3, pieces[1])], outs[:5], outs[5:], wide, sems)


SMEM, VMEM, HBM = pltpu.SMEM, pltpu.VMEM, pltpu.HBM


def call(body, name, args, outs, scratch=(), spaces=None, limit=12, hint=20, aliases=None):
    spaces = spaces or {}
    args = [
        pltpu.with_memory_space_constraint(arg, HBM) if spaces.get(i) is HBM else arg
        for i, arg in enumerate(args)
    ]
    places = {"vmem": VMEM, "hbm": HBM}
    return pl.pallas_call(
        body,
        name=name,
        out_shape=[
            places[where](shape, dtype) if where in places else jax.ShapeDtypeStruct(shape, dtype)
            for shape, dtype, where in outs
        ],
        in_specs=[pl.BlockSpec(memory_space=spaces.get(i, VMEM)) for i in range(len(args))],
        out_specs=[pl.BlockSpec(memory_space=places.get(where, VMEM)) for _, _, where in outs],
        scratch_shapes=list(scratch),
        input_output_aliases=aliases or {},
        compiler_params=pltpu.CompilerParams(vmem_limit_bytes=limit * 1024 * 1024),
        cost_estimate=pl.CostEstimate(flops=hint * 10**9, bytes_accessed=1, transcendentals=1),
    )(*args)


def partner_pairs(sections, groups, kind):
    found = []
    for section in range(sections):
        for group in range(groups):
            core = group & 1
            to_section, to_group = section, group
            if kind == "near":
                to_section = section ^ (1 if core == 0 else 2)
            elif kind == "far":
                to_section = section ^ (2 if core == 0 else 1)
            else:
                to_group = group ^ kind
            found.append((section * groups + group, to_section * groups + to_group))
    return found


def partner(value, kind):
    sections, groups = lax.axis_size("section"), lax.axis_size("dp")
    return lax.ppermute(value, ("section", "dp"), partner_pairs(sections, groups, kind))


def total(*parts):
    return sum(part.astype(f32) for part in parts).astype(bf16)


def chip_bit():
    return (lax.axis_index("dp") >> 1) & 1


def one_sum_kernel(index, keep, came, out):
    out[...] = total(keep[index], came[index])


def begin_kernel(keep, came, both, near):
    both[...] = total(keep[3], came[3])
    near[...] = total(keep[1], came[1])


def begin_pair_kernel(keep, came, pair):
    pair[0] = total(keep[3], came[3])
    pair[1] = total(keep[1], came[1])


def turn_pair_kernel(keep, came, pair, far):
    far[...] = total(keep[2], came[2], pair[0])


def own_pair_kernel(keep, came, pair, far, away, kept, halves):
    own_kernel(keep, came, pair.at[1], far, away, kept, halves)


def turn_kernel(keep, came, both, far):
    far[...] = total(keep[2], came[2], both[...])


def own_kernel(keep, came, near, far, away, kept, halves):
    rows = kept.shape[0]
    own = total(keep[0], came[0], near[...], far[...])
    halves[0] = own[:rows]
    halves[1] = own[rows:]
    bit = chip_bit()
    kept[...] = halves[bit]
    away[...] = halves[1 - bit]


def copy_kernel(value, out):
    out[...] = value[...]


def pair_kernel(left, right, out):
    out[0] = left[...]
    out[1] = right[...]


def copy_both_kernel(left, right, left_out, right_out):
    left_out[...] = left[...]
    right_out[...] = right[...]


def sum_kernel(left, right, out):
    out[...] = total(left[...], right[...])


def join_kernel(kept, back, own):
    rows = kept.shape[0]
    bit = chip_bit()
    own[pl.ds(pl.multiple_of(bit * rows, rows), rows)] = kept[...]
    own[pl.ds(pl.multiple_of((1 - bit) * rows, rows), rows)] = back[...]


class Line:
    def __init__(self):
        self.last = ()

    def tied(self, *values):
        if not self.last:
            return values
        return lax.optimization_barrier(values + self.last)[: len(values)]

    def step(self, made, *values):
        made = made(*self.tied(*values))
        self.last = (jax.tree.leaves(made)[0],)
        return made

    def hop(self, value, kind):
        return partner(self.tied(value)[0], kind)

    def gate(self, value, hint):
        copy = [(value.shape, value.dtype, "vmem")]
        return self.step(lambda v: call(copy_kernel, "gate", (v,), copy, limit=4, hint=hint)[0], value)


class Chunk:
    def __init__(self, line, keep, send):
        self.line, self.keep = line, keep
        self.came = partner(send, 1)
        self.groups = lax.axis_size("dp")

    def made(self, hint, body, name, outs, *args, scratch=()):
        return self.line.step(
            lambda *tied: call(
                body, name, tied, [(shape, bf16, "vmem") for shape in outs], scratch, limit=4, hint=hint
            ),
            *args,
        )

    def begin(self, hint):
        block = self.keep.shape[1:]
        both, near = self.made(hint, begin_kernel, "sum_begin", [block] * 2, self.keep, self.came)
        self.both, self.near = partner(both, "near"), partner(near, "near")

    def begin_merged(self, hint):
        shape = (2,) + self.keep.shape[1:]
        (pair,) = self.made(hint, begin_pair_kernel, "sum_begin", [shape], self.keep, self.came)
        self.both = self.near = partner(pair, "near")

    def begin_near(self, hint):
        body = functools.partial(one_sum_kernel, 1)
        (near,) = self.made(hint, body, "sum_near", [self.keep.shape[1:]], self.keep, self.came)
        self.near = partner(near, "near")

    def begin_both(self, keep, send, hint):
        (both,) = self.made(hint, sum_kernel, "sum_both", [keep.shape], keep, partner(send, 1))
        self.both = partner(both, "near")

    def turn(self, hint):
        body = turn_kernel if self.both is not self.near else turn_pair_kernel
        (far,) = self.made(hint, body, "sum_turn", [self.keep.shape[1:]], self.keep, self.came, self.both)
        self.far = partner(far, "far")

    def own(self, hint):
        rows, width = self.keep.shape[1:]
        half = (rows // 2, width)
        body = own_kernel if self.both is not self.near else own_pair_kernel
        away, self.kept = self.made(
            hint, body, "sum_own", [half] * 2, self.keep, self.came, self.near, self.far,
            scratch=[VMEM((2,) + half, bf16)],
        )
        self.back = partner(away, 2)

    def plus(self, came, hint):
        (self.kept,) = self.made(hint, sum_kernel, "sum_chips", [self.kept.shape], self.kept, came)

    def along(self, hint):
        self.plus(self.back, hint)
        step = 4
        while step < self.groups:
            self.back = partner(self.kept, step)
            step *= 2
            if step < self.groups:
                self.plus(self.back, hint)

    def across(self, hint):
        if self.groups > 4:
            self.plus(self.back, hint)
        self.back = partner(self.kept, 2)

    def share(self, hint):
        rows, width = self.kept.shape
        (own,) = self.made(hint, join_kernel, "sum_join", [(2 * rows, width)], self.kept, self.back)
        self.mine, self.far, self.near = own, partner(own, "far"), partner(own, "near")
        self.others = [partner(own, 1)]

    def pass_on(self, hint):
        self.far = self.line.gate(self.far, hint)
        self.both = partner(self.far, "near")
        self.others.append(partner(self.far, 1))

    def end(self, hint):
        shape = (2,) + self.far.shape
        (pair,) = self.made(hint, pair_kernel, "sum_pair", [shape], self.near, self.both)
        self.pieces = [self.mine, self.far, pair] + self.others + [partner(pair, 1)]

    def share_far(self, hint):
        rows, width = self.kept.shape
        (self.mine,) = self.made(hint, join_kernel, "sum_join", [(2 * rows, width)], self.kept, self.back)
        self.far = partner(self.mine, "far")

    def pass_pair(self, hint):
        shape = (2,) + self.mine.shape
        (self.mine,) = self.made(hint, pair_kernel, "sum_pair", [shape], self.mine, self.far)
        self.near = partner(self.mine, "near")
        self.others = [partner(self.mine, 1)]

    def end_pair(self, hint):
        pair = self.line.gate(self.near, hint)
        self.pieces = [self.mine, pair] + self.others + [partner(pair, 1)]

    def pass_near(self, hint):
        self.near = self.line.gate(self.near, hint)
        self.others.append(partner(self.near, 1))

    def end_alone(self, hint):
        both = self.line.gate(self.both, hint)
        self.pieces = [both, partner(both, 1)]


def shards(
    tokens,
    cotangent,
    lengths,
    gain_one,
    mixing_one,
    output_one,
    gain_two,
    up_two,
    down_two,
    gain_three,
    pair_three,
    fresh_three,
    output_three,
    gain_four,
    up_four,
    down_four,
):
    rows = tokens.shape[0]
    square = (D, D)
    row, wide_row, held = (rows, D), (rows, 3 * D), (2, QUARTERS, D, D)
    gain_row, packed, chances = (8, D), (QUARTERS, D, D), (HEADS, rows, rows)
    hidden_row = (QUARTERS,) + row
    back_scratch = [VMEM(wide_row, bf16), VMEM(chances, f32), VMEM((2,) + chances, bf16)]
    shared_width = SHARED * HEAD
    line = Line()

    half_one, half_three, mine_one, mine_two, mine_four, limits = call(
        prepare_kernel, "prepare",
        (mixing_one.T, output_one.T, pair_three.T, fresh_three.T, output_three.T,
         gain_one, gain_two, gain_three, gain_four, up_two, down_two, up_four, down_four, lengths.T),
        [(square, bf16, "vmem")] * 5 + [((8, rows), jnp.int32, "vmem")],
        [VMEM((8, D), f32)] + [VMEM(gain_one.shape, bf16)] * 4
        + [SMEM(lengths.T.shape, jnp.int32), pltpu.SemaphoreType.DMA((19,))],
        {i: HBM for i in range(14)},
    )
    near_one, far_one = partner(mine_one, "near"), partner(mine_one, "far")
    near_two, far_two = partner(mine_two, "near"), partner(mine_two, "far")
    limits = line.gate(limits, 0)
    near_one = line.gate(near_one, 3)
    other_near_one = partner(near_one, 1)
    both_one = partner(near_one, "far")
    far_one = line.gate(far_one, 3)
    other_far_one = partner(far_one, 1)
    near_two = line.gate(near_two, 3)
    other_near_two = partner(near_two, 1)
    both_two = partner(near_two, "far")
    mine_four = line.gate(mine_four, 3)
    near_four, far_four = partner(mine_four, "near"), partner(mine_four, "far")
    both_one = line.gate(both_one, 8)
    other_both_one = partner(both_one, 1)
    far_two = line.gate(far_two, 3)
    other_far_two = partner(far_two, 1)
    both_two = line.gate(both_two, 3)
    other_both_two = partner(both_two, 1)
    h1, mixed_one, attended_one, chances_one, mixing, output, mixing_three, out_three, gains = line.step(
        lambda *args: call(
            first_kernel, "first_forward", args,
            [(row, bf16, "vmem"), (wide_row, bf16, "vmem"), (row, bf16, "vmem"), (chances, f32, "vmem"),
             ((3 * D, D), bf16, "vmem"), (square, bf16, "vmem"), ((3 * D, D), bf16, "vmem"),
             (square, bf16, "vmem"), (gain_row, f32, "vmem")],
            [VMEM(held, bf16)], hint=6,
        ),
        limits, tokens, half_one, half_three,
        near_one, far_one, both_one, other_near_one, other_far_one, other_both_one,
    )
    near_four = line.gate(near_four, 3)
    other_near_four = partner(near_four, 1)
    both_four = partner(near_four, "far")
    far_four = line.gate(far_four, 4)
    other_far_four = partner(far_four, 1)
    h2, held_two, h3, mixed_three, attended_three, chances_three, actives, slopes = line.step(
        lambda *args: call(
            middle_kernel, "second_third_forward", args,
            [(row, bf16, "vmem"), (held, bf16, "vmem"), (row, bf16, "vmem"), (wide_row, bf16, "vmem"),
             (row, bf16, "vmem"), (chances, f32, "vmem"), (hidden_row, bf16, "vmem"),
             (hidden_row, f32, "vmem")],
            [pltpu.SemaphoreType.DMA((2,))], {6: HBM, 7: HBM}, hint=3,
        ),
        limits, h1, gains, mixing_three, out_three, mixed_one, up_two, down_two,
        near_two, far_two, both_two, other_near_two, other_far_two, other_both_two,
    )
    both_four = line.gate(both_four, 2)
    other_both_four = partner(both_four, 1)
    three_quarters = (QUARTERS - 1, D, D)
    after, grad_normed, keep, send, seed = line.step(
        lambda *args: call(
            fourth_kernel, "fourth_both", args,
            [(row, f32, "vmem"), (row, f32, "vmem"), (three_quarters, bf16, "vmem"),
             (three_quarters, bf16, "vmem"), (row, bf16, "vmem")],
            [VMEM((2, 1, D, D), bf16), VMEM(row, bf16), pltpu.SemaphoreType.DMA((3,))],
            {3: HBM, 4: HBM, 5: HBM}, hint=3,
        ),
        limits, h3, gains, cotangent, up_four, down_four,
        near_four, far_four, other_near_four, other_far_four,
    )
    four = Chunk(line, keep, send)
    out, grad_h3, last_keep, last_send, gain_grad_four = line.step(
        lambda *args: call(
            fourth_end_kernel, "fourth_end", args,
            [(row, f32, "plain"), (row, bf16, "vmem"), (square, bf16, "vmem"), (square, bf16, "vmem"),
             (gain_row, f32, "vmem")], hint=20,
        ),
        h3, gains, seed, after, grad_normed, both_four, other_both_four,
    )
    grad_h2, third_weights, grad_shared, gain_grad_three = line.step(
        lambda *args: call(
            third_back_kernel, "third_backward", args,
            [(row, bf16, "vmem"), ((2, 2 * D, D), bf16, "vmem"), ((rows, shared_width), bf16, "vmem"),
             (gain_row, f32, "vmem")],
            back_scratch, hint=8,
        ),
        h2, gains, grad_h3, mixed_three, attended_three, chances_three, mixing_three, out_three,
    )
    four.begin_both(last_keep, last_send, 20)
    four.begin_near(20)
    grad_h1, keep, send, gain_grad_two = line.step(
        lambda *args: call(
            second_back_kernel, "second_backward", args,
            [(row, bf16, "vmem"), (packed, bf16, "vmem"), (packed, bf16, "vmem"), (gain_row, f32, "vmem")], hint=20,
        ),
        h1, gains, grad_h2, held_two, actives, slopes,
    )
    two = Chunk(line, keep, send)
    four.turn(20)
    input_grad, keep, send = line.step(
        lambda *args: call(
            first_back_kernel, "first_backward", args,
            [(row, f32, "plain"), (packed, bf16, "vmem"), (packed, bf16, "vmem")],
            back_scratch, hint=8,
        ),
        tokens, gains, grad_h1, mixed_one, attended_one, chances_one, mixing, output,
        grad_shared, third_weights, gain_grad_two, gain_grad_three, gain_grad_four,
    )
    first = Chunk(line, keep, send)
    two.begin(20)
    four.own(5)
    first.begin(5)
    two.turn(20)
    four.along(5)
    two.own(1)
    four.across(20)
    first.turn(6)
    two.along(8)
    four.share_far(5)
    first.own(20)
    two.across(20)
    four.pass_pair(2)
    first.along(20)
    two.share(20)
    first.across(5)
    four.end_pair(5)
    two.pass_on(1)
    first.share(5)
    two.end(3)
    first.pass_on(2)
    feed_outs = [((D, 4 * D), f32, "hbm"), ((4 * D, D), f32, "hbm")]
    feed_scratch = [VMEM((8, D, D), f32), pltpu.SemaphoreType.DMA((8,))]
    grad_up_four, grad_down_four = line.step(
        lambda *args: call(unpack_feed_kernel, "unpack_four", args, feed_outs, feed_scratch, hint=3),
        *four.pieces,
    )
    first.pass_near(2)
    grad_up_two, grad_down_two = line.step(
        lambda *args: call(unpack_feed_kernel, "unpack_two", args, feed_outs, feed_scratch, hint=1),
        *two.pieces,
    )
    first.end_alone(8)
    attention_outs = [
        ((D, 3 * D), f32, "hbm"), (square, f32, "hbm"), ((D, 2 * D), f32, "hbm"),
        ((D // 2, D), f32, "hbm"), (square, f32, "hbm"),
    ] + [((D,), f32, "plain")] * 4
    unpacked = line.step(
        lambda *args: call(
            unpack_some_kernel, "unpack_some", args, attention_outs,
            [VMEM((6, D, D), f32), pltpu.SemaphoreType.DMA((6, 2))], hint=3,
        ),
        first.mine, first.far, first.near, *first.others,
    )
    mixing_g, output_g, pair_g, fresh_g, output_three_g, g1, g2, g3, g4 = line.step(
        lambda *args: call(
            unpack_rest_kernel, "unpack_rest", args, attention_outs,
            [VMEM((2, D, D), f32), pltpu.SemaphoreType.DMA((2, 2))], {i: HBM for i in range(2, 7)},
            hint=4, aliases={i + 2: i for i in range(5)},
        ),
        *first.pieces, *unpacked,
    )
    return (
        out, input_grad, g1, mixing_g, output_g, g2, grad_up_two, grad_down_two,
        g3, pair_g, fresh_g.T, output_three_g, g4, grad_up_four, grad_down_four,
    )


def solution(mesh):
    return jax.shard_map(
        shards,
        mesh=mesh,
        in_specs=(
            P(("section", "dp"), None),
            P(("section", "dp"), None),
            P(None, "dp"),
            P("section"),
            P(None, "section"),
            P(None, "section"),
            P("section"),
            P(None, "section"),
            P("section", None),
            P("section"),
            P(None, "section"),
            P(None, "section"),
            P(None, "section"),
            P("section"),
            P(None, "section"),
            P("section", None),
        ),
        out_specs=(P(("section", "dp"), None), P(("section", "dp"), None)) + (P(),) * 13,
        check_vma=False,
    )
```

```python
import functools

import jax
import jax.numpy as jnp
from jax import lax
from jax.experimental import pallas as pl
from jax.experimental.pallas import tpu as pltpu
from jax.sharding import PartitionSpec as P

D = 384
HEADS = 6
HEAD = 64
SHARED = 3
QUARTERS = 4

EPSILON = 1e-05
MASKED = -1e30
GELU_SCALE = 0.7978845608028654
GELU_CUBE = 0.044715

f32 = jnp.float32
bf16 = jnp.bfloat16


def nn(left, right):
    return jnp.dot(left, right, preferred_element_type=f32)


def nt(left, right):
    return lax.dot_general(left, right, (((1,), (1,)), ((), ())), preferred_element_type=f32)


def centre(hidden):
    centred = hidden - jnp.mean(hidden, -1, keepdims=True)
    spread = jnp.mean(centred * centred, -1, keepdims=True)
    rstd = lax.rsqrt(spread + EPSILON)
    return centred * rstd, rstd


def norm_back(scaled, rstd, gain, grad):
    grad_gain = jnp.sum(grad * scaled, 0, keepdims=True)
    c = grad * gain
    along = jnp.mean(c * scaled, -1, keepdims=True)
    return rstd * (c - jnp.mean(c, -1, keepdims=True) - scaled * along), grad_gain


def swapped(rank):
    return ((rank & 1) << 1) | (rank >> 1)


def place():
    return lax.axis_index("section"), lax.axis_index("dp") & 1


def select_pieces(pieces):
    near, far, both, other_near, other_far, other_both = pieces
    first = place()[1] == 0

    def pick(left, right):
        return jnp.where(first, left[...], right[...])

    return (
        (pick(near, other_near), pick(far, other_far), pick(both, other_both)),
        (pick(other_far, far), pick(other_near, near), pick(other_both, both)),
    )


def put(keep, send, rank, half_zero, half_one, rows=None):
    first = place()[1] == 0
    zero, one = rank, swapped(rank)
    kept, sent = jnp.where(first, zero, one), jnp.where(first, one, zero)
    if rows is None:
        keep[kept] = jnp.where(first, half_zero, half_one)
        send[sent] = jnp.where(first, half_one, half_zero)
    else:
        keep[kept, pl.ds(*rows)] = jnp.where(first, half_zero, half_one)
        send[sent, pl.ds(*rows)] = jnp.where(first, half_one, half_zero)


def query_blocks(rows):
    step = min(rows, 128)
    return [(first, first + step) for first in range(0, rows, step)]


def usable(first, last, limits):
    key_index = lax.broadcasted_iota(jnp.int32, (last, last - first), 0)
    query_index = lax.broadcasted_iota(jnp.int32, (last, last - first), 1) + first
    return (key_index <= query_index) & (key_index < limits[0:1, first:last])


def one_head(block, side):
    lane = lax.broadcasted_iota(jnp.int32, block.shape, 1)
    return jnp.where((lane < HEAD) if side == 0 else (lane >= HEAD), block, 0)


def pair_at(head):
    return 2 * HEAD * (head // 2)


def attend(mixed, limits, probabilities):
    blocks = query_blocks(mixed.shape[0])
    values_across = mixed[:, 2 * D :].T
    allowed = [usable(first, last, limits) for first, last in blocks]
    for head in range(HEADS):
        at = pair_at(head)
        for (first, last), mask in zip(blocks, allowed):
            queries = one_head(mixed[first:last, at : at + 2 * HEAD], head % 2)
            scores = nt(mixed[:last, D + at : D + at + 2 * HEAD], queries) * HEAD ** (-0.5)
            probabilities[head, :last, first:last] = jnp.where(mask, scores, MASKED)
    outs = []
    for head in range(HEADS):
        parts = []
        for first, last in blocks:
            scores = probabilities[head, :last, first:last]
            raised = jnp.exp(scores - jnp.max(scores, 0, keepdims=True))
            probability = raised * (1.0 / jnp.sum(raised, 0, keepdims=True))
            probabilities[head, :last, first:last] = probability
            values = values_across[HEAD * head : HEAD * head + HEAD, :last]
            parts.append(nn(values, probability.astype(bf16)))
        outs.append(jnp.concatenate(parts, 1))
    return jnp.concatenate(outs, 0).T.astype(bf16)


def attend_back(mixed, grad_heads, probabilities, grad_mixed, grad_probs, rounded):
    rows = mixed.shape[0]
    blocks = query_blocks(rows)
    keys_across = mixed[:, D : 2 * D].T
    for head in range(HEADS):
        at = pair_at(head)
        for first, last in blocks:
            grads = one_head(grad_heads[first:last, at : at + 2 * HEAD], head % 2)
            values = mixed[:last, 2 * D + at : 2 * D + at + 2 * HEAD]
            grad_probs[head, :last, first:last] = nt(values, grads)
    for head in range(HEADS):
        for first, last in blocks:
            probability = probabilities[head, :last, first:last]
            grad_prob = grad_probs[head, :last, first:last]
            middle = jnp.sum(probability * grad_prob, 0, keepdims=True)
            rounded[0, head, :last, first:last] = (probability * (grad_prob - middle)).astype(bf16)
            rounded[1, head, :last, first:last] = probability.astype(bf16)
            if last < rows:
                unused = jnp.zeros((rows - last, last - first), bf16)
                rounded[0, head, last:, first:last] = unused
                rounded[1, head, last:, first:last] = unused
    query_parts = []
    for pair in range(HEADS // 2):
        at = 2 * HEAD * pair
        queries = mixed[:, at : at + 2 * HEAD]
        grads = grad_heads[:, at : at + 2 * HEAD]
        key_grad = value_grad = 0.0
        for side in range(2):
            head = 2 * pair + side
            key_grad += nn(rounded[0, head], one_head(queries, side))
            value_grad += nn(rounded[1, head], one_head(grads, side))
            query_parts.append(nn(keys_across[HEAD * head : HEAD * head + HEAD], rounded[0, head]))
        grad_mixed[:, D + at : D + at + 2 * HEAD] = (key_grad * HEAD ** (-0.5)).astype(bf16)
        grad_mixed[:, 2 * D + at : 2 * D + at + 2 * HEAD] = value_grad.astype(bf16)
    grad_mixed[:, :D] = (jnp.concatenate(query_parts, 0).T * HEAD ** (-0.5)).astype(bf16)


def prepare_kernel(
    mixing, output, pair, fresh, output_three, gain_one, gain_two, gain_three, gain_four,
    up_two, down_two, up_four, down_four, lengths,
    one, three, mine_one, mine_two, mine_four, limits, edge, narrow_one, narrow_two, narrow_three, narrow_four, counts, sems,
):
    core = place()[1]
    count = mixing.shape[0]
    wide, small = output.shape[0], fresh.shape[0]
    halves = [[(mixing, 0), (output, count)],
              [(pair, 0), (fresh, 2 * wide), (output_three, 2 * wide + small)]]
    last = 3 * wide + small
    copies = []
    for half, target in ((0, one), (1, three)):
        for source, row in halves[half]:
            rows = source.shape[0]
            copies.append((None, source, target.at[pl.ds(row, rows)]))
            copies.append((half, source, mine_one.at[pl.ds(row, rows)]))
    copies += [(0, up_two, mine_two), (1, down_two, mine_two)]
    copies += [(0, up_four, mine_four), (1, down_four, mine_four)]
    made = [
        (half, pltpu.make_async_copy(source, target, sems.at[i]))
        for i, (half, source, target) in enumerate(copies)
    ]
    for half, copy in made:
        if half is None:
            copy.start()
        else:
            pl.when(core == half)(copy.start)
    gains = [
        pltpu.make_async_copy(gain, narrow, sems.at[len(copies) + k])
        for k, (gain, narrow) in enumerate(
            ((gain_one, narrow_one), (gain_two, narrow_two), (gain_three, narrow_three), (gain_four, narrow_four))
        )
    ]
    for copy in gains:
        copy.start()
    counted = pltpu.make_async_copy(lengths, counts, sems.at[len(copies) + len(gains)])
    counted.start()
    edge[...] = jnp.zeros_like(edge)
    for k, narrow in enumerate((narrow_one, narrow_two, narrow_three, narrow_four)):
        gains[k].wait()
        edge[k : k + 1, : narrow.shape[0]] = narrow[...].astype(f32).reshape(1, narrow.shape[0])
    counted.wait()
    limits[...] = jnp.full(limits.shape, counts[0, place()[0]], jnp.int32)
    rows = D - last
    block = jnp.concatenate([edge[...], jnp.zeros((rows - 8, D), f32)], 0).astype(bf16)
    three[last:] = block

    @pl.when(core != 0)
    def _():
        mine_one[last:] = block

    for half, copy in made:
        if half is None:
            copy.wait()
        else:
            pl.when(core == half)(copy.wait)


def first_kernel(limits, tokens, own0, own1, *rest):
    h1, mixed, attended, probabilities, mixing, output, mixing_three, output_three, gains, held = rest[6:]
    section = place()[0]
    for half, (own, came) in enumerate(zip((own0, own1), select_pieces(rest[:6]))):
        held[half, section] = own[...]
        for rank in (1, 2, 3):
            held[half, section ^ rank] = came[rank - 1]
    shared_width = SHARED * HEAD
    mixing_three[2 * D : 2 * D + shared_width, :] = jnp.zeros((shared_width, D), bf16)
    for j in range(QUARTERS):
        mixing[288 * j : 288 * j + 288, :] = held[0, j, :288]
        output[96 * j : 96 * j + 96, :] = held[0, j, 288:]
        mixing_three[192 * j : 192 * j + 192, :] = held[1, j, :192]
        mixing_three[960 + 48 * j : 960 + 48 * j + 48, :] = held[1, j, 192:240]
        output_three[96 * j : 96 * j + 96, :] = held[1, j, 240:336]
        gains[0:8, 96 * j : 96 * j + 96] = held[1, j, 336:352, :96].astype(f32)[:8]
    hidden = tokens[...].astype(f32)
    scaled, _ = centre(hidden)
    normed = (scaled * gains[0:1, :]).astype(bf16)
    mixed[...] = nt(normed, mixing[...]).astype(bf16)
    attended[...] = attend(mixed, limits, probabilities)
    h1[...] = (hidden + nt(attended[...], output[...])).astype(bf16)


def bring(own0, own1, held, sems):
    copies = [
        pltpu.make_async_copy(own0, held.at[0, 0], sems.at[0]),
        pltpu.make_async_copy(own1, held.at[1, 0], sems.at[1]),
    ]
    for copy in copies:
        copy.start()
    return copies


def middle_kernel(limits, h1, gains, mixing_three, output_three, mixed_one, own0, own1, *rest):
    h2, held, h3, mixed, attended, probabilities, actives, slopes, sems = rest[6:]
    copies = bring(own0, own1, held, sems)
    hidden = h1[...].astype(f32)
    scaled, _ = centre(hidden)
    normed = (scaled * gains[1:2, :]).astype(bf16)
    ups, downs = select_pieces(rest[:6])
    for rank in (1, 2, 3):
        held[0, rank], held[1, rank] = ups[rank - 1], downs[rank - 1]
    for copy in copies:
        copy.wait()
    for rank in range(QUARTERS):
        slopes[rank] = nn(normed, held[0, rank])
    for rank in range(QUARTERS):
        actives[rank], slopes[rank] = feed_parts(slopes[rank])
    total = hidden
    for rank in range(QUARTERS):
        total += nn(actives[rank], held[1, rank])
    h2[...] = total.astype(bf16)
    hidden = h2[...].astype(f32)
    scaled, _ = centre(hidden)
    normed = (scaled * gains[2:3, :]).astype(bf16)
    mixed[...] = nt(normed, mixing_three[...]).astype(bf16)
    shared_width = SHARED * HEAD
    mixed[:, 2 * D : 2 * D + shared_width] = mixed_one[:, 2 * D : 2 * D + shared_width]
    attended[...] = attend(mixed, limits, probabilities)
    h3[...] = (hidden + nt(attended[...], output_three[...])).astype(bf16)


def feed_parts(upward):
    square = upward * upward
    rising = 0.5 + 0.5 * jnp.tanh(upward * (GELU_SCALE + (GELU_SCALE * GELU_CUBE) * square))
    active = upward * rising
    steep = 2.0 * GELU_SCALE + (6.0 * GELU_SCALE * GELU_CUBE) * square
    return active.astype(bf16), rising + active * (1.0 - rising) * steep


def quarter_back(up, down, normed_across, grad_out, active, slope):
    grad_upward = (nt(grad_out, down) * slope).astype(bf16)
    grad_down = nn(active.T, grad_out).astype(bf16)
    return nn(normed_across, grad_upward).astype(bf16), grad_down, nt(grad_upward, up)


def fourth_kernel(limits, h3, gains, cotangent, own0, own1, near, far, other_near, other_far, *rest):
    total, grad_normed, keep, send, seed, held, brought, sems = rest
    seeding = pltpu.make_async_copy(cotangent, brought, sems.at[2])
    seeding.start()
    copies = bring(own0, own1, held, sems)
    hidden = h3[...].astype(f32)
    scaled, _ = centre(hidden)
    normed = (scaled * gains[3:4, :]).astype(bf16)
    normed_across = normed.T
    first = place()[1] == 0
    after, grads = hidden, jnp.zeros(hidden.shape, f32)
    for rank in (1, 2, 0):
        if rank == 1:
            up = jnp.where(first, near[...], other_near[...])
            down = jnp.where(first, other_far[...], far[...])
        elif rank == 2:
            up = jnp.where(first, far[...], other_far[...])
            down = jnp.where(first, other_near[...], near[...])
        else:
            for copy in copies:
                copy.wait()
            up, down = held[0, 0], held[1, 0]
        active, slope = feed_parts(nn(normed, up))
        after += nn(active, down)
        if rank == 1:
            seeding.wait()
            row = lax.broadcasted_iota(jnp.int32, hidden.shape, 0)
            grad_out = jnp.where(row < limits[0:1, :1], brought[...], 0)
            seed[...] = grad_out
        grad_up, grad_down, grad = quarter_back(up, down, normed_across, grad_out, active, slope)
        put(keep, send, rank, grad_up, grad_down)
        grads += grad
    total[...] = after
    grad_normed[...] = grads


def fourth_end_kernel(
    h3, gains, seed, total, grads, both, other_both, out, grad_h3, keep, send, grad_gain
):
    scaled, rstd = centre(h3[...].astype(f32))
    gain = gains[3:4, :]
    normed = (scaled * gain).astype(bf16)
    first = place()[1] == 0
    up = jnp.where(first, both[...], other_both[...])
    down = jnp.where(first, other_both[...], both[...])
    active, slope = feed_parts(nn(normed, up))
    out[...] = total[...] + nn(active, down)
    grad_up, grad_down, grad = quarter_back(up, down, normed.T, seed[...], active, slope)
    keep[...] = jnp.where(first, grad_up, grad_down)
    send[...] = jnp.where(first, grad_down, grad_up)
    grad_hidden, one_gain = norm_back(scaled, rstd, gain, grads[...] + grad)
    grad_gain[0:1, :] = one_gain
    grad_h3[...] = (seed[...].astype(f32) + grad_hidden).astype(bf16)


def attention_back(hidden, grad_out, mixed, attended, probabilities, mixing, output, gain, scratch, shared, value_grad):
    scaled, rstd = centre(hidden)
    normed_across = (scaled * gain).astype(bf16).T
    grad_heads = nn(grad_out, output[...]).astype(bf16)
    grad_output = nn(attended[...].T, grad_out).astype(bf16)
    grad_mixed = scratch[0]
    attend_back(mixed, grad_heads, probabilities, *scratch)
    shared(grad_mixed)
    grad_pair = nn(normed_across, grad_mixed[:, : 2 * D]).astype(bf16)
    grad_values = value_grad(scaled, gain, normed_across, grad_mixed)
    grad_hidden, grad_gain = norm_back(scaled, rstd, gain, nn(grad_mixed[...], mixing[...]))
    return grad_hidden, grad_gain, grad_pair, grad_values, grad_output


def third_back_kernel(
    h2, gains, grad_h3, mixed, attended, probabilities, mixing, output,
    grad_h2, grad_weights, grad_shared, grad_gain, *scratch,
):
    shared_width = SHARED * HEAD

    def hand_over(grads):
        grad_shared[...] = grads[:, 2 * D : 2 * D + shared_width]
        grads[:, 2 * D : 2 * D + shared_width] = jnp.zeros((grads.shape[0], shared_width), bf16)

    def fresh_grad(scaled, gain, normed_across, grads):
        across = grads[:, 2 * D + 2 * HEAD :].T
        return nn(across[HEAD:], (scaled * gain).astype(bf16)).astype(bf16)

    grad_hidden, one_gain, grad_pair, grad_fresh, grad_output = attention_back(
        h2[...].astype(f32), grad_h3[...], mixed, attended, probabilities, mixing, output,
        gains[2:3, :], scratch, hand_over, fresh_grad,
    )
    grad_weights[0, :D] = grad_pair[:, :D]
    grad_weights[0, D:] = grad_pair[:, D:]
    grad_weights[1, :shared_width] = jnp.zeros((shared_width, D), bf16)
    grad_weights[1, shared_width:D] = grad_fresh
    grad_weights[1, D:] = grad_output
    grad_gain[0:1, :] = one_gain
    grad_h2[...] = (grad_h3[...].astype(f32) + grad_hidden).astype(bf16)


def second_back_kernel(h1, gains, grad_h2, held, actives, slopes, grad_h1, keep, send, grad_gain):
    scaled, rstd = centre(h1[...].astype(f32))
    gain = gains[1:2, :]
    normed_across = (scaled * gain).astype(bf16).T
    grads = jnp.zeros(scaled.shape, f32)
    for rank in range(QUARTERS):
        grad_up, grad_down, grad = quarter_back(
            held[0, rank], held[1, rank], normed_across, grad_h2[...], actives[rank], slopes[rank]
        )
        put(keep, send, rank, grad_up, grad_down)
        grads += grad
    grad_hidden, one_gain = norm_back(scaled, rstd, gain, grads)
    grad_gain[0:1, :] = one_gain
    grad_h1[...] = (grad_h2[...].astype(f32) + grad_hidden).astype(bf16)


def first_back_kernel(
    tokens, gains, grad_h1, mixed, attended, probabilities, mixing, output,
    grad_shared, third_weights, gain_two, gain_three, gain_four,
    input_grad, keep, send, *scratch,
):
    shared_width = SHARED * HEAD

    def take_over(grads):
        at = slice(2 * D, 2 * D + shared_width)
        grads[:, at] = (grads[:, at].astype(f32) + grad_shared[...].astype(f32)).astype(bf16)

    def value_grad(scaled, gain, normed_across, grads):
        return nn(normed_across, grads[:, 2 * D :]).astype(bf16)

    grad_hidden, gain_one, grad_pair, grad_values, grad_output = attention_back(
        tokens[...].astype(f32), grad_h1[...], mixed, attended, probabilities, mixing, output,
        gains[0:1, :], scratch, take_over, value_grad,
    )
    input_grad[...] = grad_h1[...].astype(f32) + grad_hidden
    section, part = place()[0], D // 2
    gain_rows = jnp.concatenate(
        [gain_one, gain_two[0:1, :], gain_three[0:1, :], gain_four[0:1, :], jnp.zeros((12, D), f32)], 0
    ).astype(bf16)
    for j in range(QUARTERS):
        at = slice(part * (j % 2), part * (j % 2) + part)
        zero = (grad_pair[:, :D], grad_pair[:, D:])[j // 2][at]
        one = (grad_values, grad_output)[j // 2][at]
        put(keep, send, section ^ j, zero, one, (0, part))
        below = third_weights[1, part * j : part * j + part]
        if j == 0:
            below = jnp.concatenate([gain_rows, below[16:]], 0)
        put(keep, send, section ^ j, third_weights[0, part * j : part * j + part], below, (part, part))


def pieces_of(refs):
    if len(refs) == 4:
        for own, (mine, pair) in ((True, refs[:2]), (False, refs[2:])):
            yield own, 0, mine[0]
            yield own, 2, mine[1]
            yield own, 1, pair[0]
            yield own, 3, pair[1]
        return
    for own, (mine, far, pair) in ((True, refs[:3]), (False, refs[3:])):
        yield own, 0, mine[...]
        yield own, 2, far[...]
        yield own, 1, pair[0]
        yield own, 3, pair[1]


def unpack_feed_kernel(*rest):
    up, down, wide, sems = rest[-4:]
    section, core = place()
    steps = []
    for slot, (own, rank, value) in enumerate(pieces_of(rest[:-4])):
        wide[slot] = value.astype(f32)
        zero = (core == 0) if own else (core != 0)
        column = pl.ds(pl.multiple_of((section ^ rank) * D, D), D)
        below = pl.ds(pl.multiple_of((section ^ swapped(rank)) * D, D), D)
        steps += [
            (zero, pltpu.make_async_copy(wide.at[slot], up.at[:, column], sems.at[slot])),
            (jnp.logical_not(zero), pltpu.make_async_copy(wide.at[slot], down.at[below, :], sems.at[slot])),
        ]
        for flag, copy in steps[-2:]:
            pl.when(flag)(copy.start)
    for flag, copy in steps:
        pl.when(flag)(copy.wait)


def unpack_attention(pieces, targets, gains, wide, sems):
    mixing, output, pair, fresh, output_three = targets
    section, core = place()
    part = D // 2
    steps = []
    for slot, (own, rank, value) in enumerate(pieces):
        wide[slot] = value[...].astype(f32)
        zero = (core == 0) if own else (core != 0)
        j0, j1 = section ^ rank, section ^ swapped(rank)
        column = pl.ds(pl.multiple_of((j0 >> 1) * D, D), D)
        row0 = pl.ds(pl.multiple_of((j0 & 1) * part, part), part)
        row1 = pl.ds(pl.multiple_of((j1 & 1) * part, part), part)
        one = jnp.logical_not(zero)

        @pl.when(one & (j1 == 0))
        def _():
            for k, ref in enumerate(gains):
                ref[...] = wide[slot, part + k]

        for low, flag, target in (
            (0, zero, mixing.at[row0, column]),
            (1, zero, pair.at[row0, column]),
            (0, one & (j1 < 2), mixing.at[row1, 2 * D :]),
            (1, one & (j1 == 1), fresh),
            (0, one & (j1 >= 2), output.at[row1, :]),
            (1, one & (j1 >= 2), output_three.at[row1, :]),
        ):
            copy = pltpu.make_async_copy(
                wide.at[slot, part * low : part * low + part], target, sems.at[slot, low]
            )
            steps.append((flag, copy))
            pl.when(flag)(copy.start)
    for flag, copy in steps:
        pl.when(flag)(copy.wait)


def unpack_some_kernel(*rest):
    pieces, outs, (wide, sems) = rest[:6], rest[6:-2], rest[-2:]
    ranked = [(own, rank, pieces[3 * k + i]) for k, own in enumerate((True, False)) for i, rank in enumerate((0, 2, 1))]
    for ref in outs[5:]:
        ref[...] = jnp.zeros(ref.shape, f32)
    unpack_attention(ranked, outs[:5], outs[5:], wide, sems)


def unpack_rest_kernel(*rest):
    pieces, before, outs, (wide, sems) = rest[:2], rest[7:11], rest[11:-2], rest[-2:]
    for ref, old in zip(outs[5:], before):
        ref[...] = old[...]
    unpack_attention([(True, 3, pieces[0]), (False, 3, pieces[1])], outs[:5], outs[5:], wide, sems)


SMEM, VMEM, HBM = pltpu.SMEM, pltpu.VMEM, pltpu.HBM


def call(body, name, args, outs, scratch=(), spaces=None, limit=12, hint=20, aliases=None):
    spaces = spaces or {}
    args = [
        pltpu.with_memory_space_constraint(arg, HBM) if spaces.get(i) is HBM else arg
        for i, arg in enumerate(args)
    ]
    places = {"vmem": VMEM, "hbm": HBM}
    return pl.pallas_call(
        body,
        name=name,
        out_shape=[
            places[where](shape, dtype) if where in places else jax.ShapeDtypeStruct(shape, dtype)
            for shape, dtype, where in outs
        ],
        in_specs=[pl.BlockSpec(memory_space=spaces.get(i, VMEM)) for i in range(len(args))],
        out_specs=[pl.BlockSpec(memory_space=places.get(where, VMEM)) for _, _, where in outs],
        scratch_shapes=list(scratch),
        input_output_aliases=aliases or {},
        compiler_params=pltpu.CompilerParams(vmem_limit_bytes=limit * 1024 * 1024),
        cost_estimate=pl.CostEstimate(flops=hint * 10**9, bytes_accessed=1, transcendentals=1),
    )(*args)


def partner_pairs(sections, groups, kind):
    found = []
    for section in range(sections):
        for group in range(groups):
            core = group & 1
            to_section, to_group = section, group
            if kind == "near":
                to_section = section ^ (1 if core == 0 else 2)
            elif kind == "far":
                to_section = section ^ (2 if core == 0 else 1)
            else:
                to_group = group ^ kind
            found.append((section * groups + group, to_section * groups + to_group))
    return found


def partner(value, kind):
    sections, groups = lax.axis_size("section"), lax.axis_size("dp")
    return lax.ppermute(value, ("section", "dp"), partner_pairs(sections, groups, kind))


def total(*parts):
    return sum(part.astype(f32) for part in parts).astype(bf16)


def chip_bit():
    return (lax.axis_index("dp") >> 1) & 1


def one_sum_kernel(index, keep, came, out):
    out[...] = total(keep[index], came[index])


def begin_kernel(keep, came, both, near):
    both[...] = total(keep[3], came[3])
    near[...] = total(keep[1], came[1])


def begin_pair_kernel(keep, came, pair):
    pair[0] = total(keep[3], came[3])
    pair[1] = total(keep[1], came[1])


def turn_pair_kernel(keep, came, pair, far):
    far[...] = total(keep[2], came[2], pair[0])


def own_pair_kernel(keep, came, pair, far, away, kept, halves):
    own_kernel(keep, came, pair.at[1], far, away, kept, halves)


def turn_kernel(keep, came, both, far):
    far[...] = total(keep[2], came[2], both[...])


def own_kernel(keep, came, near, far, away, kept, halves):
    rows = kept.shape[0]
    own = total(keep[0], came[0], near[...], far[...])
    halves[0] = own[:rows]
    halves[1] = own[rows:]
    bit = chip_bit()
    kept[...] = halves[bit]
    away[...] = halves[1 - bit]


def copy_kernel(value, out):
    out[...] = value[...]


def pair_kernel(left, right, out):
    out[0] = left[...]
    out[1] = right[...]


def copy_both_kernel(left, right, left_out, right_out):
    left_out[...] = left[...]
    right_out[...] = right[...]


def sum_kernel(left, right, out):
    out[...] = total(left[...], right[...])


def join_kernel(kept, back, own):
    rows = kept.shape[0]
    bit = chip_bit()
    own[pl.ds(pl.multiple_of(bit * rows, rows), rows)] = kept[...]
    own[pl.ds(pl.multiple_of((1 - bit) * rows, rows), rows)] = back[...]


class Line:
    def __init__(self):
        self.last = ()

    def tied(self, *values):
        if not self.last:
            return values
        return lax.optimization_barrier(values + self.last)[: len(values)]

    def step(self, made, *values):
        made = made(*self.tied(*values))
        self.last = (jax.tree.leaves(made)[0],)
        return made

    def hop(self, value, kind):
        return partner(self.tied(value)[0], kind)

    def gate(self, value, hint):
        copy = [(value.shape, value.dtype, "vmem")]
        return self.step(lambda v: call(copy_kernel, "gate", (v,), copy, limit=4, hint=hint)[0], value)


class Chunk:
    def __init__(self, line, keep, send):
        self.line, self.keep = line, keep
        self.came = partner(send, 1)
        self.groups = lax.axis_size("dp")

    def made(self, hint, body, name, outs, *args, scratch=()):
        return self.line.step(
            lambda *tied: call(
                body, name, tied, [(shape, bf16, "vmem") for shape in outs], scratch, limit=4, hint=hint
            ),
            *args,
        )

    def begin(self, hint):
        block = self.keep.shape[1:]
        both, near = self.made(hint, begin_kernel, "sum_begin", [block] * 2, self.keep, self.came)
        self.both, self.near = partner(both, "near"), partner(near, "near")

    def begin_merged(self, hint):
        shape = (2,) + self.keep.shape[1:]
        (pair,) = self.made(hint, begin_pair_kernel, "sum_begin", [shape], self.keep, self.came)
        self.both = self.near = partner(pair, "near")

    def begin_near(self, hint):
        body = functools.partial(one_sum_kernel, 1)
        (near,) = self.made(hint, body, "sum_near", [self.keep.shape[1:]], self.keep, self.came)
        self.near = partner(near, "near")

    def begin_both(self, keep, send, hint):
        (both,) = self.made(hint, sum_kernel, "sum_both", [keep.shape], keep, partner(send, 1))
        self.both = partner(both, "near")

    def turn(self, hint):
        body = turn_kernel if self.both is not self.near else turn_pair_kernel
        (far,) = self.made(hint, body, "sum_turn", [self.keep.shape[1:]], self.keep, self.came, self.both)
        self.far = partner(far, "far")

    def own(self, hint):
        rows, width = self.keep.shape[1:]
        half = (rows // 2, width)
        body = own_kernel if self.both is not self.near else own_pair_kernel
        away, self.kept = self.made(
            hint, body, "sum_own", [half] * 2, self.keep, self.came, self.near, self.far,
            scratch=[VMEM((2,) + half, bf16)],
        )
        self.back = partner(away, 2)

    def plus(self, came, hint):
        (self.kept,) = self.made(hint, sum_kernel, "sum_chips", [self.kept.shape], self.kept, came)

    def along(self, hint):
        self.plus(self.back, hint)
        step = 4
        while step < self.groups:
            self.back = partner(self.kept, step)
            step *= 2
            if step < self.groups:
                self.plus(self.back, hint)

    def across(self, hint):
        if self.groups > 4:
            self.plus(self.back, hint)
        self.back = partner(self.kept, 2)

    def share(self, hint):
        rows, width = self.kept.shape
        (own,) = self.made(hint, join_kernel, "sum_join", [(2 * rows, width)], self.kept, self.back)
        self.mine, self.far, self.near = own, partner(own, "far"), partner(own, "near")
        self.others = [partner(own, 1)]

    def pass_on(self, hint):
        self.far = self.line.gate(self.far, hint)
        self.both = partner(self.far, "near")
        self.others.append(partner(self.far, 1))

    def end(self, hint):
        shape = (2,) + self.far.shape
        (pair,) = self.made(hint, pair_kernel, "sum_pair", [shape], self.near, self.both)
        self.pieces = [self.mine, self.far, pair] + self.others + [partner(pair, 1)]

    def share_far(self, hint):
        rows, width = self.kept.shape
        (self.mine,) = self.made(hint, join_kernel, "sum_join", [(2 * rows, width)], self.kept, self.back)
        self.far = partner(self.mine, "far")

    def pass_pair(self, hint):
        shape = (2,) + self.mine.shape
        (self.mine,) = self.made(hint, pair_kernel, "sum_pair", [shape], self.mine, self.far)
        self.near = partner(self.mine, "near")
        self.others = [partner(self.mine, 1)]

    def end_pair(self, hint):
        pair = self.line.gate(self.near, hint)
        self.pieces = [self.mine, pair] + self.others + [partner(pair, 1)]

    def pass_near(self, hint):
        self.near = self.line.gate(self.near, hint)
        self.others.append(partner(self.near, 1))

    def end_alone(self, hint):
        both = self.line.gate(self.both, hint)
        self.pieces = [both, partner(both, 1)]


def shards(
    tokens,
    cotangent,
    lengths,
    gain_one,
    mixing_one,
    output_one,
    gain_two,
    up_two,
    down_two,
    gain_three,
    pair_three,
    fresh_three,
    output_three,
    gain_four,
    up_four,
    down_four,
):
    rows = tokens.shape[0]
    square = (D, D)
    row, wide_row, held = (rows, D), (rows, 3 * D), (2, QUARTERS, D, D)
    gain_row, packed, chances = (8, D), (QUARTERS, D, D), (HEADS, rows, rows)
    hidden_row = (QUARTERS,) + row
    back_scratch = [VMEM(wide_row, bf16), VMEM(chances, f32), VMEM((2,) + chances, bf16)]
    shared_width = SHARED * HEAD
    line = Line()

    half_one, half_three, mine_one, mine_two, mine_four, limits = call(
        prepare_kernel, "prepare",
        (mixing_one.T, output_one.T, pair_three.T, fresh_three.T, output_three.T,
         gain_one, gain_two, gain_three, gain_four, up_two, down_two, up_four, down_four, lengths.T),
        [(square, bf16, "vmem")] * 5 + [((8, rows), jnp.int32, "vmem")],
        [VMEM((8, D), f32)] + [VMEM(gain_one.shape, bf16)] * 4
        + [SMEM(lengths.T.shape, jnp.int32), pltpu.SemaphoreType.DMA((19,))],
        {i: HBM for i in range(14)},
    )
    near_one, far_one = partner(mine_one, "near"), partner(mine_one, "far")
    near_two, far_two = partner(mine_two, "near"), partner(mine_two, "far")
    limits = line.gate(limits, 0)
    near_one = line.gate(near_one, 3)
    other_near_one = partner(near_one, 1)
    both_one = partner(near_one, "far")
    far_one = line.gate(far_one, 3)
    other_far_one = partner(far_one, 1)
    near_two = line.gate(near_two, 3)
    other_near_two = partner(near_two, 1)
    both_two = partner(near_two, "far")
    mine_four = line.gate(mine_four, 3)
    near_four, far_four = partner(mine_four, "near"), partner(mine_four, "far")
    both_one = line.gate(both_one, 8)
    other_both_one = partner(both_one, 1)
    far_two = line.gate(far_two, 3)
    other_far_two = partner(far_two, 1)
    both_two = line.gate(both_two, 3)
    other_both_two = partner(both_two, 1)
    h1, mixed_one, attended_one, chances_one, mixing, output, mixing_three, out_three, gains = line.step(
        lambda *args: call(
            first_kernel, "first_forward", args,
            [(row, bf16, "vmem"), (wide_row, bf16, "vmem"), (row, bf16, "vmem"), (chances, f32, "vmem"),
             ((3 * D, D), bf16, "vmem"), (square, bf16, "vmem"), ((3 * D, D), bf16, "vmem"),
             (square, bf16, "vmem"), (gain_row, f32, "vmem")],
            [VMEM(held, bf16)], hint=6,
        ),
        limits, tokens, half_one, half_three,
        near_one, far_one, both_one, other_near_one, other_far_one, other_both_one,
    )
    near_four = line.gate(near_four, 3)
    other_near_four = partner(near_four, 1)
    both_four = partner(near_four, "far")
    far_four = line.gate(far_four, 4)
    other_far_four = partner(far_four, 1)
    h2, held_two, h3, mixed_three, attended_three, chances_three, actives, slopes = line.step(
        lambda *args: call(
            middle_kernel, "second_third_forward", args,
            [(row, bf16, "vmem"), (held, bf16, "vmem"), (row, bf16, "vmem"), (wide_row, bf16, "vmem"),
             (row, bf16, "vmem"), (chances, f32, "vmem"), (hidden_row, bf16, "vmem"),
             (hidden_row, f32, "vmem")],
            [pltpu.SemaphoreType.DMA((2,))], {6: HBM, 7: HBM}, hint=3,
        ),
        limits, h1, gains, mixing_three, out_three, mixed_one, up_two, down_two,
        near_two, far_two, both_two, other_near_two, other_far_two, other_both_two,
    )
    both_four = line.gate(both_four, 2)
    other_both_four = partner(both_four, 1)
    three_quarters = (QUARTERS - 1, D, D)
    after, grad_normed, keep, send, seed = line.step(
        lambda *args: call(
            fourth_kernel, "fourth_both", args,
            [(row, f32, "vmem"), (row, f32, "vmem"), (three_quarters, bf16, "vmem"),
             (three_quarters, bf16, "vmem"), (row, bf16, "vmem")],
            [VMEM((2, 1, D, D), bf16), VMEM(row, bf16), pltpu.SemaphoreType.DMA((3,))],
            {3: HBM, 4: HBM, 5: HBM}, hint=3,
        ),
        limits, h3, gains, cotangent, up_four, down_four,
        near_four, far_four, other_near_four, other_far_four,
    )
    four = Chunk(line, keep, send)
    out, grad_h3, last_keep, last_send, gain_grad_four = line.step(
        lambda *args: call(
            fourth_end_kernel, "fourth_end", args,
            [(row, f32, "plain"), (row, bf16, "vmem"), (square, bf16, "vmem"), (square, bf16, "vmem"),
             (gain_row, f32, "vmem")], hint=20,
        ),
        h3, gains, seed, after, grad_normed, both_four, other_both_four,
    )
    grad_h2, third_weights, grad_shared, gain_grad_three = line.step(
        lambda *args: call(
            third_back_kernel, "third_backward", args,
            [(row, bf16, "vmem"), ((2, 2 * D, D), bf16, "vmem"), ((rows, shared_width), bf16, "vmem"),
             (gain_row, f32, "vmem")],
            back_scratch, hint=8,
        ),
        h2, gains, grad_h3, mixed_three, attended_three, chances_three, mixing_three, out_three,
    )
    four.begin_both(last_keep, last_send, 20)
    four.begin_near(20)
    grad_h1, keep, send, gain_grad_two = line.step(
        lambda *args: call(
            second_back_kernel, "second_backward", args,
            [(row, bf16, "vmem"), (packed, bf16, "vmem"), (packed, bf16, "vmem"), (gain_row, f32, "vmem")], hint=20,
        ),
        h1, gains, grad_h2, held_two, actives, slopes,
    )
    two = Chunk(line, keep, send)
    input_grad, keep, send = line.step(
        lambda *args: call(
            first_back_kernel, "first_backward", args,
            [(row, f32, "plain"), (packed, bf16, "vmem"), (packed, bf16, "vmem")],
            back_scratch, hint=8,
        ),
        tokens, gains, grad_h1, mixed_one, attended_one, chances_one, mixing, output,
        grad_shared, third_weights, gain_grad_two, gain_grad_three, gain_grad_four,
    )
    first = Chunk(line, keep, send)
    four.turn(20)
    two.begin(20)
    first.begin(5)
    four.own(5)
    two.turn(20)
    four.along(5)
    two.own(1)
    four.across(20)
    first.turn(6)
    two.along(8)
    four.share_far(5)
    first.own(20)
    two.across(20)
    four.pass_pair(2)
    first.along(20)
    two.share(20)
    first.across(5)
    four.end_pair(5)
    two.pass_on(1)
    first.share(5)
    two.end(3)
    first.pass_on(2)
    feed_outs = [((D, 4 * D), f32, "hbm"), ((4 * D, D), f32, "hbm")]
    feed_scratch = [VMEM((8, D, D), f32), pltpu.SemaphoreType.DMA((8,))]
    grad_up_four, grad_down_four = line.step(
        lambda *args: call(unpack_feed_kernel, "unpack_four", args, feed_outs, feed_scratch, hint=3),
        *four.pieces,
    )
    first.pass_near(2)
    grad_up_two, grad_down_two = line.step(
        lambda *args: call(unpack_feed_kernel, "unpack_two", args, feed_outs, feed_scratch, hint=1),
        *two.pieces,
    )
    first.end_alone(8)
    attention_outs = [
        ((D, 3 * D), f32, "hbm"), (square, f32, "hbm"), ((D, 2 * D), f32, "hbm"),
        ((D // 2, D), f32, "hbm"), (square, f32, "hbm"),
    ] + [((D,), f32, "plain")] * 4
    unpacked = line.step(
        lambda *args: call(
            unpack_some_kernel, "unpack_some", args, attention_outs,
            [VMEM((6, D, D), f32), pltpu.SemaphoreType.DMA((6, 2))], hint=3,
        ),
        first.mine, first.far, first.near, *first.others,
    )
    mixing_g, output_g, pair_g, fresh_g, output_three_g, g1, g2, g3, g4 = line.step(
        lambda *args: call(
            unpack_rest_kernel, "unpack_rest", args, attention_outs,
            [VMEM((2, D, D), f32), pltpu.SemaphoreType.DMA((2, 2))], {i: HBM for i in range(2, 7)},
            hint=4, aliases={i + 2: i for i in range(5)},
        ),
        *first.pieces, *unpacked,
    )
    return (
        out, input_grad, g1, mixing_g, output_g, g2, grad_up_two, grad_down_two,
        g3, pair_g, fresh_g.T, output_three_g, g4, grad_up_four, grad_down_four,
    )


def solution(mesh):
    return jax.shard_map(
        shards,
        mesh=mesh,
        in_specs=(
            P(("section", "dp"), None),
            P(("section", "dp"), None),
            P(None, "dp"),
            P("section"),
            P(None, "section"),
            P(None, "section"),
            P("section"),
            P(None, "section"),
            P("section", None),
            P("section"),
            P(None, "section"),
            P(None, "section"),
            P(None, "section"),
            P("section"),
            P(None, "section"),
            P("section", None),
        ),
        out_specs=(P(("section", "dp"), None), P(("section", "dp"), None)) + (P(),) * 13,
        check_vma=False,
    )
```

```python
import functools

import jax
import jax.numpy as jnp
from jax import lax
from jax.experimental import pallas as pl
from jax.experimental.pallas import tpu as pltpu
from jax.sharding import PartitionSpec as P

D = 384
HEADS = 6
HEAD = 64
SHARED = 3
QUARTERS = 4

EPSILON = 1e-05
MASKED = -1e30
GELU_SCALE = 0.7978845608028654
GELU_CUBE = 0.044715

f32 = jnp.float32
bf16 = jnp.bfloat16


def nn(left, right):
    return jnp.dot(left, right, preferred_element_type=f32)


def nt(left, right):
    return lax.dot_general(left, right, (((1,), (1,)), ((), ())), preferred_element_type=f32)


def centre(hidden):
    centred = hidden - jnp.mean(hidden, -1, keepdims=True)
    spread = jnp.mean(centred * centred, -1, keepdims=True)
    rstd = lax.rsqrt(spread + EPSILON)
    return centred * rstd, rstd


def norm_back(scaled, rstd, gain, grad):
    grad_gain = jnp.sum(grad * scaled, 0, keepdims=True)
    c = grad * gain
    along = jnp.mean(c * scaled, -1, keepdims=True)
    return rstd * (c - jnp.mean(c, -1, keepdims=True) - scaled * along), grad_gain


def swapped(rank):
    return ((rank & 1) << 1) | (rank >> 1)


def place():
    return lax.axis_index("section"), lax.axis_index("dp") & 1


def select_pieces(pieces):
    near, far, both, other_near, other_far, other_both = pieces
    first = place()[1] == 0

    def pick(left, right):
        return jnp.where(first, left[...], right[...])

    return (
        (pick(near, other_near), pick(far, other_far), pick(both, other_both)),
        (pick(other_far, far), pick(other_near, near), pick(other_both, both)),
    )


def put(keep, send, rank, half_zero, half_one, rows=None):
    first = place()[1] == 0
    zero, one = rank, swapped(rank)
    kept, sent = jnp.where(first, zero, one), jnp.where(first, one, zero)
    if rows is None:
        keep[kept] = jnp.where(first, half_zero, half_one)
        send[sent] = jnp.where(first, half_one, half_zero)
    else:
        keep[kept, pl.ds(*rows)] = jnp.where(first, half_zero, half_one)
        send[sent, pl.ds(*rows)] = jnp.where(first, half_one, half_zero)


def query_blocks(rows):
    step = min(rows, 128)
    return [(first, first + step) for first in range(0, rows, step)]


def usable(first, last, limits):
    key_index = lax.broadcasted_iota(jnp.int32, (last, last - first), 0)
    query_index = lax.broadcasted_iota(jnp.int32, (last, last - first), 1) + first
    return (key_index <= query_index) & (key_index < limits[0:1, first:last])


def one_head(block, side):
    lane = lax.broadcasted_iota(jnp.int32, block.shape, 1)
    return jnp.where((lane < HEAD) if side == 0 else (lane >= HEAD), block, 0)


def pair_at(head):
    return 2 * HEAD * (head // 2)


def attend(mixed, limits, probabilities):
    blocks = query_blocks(mixed.shape[0])
    values_across = mixed[:, 2 * D :].T
    allowed = [usable(first, last, limits) for first, last in blocks]
    for head in range(HEADS):
        at = pair_at(head)
        for (first, last), mask in zip(blocks, allowed):
            queries = one_head(mixed[first:last, at : at + 2 * HEAD], head % 2)
            scores = nt(mixed[:last, D + at : D + at + 2 * HEAD], queries) * HEAD ** (-0.5)
            probabilities[head, :last, first:last] = jnp.where(mask, scores, MASKED)
    outs = []
    for head in range(HEADS):
        parts = []
        for first, last in blocks:
            scores = probabilities[head, :last, first:last]
            raised = jnp.exp(scores - jnp.max(scores, 0, keepdims=True))
            probability = raised * (1.0 / jnp.sum(raised, 0, keepdims=True))
            probabilities[head, :last, first:last] = probability
            values = values_across[HEAD * head : HEAD * head + HEAD, :last]
            parts.append(nn(values, probability.astype(bf16)))
        outs.append(jnp.concatenate(parts, 1))
    return jnp.concatenate(outs, 0).T.astype(bf16)


def attend_back(mixed, grad_heads, probabilities, grad_mixed, grad_probs, rounded):
    rows = mixed.shape[0]
    blocks = query_blocks(rows)
    keys_across = mixed[:, D : 2 * D].T
    for head in range(HEADS):
        at = pair_at(head)
        for first, last in blocks:
            grads = one_head(grad_heads[first:last, at : at + 2 * HEAD], head % 2)
            values = mixed[:last, 2 * D + at : 2 * D + at + 2 * HEAD]
            grad_probs[head, :last, first:last] = nt(values, grads)
    for head in range(HEADS):
        for first, last in blocks:
            probability = probabilities[head, :last, first:last]
            grad_prob = grad_probs[head, :last, first:last]
            middle = jnp.sum(probability * grad_prob, 0, keepdims=True)
            rounded[0, head, :last, first:last] = (probability * (grad_prob - middle)).astype(bf16)
            rounded[1, head, :last, first:last] = probability.astype(bf16)
            if last < rows:
                unused = jnp.zeros((rows - last, last - first), bf16)
                rounded[0, head, last:, first:last] = unused
                rounded[1, head, last:, first:last] = unused
    query_parts = []
    for pair in range(HEADS // 2):
        at = 2 * HEAD * pair
        queries = mixed[:, at : at + 2 * HEAD]
        grads = grad_heads[:, at : at + 2 * HEAD]
        key_grad = value_grad = 0.0
        for side in range(2):
            head = 2 * pair + side
            key_grad += nn(rounded[0, head], one_head(queries, side))
            value_grad += nn(rounded[1, head], one_head(grads, side))
            query_parts.append(nn(keys_across[HEAD * head : HEAD * head + HEAD], rounded[0, head]))
        grad_mixed[:, D + at : D + at + 2 * HEAD] = (key_grad * HEAD ** (-0.5)).astype(bf16)
        grad_mixed[:, 2 * D + at : 2 * D + at + 2 * HEAD] = value_grad.astype(bf16)
    grad_mixed[:, :D] = (jnp.concatenate(query_parts, 0).T * HEAD ** (-0.5)).astype(bf16)


def prepare_kernel(
    mixing, output, pair, fresh, output_three, gain_one, gain_two, gain_three, gain_four,
    up_two, down_two, up_four, down_four, lengths,
    one, three, mine_one, mine_two, mine_four, limits, edge, narrow_one, narrow_two, narrow_three, narrow_four, counts, sems,
):
    core = place()[1]
    count = mixing.shape[0]
    wide, small = output.shape[0], fresh.shape[0]
    halves = [[(mixing, 0), (output, count)],
              [(pair, 0), (fresh, 2 * wide), (output_three, 2 * wide + small)]]
    last = 3 * wide + small
    copies = []
    for half, target in ((0, one), (1, three)):
        for source, row in halves[half]:
            rows = source.shape[0]
            copies.append((None, source, target.at[pl.ds(row, rows)]))
            copies.append((half, source, mine_one.at[pl.ds(row, rows)]))
    copies += [(0, up_two, mine_two), (1, down_two, mine_two)]
    copies += [(0, up_four, mine_four), (1, down_four, mine_four)]
    made = [
        (half, pltpu.make_async_copy(source, target, sems.at[i]))
        for i, (half, source, target) in enumerate(copies)
    ]
    for half, copy in made:
        if half is None:
            copy.start()
        else:
            pl.when(core == half)(copy.start)
    gains = [
        pltpu.make_async_copy(gain, narrow, sems.at[len(copies) + k])
        for k, (gain, narrow) in enumerate(
            ((gain_one, narrow_one), (gain_two, narrow_two), (gain_three, narrow_three), (gain_four, narrow_four))
        )
    ]
    for copy in gains:
        copy.start()
    counted = pltpu.make_async_copy(lengths, counts, sems.at[len(copies) + len(gains)])
    counted.start()
    edge[...] = jnp.zeros_like(edge)
    for k, narrow in enumerate((narrow_one, narrow_two, narrow_three, narrow_four)):
        gains[k].wait()
        edge[k : k + 1, : narrow.shape[0]] = narrow[...].astype(f32).reshape(1, narrow.shape[0])
    counted.wait()
    limits[...] = jnp.full(limits.shape, counts[0, place()[0]], jnp.int32)
    rows = D - last
    block = jnp.concatenate([edge[...], jnp.zeros((rows - 8, D), f32)], 0).astype(bf16)
    three[last:] = block

    @pl.when(core != 0)
    def _():
        mine_one[last:] = block

    for half, copy in made:
        if half is None:
            copy.wait()
        else:
            pl.when(core == half)(copy.wait)


def first_kernel(limits, tokens, own0, own1, *rest):
    h1, mixed, attended, probabilities, mixing, output, mixing_three, output_three, gains, held = rest[6:]
    section = place()[0]
    for half, (own, came) in enumerate(zip((own0, own1), select_pieces(rest[:6]))):
        held[half, section] = own[...]
        for rank in (1, 2, 3):
            held[half, section ^ rank] = came[rank - 1]
    shared_width = SHARED * HEAD
    mixing_three[2 * D : 2 * D + shared_width, :] = jnp.zeros((shared_width, D), bf16)
    for j in range(QUARTERS):
        mixing[288 * j : 288 * j + 288, :] = held[0, j, :288]
        output[96 * j : 96 * j + 96, :] = held[0, j, 288:]
        mixing_three[192 * j : 192 * j + 192, :] = held[1, j, :192]
        mixing_three[960 + 48 * j : 960 + 48 * j + 48, :] = held[1, j, 192:240]
        output_three[96 * j : 96 * j + 96, :] = held[1, j, 240:336]
        gains[0:8, 96 * j : 96 * j + 96] = held[1, j, 336:352, :96].astype(f32)[:8]
    hidden = tokens[...].astype(f32)
    scaled, _ = centre(hidden)
    normed = (scaled * gains[0:1, :]).astype(bf16)
    mixed[...] = nt(normed, mixing[...]).astype(bf16)
    attended[...] = attend(mixed, limits, probabilities)
    h1[...] = (hidden + nt(attended[...], output[...])).astype(bf16)


def bring(own0, own1, held, sems):
    copies = [
        pltpu.make_async_copy(own0, held.at[0, 0], sems.at[0]),
        pltpu.make_async_copy(own1, held.at[1, 0], sems.at[1]),
    ]
    for copy in copies:
        copy.start()
    return copies


def middle_kernel(limits, h1, gains, mixing_three, output_three, mixed_one, own0, own1, *rest):
    h2, held, h3, mixed, attended, probabilities, actives, slopes, sems = rest[6:]
    copies = bring(own0, own1, held, sems)
    hidden = h1[...].astype(f32)
    scaled, _ = centre(hidden)
    normed = (scaled * gains[1:2, :]).astype(bf16)
    ups, downs = select_pieces(rest[:6])
    for rank in (1, 2, 3):
        held[0, rank], held[1, rank] = ups[rank - 1], downs[rank - 1]
    for copy in copies:
        copy.wait()
    for rank in range(QUARTERS):
        slopes[rank] = nn(normed, held[0, rank])
    for rank in range(QUARTERS):
        actives[rank], slopes[rank] = feed_parts(slopes[rank])
    total = hidden
    for rank in range(QUARTERS):
        total += nn(actives[rank], held[1, rank])
    h2[...] = total.astype(bf16)
    hidden = h2[...].astype(f32)
    scaled, _ = centre(hidden)
    normed = (scaled * gains[2:3, :]).astype(bf16)
    mixed[...] = nt(normed, mixing_three[...]).astype(bf16)
    shared_width = SHARED * HEAD
    mixed[:, 2 * D : 2 * D + shared_width] = mixed_one[:, 2 * D : 2 * D + shared_width]
    attended[...] = attend(mixed, limits, probabilities)
    h3[...] = (hidden + nt(attended[...], output_three[...])).astype(bf16)


def feed_parts(upward):
    square = upward * upward
    rising = 0.5 + 0.5 * jnp.tanh(upward * (GELU_SCALE + (GELU_SCALE * GELU_CUBE) * square))
    active = upward * rising
    steep = 2.0 * GELU_SCALE + (6.0 * GELU_SCALE * GELU_CUBE) * square
    return active.astype(bf16), rising + active * (1.0 - rising) * steep


def quarter_back(up, down, normed_across, grad_out, active, slope):
    grad_upward = (nt(grad_out, down) * slope).astype(bf16)
    grad_down = nn(active.T, grad_out).astype(bf16)
    return nn(normed_across, grad_upward).astype(bf16), grad_down, nt(grad_upward, up)


def fourth_kernel(limits, h3, gains, cotangent, own0, own1, near, far, other_near, other_far, *rest):
    total, grad_normed, keep, send, seed, held, brought, upwards, actives, slopes, sems = rest
    seeding = pltpu.make_async_copy(cotangent, brought, sems.at[2])
    seeding.start()
    copies = bring(own0, own1, held, sems)
    hidden = h3[...].astype(f32)
    scaled, _ = centre(hidden)
    normed = (scaled * gains[3:4, :]).astype(bf16)
    normed_across = normed.T
    first = place()[1] == 0
    held[0, 1] = jnp.where(first, near[...], other_near[...])
    held[1, 1] = jnp.where(first, other_far[...], far[...])
    held[0, 2] = jnp.where(first, far[...], other_far[...])
    held[1, 2] = jnp.where(first, other_near[...], near[...])
    for rank in (1, 2):
        upwards[rank] = nn(normed, held[0, rank])
    for copy in copies:
        copy.wait()
    upwards[0] = nn(normed, held[0, 0])
    seeding.wait()
    row = lax.broadcasted_iota(jnp.int32, hidden.shape, 0)
    grad_out = jnp.where(row < limits[0:1, :1], brought[...], 0)
    seed[...] = grad_out
    for rank in (1, 2, 0):
        actives[rank], slopes[rank] = feed_parts(upwards[rank])
    for rank in (1, 2, 0):
        upwards[rank] = nt(grad_out, held[1, rank]) * slopes[rank]
    after, grads = hidden, jnp.zeros(hidden.shape, f32)
    for rank in (1, 2, 0):
        grad_upward = upwards[rank].astype(bf16)
        grad_down = nn(actives[rank].T, grad_out).astype(bf16)
        put(keep, send, rank, nn(normed_across, grad_upward).astype(bf16), grad_down)
        grads += nt(grad_upward, held[0, rank])
        after += nn(actives[rank], held[1, rank])
    total[...] = after
    grad_normed[...] = grads


def fourth_end_kernel(
    h3, gains, seed, total, grads, both, other_both, out, grad_h3, keep, send, grad_gain
):
    scaled, rstd = centre(h3[...].astype(f32))
    gain = gains[3:4, :]
    normed = (scaled * gain).astype(bf16)
    first = place()[1] == 0
    up = jnp.where(first, both[...], other_both[...])
    down = jnp.where(first, other_both[...], both[...])
    active, slope = feed_parts(nn(normed, up))
    out[...] = total[...] + nn(active, down)
    grad_up, grad_down, grad = quarter_back(up, down, normed.T, seed[...], active, slope)
    keep[...] = jnp.where(first, grad_up, grad_down)
    send[...] = jnp.where(first, grad_down, grad_up)
    grad_hidden, one_gain = norm_back(scaled, rstd, gain, grads[...] + grad)
    grad_gain[0:1, :] = one_gain
    grad_h3[...] = (seed[...].astype(f32) + grad_hidden).astype(bf16)


def attention_back(hidden, grad_out, mixed, attended, probabilities, mixing, output, gain, scratch, shared, value_grad):
    scaled, rstd = centre(hidden)
    normed_across = (scaled * gain).astype(bf16).T
    grad_heads = nn(grad_out, output[...]).astype(bf16)
    grad_output = nn(attended[...].T, grad_out).astype(bf16)
    grad_mixed = scratch[0]
    attend_back(mixed, grad_heads, probabilities, *scratch)
    shared(grad_mixed)
    grad_pair = nn(normed_across, grad_mixed[:, : 2 * D]).astype(bf16)
    grad_values = value_grad(scaled, gain, normed_across, grad_mixed)
    grad_hidden, grad_gain = norm_back(scaled, rstd, gain, nn(grad_mixed[...], mixing[...]))
    return grad_hidden, grad_gain, grad_pair, grad_values, grad_output


def third_back_kernel(
    h2, gains, grad_h3, mixed, attended, probabilities, mixing, output,
    grad_h2, grad_weights, grad_shared, grad_gain, *scratch,
):
    shared_width = SHARED * HEAD

    def hand_over(grads):
        grad_shared[...] = grads[:, 2 * D : 2 * D + shared_width]
        grads[:, 2 * D : 2 * D + shared_width] = jnp.zeros((grads.shape[0], shared_width), bf16)

    def fresh_grad(scaled, gain, normed_across, grads):
        across = grads[:, 2 * D + 2 * HEAD :].T
        return nn(across[HEAD:], (scaled * gain).astype(bf16)).astype(bf16)

    grad_hidden, one_gain, grad_pair, grad_fresh, grad_output = attention_back(
        h2[...].astype(f32), grad_h3[...], mixed, attended, probabilities, mixing, output,
        gains[2:3, :], scratch, hand_over, fresh_grad,
    )
    grad_weights[0, :D] = grad_pair[:, :D]
    grad_weights[0, D:] = grad_pair[:, D:]
    grad_weights[1, :shared_width] = jnp.zeros((shared_width, D), bf16)
    grad_weights[1, shared_width:D] = grad_fresh
    grad_weights[1, D:] = grad_output
    grad_gain[0:1, :] = one_gain
    grad_h2[...] = (grad_h3[...].astype(f32) + grad_hidden).astype(bf16)


def second_back_kernel(h1, gains, grad_h2, held, actives, slopes, grad_h1, keep, send, grad_gain):
    scaled, rstd = centre(h1[...].astype(f32))
    gain = gains[1:2, :]
    normed_across = (scaled * gain).astype(bf16).T
    grads = jnp.zeros(scaled.shape, f32)
    for rank in range(QUARTERS):
        grad_up, grad_down, grad = quarter_back(
            held[0, rank], held[1, rank], normed_across, grad_h2[...], actives[rank], slopes[rank]
        )
        put(keep, send, rank, grad_up, grad_down)
        grads += grad
    grad_hidden, one_gain = norm_back(scaled, rstd, gain, grads)
    grad_gain[0:1, :] = one_gain
    grad_h1[...] = (grad_h2[...].astype(f32) + grad_hidden).astype(bf16)


def first_back_kernel(
    tokens, gains, grad_h1, mixed, attended, probabilities, mixing, output,
    grad_shared, third_weights, gain_two, gain_three, gain_four,
    input_grad, keep, send, *scratch,
):
    shared_width = SHARED * HEAD

    def take_over(grads):
        at = slice(2 * D, 2 * D + shared_width)
        grads[:, at] = (grads[:, at].astype(f32) + grad_shared[...].astype(f32)).astype(bf16)

    def value_grad(scaled, gain, normed_across, grads):
        return nn(normed_across, grads[:, 2 * D :]).astype(bf16)

    grad_hidden, gain_one, grad_pair, grad_values, grad_output = attention_back(
        tokens[...].astype(f32), grad_h1[...], mixed, attended, probabilities, mixing, output,
        gains[0:1, :], scratch, take_over, value_grad,
    )
    input_grad[...] = grad_h1[...].astype(f32) + grad_hidden
    section, part = place()[0], D // 2
    gain_rows = jnp.concatenate(
        [gain_one, gain_two[0:1, :], gain_three[0:1, :], gain_four[0:1, :], jnp.zeros((12, D), f32)], 0
    ).astype(bf16)
    for j in range(QUARTERS):
        at = slice(part * (j % 2), part * (j % 2) + part)
        zero = (grad_pair[:, :D], grad_pair[:, D:])[j // 2][at]
        one = (grad_values, grad_output)[j // 2][at]
        put(keep, send, section ^ j, zero, one, (0, part))
        below = third_weights[1, part * j : part * j + part]
        if j == 0:
            below = jnp.concatenate([gain_rows, below[16:]], 0)
        put(keep, send, section ^ j, third_weights[0, part * j : part * j + part], below, (part, part))


def pieces_of(refs):
    if len(refs) == 4:
        for own, (mine, pair) in ((True, refs[:2]), (False, refs[2:])):
            yield own, 0, mine[0]
            yield own, 2, mine[1]
            yield own, 1, pair[0]
            yield own, 3, pair[1]
        return
    for own, (mine, far, pair) in ((True, refs[:3]), (False, refs[3:])):
        yield own, 0, mine[...]
        yield own, 2, far[...]
        yield own, 1, pair[0]
        yield own, 3, pair[1]


def unpack_feed_kernel(*rest):
    up, down, wide, sems = rest[-4:]
    section, core = place()
    steps = []
    for slot, (own, rank, value) in enumerate(pieces_of(rest[:-4])):
        wide[slot] = value.astype(f32)
        zero = (core == 0) if own else (core != 0)
        column = pl.ds(pl.multiple_of((section ^ rank) * D, D), D)
        below = pl.ds(pl.multiple_of((section ^ swapped(rank)) * D, D), D)
        steps += [
            (zero, pltpu.make_async_copy(wide.at[slot], up.at[:, column], sems.at[slot])),
            (jnp.logical_not(zero), pltpu.make_async_copy(wide.at[slot], down.at[below, :], sems.at[slot])),
        ]
        for flag, copy in steps[-2:]:
            pl.when(flag)(copy.start)
    for flag, copy in steps:
        pl.when(flag)(copy.wait)


def unpack_attention(pieces, targets, gains, wide, sems):
    mixing, output, pair, fresh, output_three = targets
    section, core = place()
    part = D // 2
    steps = []
    for slot, (own, rank, value) in enumerate(pieces):
        wide[slot] = value[...].astype(f32)
        zero = (core == 0) if own else (core != 0)
        j0, j1 = section ^ rank, section ^ swapped(rank)
        column = pl.ds(pl.multiple_of((j0 >> 1) * D, D), D)
        row0 = pl.ds(pl.multiple_of((j0 & 1) * part, part), part)
        row1 = pl.ds(pl.multiple_of((j1 & 1) * part, part), part)
        one = jnp.logical_not(zero)

        @pl.when(one & (j1 == 0))
        def _():
            for k, ref in enumerate(gains):
                ref[...] = wide[slot, part + k]

        for low, flag, target in (
            (0, zero, mixing.at[row0, column]),
            (1, zero, pair.at[row0, column]),
            (0, one & (j1 < 2), mixing.at[row1, 2 * D :]),
            (1, one & (j1 == 1), fresh),
            (0, one & (j1 >= 2), output.at[row1, :]),
            (1, one & (j1 >= 2), output_three.at[row1, :]),
        ):
            copy = pltpu.make_async_copy(
                wide.at[slot, part * low : part * low + part], target, sems.at[slot, low]
            )
            steps.append((flag, copy))
            pl.when(flag)(copy.start)
    for flag, copy in steps:
        pl.when(flag)(copy.wait)


def unpack_some_kernel(*rest):
    pieces, outs, (wide, sems) = rest[:6], rest[6:-2], rest[-2:]
    ranked = [(own, rank, pieces[3 * k + i]) for k, own in enumerate((True, False)) for i, rank in enumerate((0, 2, 1))]
    for ref in outs[5:]:
        ref[...] = jnp.zeros(ref.shape, f32)
    unpack_attention(ranked, outs[:5], outs[5:], wide, sems)


def unpack_rest_kernel(*rest):
    pieces, before, outs, (wide, sems) = rest[:2], rest[7:11], rest[11:-2], rest[-2:]
    for ref, old in zip(outs[5:], before):
        ref[...] = old[...]
    unpack_attention([(True, 3, pieces[0]), (False, 3, pieces[1])], outs[:5], outs[5:], wide, sems)


SMEM, VMEM, HBM = pltpu.SMEM, pltpu.VMEM, pltpu.HBM


def call(body, name, args, outs, scratch=(), spaces=None, limit=12, hint=20, aliases=None):
    spaces = spaces or {}
    args = [
        pltpu.with_memory_space_constraint(arg, HBM) if spaces.get(i) is HBM else arg
        for i, arg in enumerate(args)
    ]
    places = {"vmem": VMEM, "hbm": HBM}
    return pl.pallas_call(
        body,
        name=name,
        out_shape=[
            places[where](shape, dtype) if where in places else jax.ShapeDtypeStruct(shape, dtype)
            for shape, dtype, where in outs
        ],
        in_specs=[pl.BlockSpec(memory_space=spaces.get(i, VMEM)) for i in range(len(args))],
        out_specs=[pl.BlockSpec(memory_space=places.get(where, VMEM)) for _, _, where in outs],
        scratch_shapes=list(scratch),
        input_output_aliases=aliases or {},
        compiler_params=pltpu.CompilerParams(vmem_limit_bytes=limit * 1024 * 1024),
        cost_estimate=pl.CostEstimate(flops=hint * 10**9, bytes_accessed=1, transcendentals=1),
    )(*args)


def partner_pairs(sections, groups, kind):
    found = []
    for section in range(sections):
        for group in range(groups):
            core = group & 1
            to_section, to_group = section, group
            if kind == "near":
                to_section = section ^ (1 if core == 0 else 2)
            elif kind == "far":
                to_section = section ^ (2 if core == 0 else 1)
            else:
                to_group = group ^ kind
            found.append((section * groups + group, to_section * groups + to_group))
    return found


def partner(value, kind):
    sections, groups = lax.axis_size("section"), lax.axis_size("dp")
    return lax.ppermute(value, ("section", "dp"), partner_pairs(sections, groups, kind))


def total(*parts):
    return sum(part.astype(f32) for part in parts).astype(bf16)


def chip_bit():
    return (lax.axis_index("dp") >> 1) & 1


def one_sum_kernel(index, keep, came, out):
    out[...] = total(keep[index], came[index])


def begin_kernel(keep, came, both, near):
    both[...] = total(keep[3], came[3])
    near[...] = total(keep[1], came[1])


def begin_pair_kernel(keep, came, pair):
    pair[0] = total(keep[3], came[3])
    pair[1] = total(keep[1], came[1])


def turn_pair_kernel(keep, came, pair, far):
    far[...] = total(keep[2], came[2], pair[0])


def own_pair_kernel(keep, came, pair, far, away, kept, halves):
    own_kernel(keep, came, pair.at[1], far, away, kept, halves)


def turn_kernel(keep, came, both, far):
    far[...] = total(keep[2], came[2], both[...])


def own_kernel(keep, came, near, far, away, kept, halves):
    rows = kept.shape[0]
    own = total(keep[0], came[0], near[...], far[...])
    halves[0] = own[:rows]
    halves[1] = own[rows:]
    bit = chip_bit()
    kept[...] = halves[bit]
    away[...] = halves[1 - bit]


def copy_kernel(value, out):
    out[...] = value[...]


def pair_kernel(left, right, out):
    out[0] = left[...]
    out[1] = right[...]


def copy_both_kernel(left, right, left_out, right_out):
    left_out[...] = left[...]
    right_out[...] = right[...]


def sum_kernel(left, right, out):
    out[...] = total(left[...], right[...])


def join_kernel(kept, back, own):
    rows = kept.shape[0]
    bit = chip_bit()
    own[pl.ds(pl.multiple_of(bit * rows, rows), rows)] = kept[...]
    own[pl.ds(pl.multiple_of((1 - bit) * rows, rows), rows)] = back[...]


class Line:
    def __init__(self):
        self.last = ()

    def tied(self, *values):
        if not self.last:
            return values
        return lax.optimization_barrier(values + self.last)[: len(values)]

    def step(self, made, *values):
        made = made(*self.tied(*values))
        self.last = (jax.tree.leaves(made)[0],)
        return made

    def hop(self, value, kind):
        return partner(self.tied(value)[0], kind)

    def gate(self, value, hint):
        copy = [(value.shape, value.dtype, "vmem")]
        return self.step(lambda v: call(copy_kernel, "gate", (v,), copy, limit=4, hint=hint)[0], value)


class Chunk:
    def __init__(self, line, keep, send):
        self.line, self.keep = line, keep
        self.came = partner(send, 1)
        self.groups = lax.axis_size("dp")

    def made(self, hint, body, name, outs, *args, scratch=()):
        return self.line.step(
            lambda *tied: call(
                body, name, tied, [(shape, bf16, "vmem") for shape in outs], scratch, limit=4, hint=hint
            ),
            *args,
        )

    def begin(self, hint):
        block = self.keep.shape[1:]
        both, near = self.made(hint, begin_kernel, "sum_begin", [block] * 2, self.keep, self.came)
        self.both, self.near = partner(both, "near"), partner(near, "near")

    def begin_merged(self, hint):
        shape = (2,) + self.keep.shape[1:]
        (pair,) = self.made(hint, begin_pair_kernel, "sum_begin", [shape], self.keep, self.came)
        self.both = self.near = partner(pair, "near")

    def begin_near(self, hint):
        body = functools.partial(one_sum_kernel, 1)
        (near,) = self.made(hint, body, "sum_near", [self.keep.shape[1:]], self.keep, self.came)
        self.near = partner(near, "near")

    def begin_both(self, keep, send, hint):
        (both,) = self.made(hint, sum_kernel, "sum_both", [keep.shape], keep, partner(send, 1))
        self.both = partner(both, "near")

    def turn(self, hint):
        body = turn_kernel if self.both is not self.near else turn_pair_kernel
        (far,) = self.made(hint, body, "sum_turn", [self.keep.shape[1:]], self.keep, self.came, self.both)
        self.far = partner(far, "far")

    def own(self, hint):
        rows, width = self.keep.shape[1:]
        half = (rows // 2, width)
        body = own_kernel if self.both is not self.near else own_pair_kernel
        away, self.kept = self.made(
            hint, body, "sum_own", [half] * 2, self.keep, self.came, self.near, self.far,
            scratch=[VMEM((2,) + half, bf16)],
        )
        self.back = partner(away, 2)

    def plus(self, came, hint):
        (self.kept,) = self.made(hint, sum_kernel, "sum_chips", [self.kept.shape], self.kept, came)

    def along(self, hint):
        self.plus(self.back, hint)
        step = 4
        while step < self.groups:
            self.back = partner(self.kept, step)
            step *= 2
            if step < self.groups:
                self.plus(self.back, hint)

    def across(self, hint):
        if self.groups > 4:
            self.plus(self.back, hint)
        self.back = partner(self.kept, 2)

    def share(self, hint):
        rows, width = self.kept.shape
        (own,) = self.made(hint, join_kernel, "sum_join", [(2 * rows, width)], self.kept, self.back)
        self.mine, self.far, self.near = own, partner(own, "far"), partner(own, "near")
        self.others = [partner(own, 1)]

    def pass_on(self, hint):
        self.far = self.line.gate(self.far, hint)
        self.both = partner(self.far, "near")
        self.others.append(partner(self.far, 1))

    def end(self, hint):
        shape = (2,) + self.far.shape
        (pair,) = self.made(hint, pair_kernel, "sum_pair", [shape], self.near, self.both)
        self.pieces = [self.mine, self.far, pair] + self.others + [partner(pair, 1)]

    def share_far(self, hint):
        rows, width = self.kept.shape
        (self.mine,) = self.made(hint, join_kernel, "sum_join", [(2 * rows, width)], self.kept, self.back)
        self.far = partner(self.mine, "far")

    def pass_pair(self, hint):
        shape = (2,) + self.mine.shape
        (self.mine,) = self.made(hint, pair_kernel, "sum_pair", [shape], self.mine, self.far)
        self.near = partner(self.mine, "near")
        self.others = [partner(self.mine, 1)]

    def end_pair(self, hint):
        pair = self.line.gate(self.near, hint)
        self.pieces = [self.mine, pair] + self.others + [partner(pair, 1)]

    def pass_near(self, hint):
        self.near = self.line.gate(self.near, hint)
        self.others.append(partner(self.near, 1))

    def end_alone(self, hint):
        both = self.line.gate(self.both, hint)
        self.pieces = [both, partner(both, 1)]


def shards(
    tokens,
    cotangent,
    lengths,
    gain_one,
    mixing_one,
    output_one,
    gain_two,
    up_two,
    down_two,
    gain_three,
    pair_three,
    fresh_three,
    output_three,
    gain_four,
    up_four,
    down_four,
):
    rows = tokens.shape[0]
    square = (D, D)
    row, wide_row, held = (rows, D), (rows, 3 * D), (2, QUARTERS, D, D)
    gain_row, packed, chances = (8, D), (QUARTERS, D, D), (HEADS, rows, rows)
    hidden_row = (QUARTERS,) + row
    back_scratch = [VMEM(wide_row, bf16), VMEM(chances, f32), VMEM((2,) + chances, bf16)]
    shared_width = SHARED * HEAD
    line = Line()

    half_one, half_three, mine_one, mine_two, mine_four, limits = call(
        prepare_kernel, "prepare",
        (mixing_one.T, output_one.T, pair_three.T, fresh_three.T, output_three.T,
         gain_one, gain_two, gain_three, gain_four, up_two, down_two, up_four, down_four, lengths.T),
        [(square, bf16, "vmem")] * 5 + [((8, rows), jnp.int32, "vmem")],
        [VMEM((8, D), f32)] + [VMEM(gain_one.shape, bf16)] * 4
        + [SMEM(lengths.T.shape, jnp.int32), pltpu.SemaphoreType.DMA((19,))],
        {i: HBM for i in range(14)},
    )
    near_one, far_one = partner(mine_one, "near"), partner(mine_one, "far")
    near_two, far_two = partner(mine_two, "near"), partner(mine_two, "far")
    limits = line.gate(limits, 0)
    near_one = line.gate(near_one, 3)
    other_near_one = partner(near_one, 1)
    both_one = partner(near_one, "far")
    far_one = line.gate(far_one, 3)
    other_far_one = partner(far_one, 1)
    near_two = line.gate(near_two, 3)
    other_near_two = partner(near_two, 1)
    both_two = partner(near_two, "far")
    mine_four = line.gate(mine_four, 3)
    near_four, far_four = partner(mine_four, "near"), partner(mine_four, "far")
    both_one = line.gate(both_one, 8)
    other_both_one = partner(both_one, 1)
    far_two = line.gate(far_two, 3)
    other_far_two = partner(far_two, 1)
    both_two = line.gate(both_two, 3)
    other_both_two = partner(both_two, 1)
    h1, mixed_one, attended_one, chances_one, mixing, output, mixing_three, out_three, gains = line.step(
        lambda *args: call(
            first_kernel, "first_forward", args,
            [(row, bf16, "vmem"), (wide_row, bf16, "vmem"), (row, bf16, "vmem"), (chances, f32, "vmem"),
             ((3 * D, D), bf16, "vmem"), (square, bf16, "vmem"), ((3 * D, D), bf16, "vmem"),
             (square, bf16, "vmem"), (gain_row, f32, "vmem")],
            [VMEM(held, bf16)], hint=6,
        ),
        limits, tokens, half_one, half_three,
        near_one, far_one, both_one, other_near_one, other_far_one, other_both_one,
    )
    near_four = line.gate(near_four, 3)
    other_near_four = partner(near_four, 1)
    both_four = partner(near_four, "far")
    far_four = line.gate(far_four, 4)
    other_far_four = partner(far_four, 1)
    h2, held_two, h3, mixed_three, attended_three, chances_three, actives, slopes = line.step(
        lambda *args: call(
            middle_kernel, "second_third_forward", args,
            [(row, bf16, "vmem"), (held, bf16, "vmem"), (row, bf16, "vmem"), (wide_row, bf16, "vmem"),
             (row, bf16, "vmem"), (chances, f32, "vmem"), (hidden_row, bf16, "vmem"),
             (hidden_row, f32, "vmem")],
            [pltpu.SemaphoreType.DMA((2,))], {6: HBM, 7: HBM}, hint=3,
        ),
        limits, h1, gains, mixing_three, out_three, mixed_one, up_two, down_two,
        near_two, far_two, both_two, other_near_two, other_far_two, other_both_two,
    )
    both_four = line.gate(both_four, 2)
    other_both_four = partner(both_four, 1)
    three_quarters = (QUARTERS - 1, D, D)
    after, grad_normed, keep, send, seed = line.step(
        lambda *args: call(
            fourth_kernel, "fourth_both", args,
            [(row, f32, "vmem"), (row, f32, "vmem"), (three_quarters, bf16, "vmem"),
             (three_quarters, bf16, "vmem"), (row, bf16, "vmem")],
            [VMEM((2, QUARTERS - 1, D, D), bf16), VMEM(row, bf16), VMEM((QUARTERS - 1,) + row, f32),
             VMEM((QUARTERS - 1,) + row, bf16), VMEM((QUARTERS - 1,) + row, f32), pltpu.SemaphoreType.DMA((3,))],
            {3: HBM, 4: HBM, 5: HBM}, hint=3,
        ),
        limits, h3, gains, cotangent, up_four, down_four,
        near_four, far_four, other_near_four, other_far_four,
    )
    four = Chunk(line, keep, send)
    out, grad_h3, last_keep, last_send, gain_grad_four = line.step(
        lambda *args: call(
            fourth_end_kernel, "fourth_end", args,
            [(row, f32, "plain"), (row, bf16, "vmem"), (square, bf16, "vmem"), (square, bf16, "vmem"),
             (gain_row, f32, "vmem")], hint=20,
        ),
        h3, gains, seed, after, grad_normed, both_four, other_both_four,
    )
    grad_h2, third_weights, grad_shared, gain_grad_three = line.step(
        lambda *args: call(
            third_back_kernel, "third_backward", args,
            [(row, bf16, "vmem"), ((2, 2 * D, D), bf16, "vmem"), ((rows, shared_width), bf16, "vmem"),
             (gain_row, f32, "vmem")],
            back_scratch, hint=8,
        ),
        h2, gains, grad_h3, mixed_three, attended_three, chances_three, mixing_three, out_three,
    )
    four.begin_both(last_keep, last_send, 20)
    four.begin_near(20)
    grad_h1, keep, send, gain_grad_two = line.step(
        lambda *args: call(
            second_back_kernel, "second_backward", args,
            [(row, bf16, "vmem"), (packed, bf16, "vmem"), (packed, bf16, "vmem"), (gain_row, f32, "vmem")], hint=20,
        ),
        h1, gains, grad_h2, held_two, actives, slopes,
    )
    two = Chunk(line, keep, send)
    input_grad, keep, send = line.step(
        lambda *args: call(
            first_back_kernel, "first_backward", args,
            [(row, f32, "plain"), (packed, bf16, "vmem"), (packed, bf16, "vmem")],
            back_scratch, hint=8,
        ),
        tokens, gains, grad_h1, mixed_one, attended_one, chances_one, mixing, output,
        grad_shared, third_weights, gain_grad_two, gain_grad_three, gain_grad_four,
    )
    first = Chunk(line, keep, send)
    four.turn(20)
    two.begin(20)
    first.begin(5)
    four.own(5)
    two.turn(20)
    four.along(5)
    two.own(1)
    four.across(20)
    first.turn(6)
    two.along(8)
    four.share_far(5)
    first.own(20)
    two.across(20)
    four.pass_pair(2)
    first.along(20)
    two.share(20)
    first.across(5)
    four.end_pair(5)
    two.pass_on(1)
    first.share(5)
    two.end(3)
    first.pass_on(2)
    feed_outs = [((D, 4 * D), f32, "hbm"), ((4 * D, D), f32, "hbm")]
    feed_scratch = [VMEM((8, D, D), f32), pltpu.SemaphoreType.DMA((8,))]
    grad_up_four, grad_down_four = line.step(
        lambda *args: call(unpack_feed_kernel, "unpack_four", args, feed_outs, feed_scratch, hint=3),
        *four.pieces,
    )
    first.pass_near(2)
    grad_up_two, grad_down_two = line.step(
        lambda *args: call(unpack_feed_kernel, "unpack_two", args, feed_outs, feed_scratch, hint=1),
        *two.pieces,
    )
    first.end_alone(8)
    attention_outs = [
        ((D, 3 * D), f32, "hbm"), (square, f32, "hbm"), ((D, 2 * D), f32, "hbm"),
        ((D // 2, D), f32, "hbm"), (square, f32, "hbm"),
    ] + [((D,), f32, "plain")] * 4
    unpacked = line.step(
        lambda *args: call(
            unpack_some_kernel, "unpack_some", args, attention_outs,
            [VMEM((6, D, D), f32), pltpu.SemaphoreType.DMA((6, 2))], hint=3,
        ),
        first.mine, first.far, first.near, *first.others,
    )
    mixing_g, output_g, pair_g, fresh_g, output_three_g, g1, g2, g3, g4 = line.step(
        lambda *args: call(
            unpack_rest_kernel, "unpack_rest", args, attention_outs,
            [VMEM((2, D, D), f32), pltpu.SemaphoreType.DMA((2, 2))], {i: HBM for i in range(2, 7)},
            hint=4, aliases={i + 2: i for i in range(5)},
        ),
        *first.pieces, *unpacked,
    )
    return (
        out, input_grad, g1, mixing_g, output_g, g2, grad_up_two, grad_down_two,
        g3, pair_g, fresh_g.T, output_three_g, g4, grad_up_four, grad_down_four,
    )


def solution(mesh):
    return jax.shard_map(
        shards,
        mesh=mesh,
        in_specs=(
            P(("section", "dp"), None),
            P(("section", "dp"), None),
            P(None, "dp"),
            P("section"),
            P(None, "section"),
            P(None, "section"),
            P("section"),
            P(None, "section"),
            P("section", None),
            P("section"),
            P(None, "section"),
            P(None, "section"),
            P(None, "section"),
            P("section"),
            P(None, "section"),
            P("section", None),
        ),
        out_specs=(P(("section", "dp"), None), P(("section", "dp"), None)) + (P(),) * 13,
        check_vma=False,
    )
```
